512 devices in a mesh: gx: 8 (over z_lo), gy: 8 (over y, core), gz: 8 (over z_hi, x).
Axes of the slice: x: 4, y: 4, z: 16 (z_hi: 2, z_lo: 8; z = z_hi * 8 + z_lo), core: 2. Of those that a mesh axis runs over, the one named last changes fastest.
Arguments:
- orbitals: float32 [16, 32, 32, 1024], P(None, 'gx', 'gy', 'gz'), may hold values from -5000 to 5000
- potential: float32 [32, 32, 1024], P('gx', 'gy', 'gz'), may hold values from 0 to 2
Outputs:
- q_block: float32 [16, 32, 32, 1024], P(None, 'gx', 'gy', 'gz')
- ritz: float32 [16, 16], replicated
The draws below stay inside these ranges and needn't reach their ends.
All inputs are finite; a program needn't handle non-finite values.
Results may differ from the reference program's by a relative error of at most 0.0003.
Values sent between devices are 32-bit elements; how exact they have to be, the bound alone decides.
No kernel may reach another device: no remote copies, remote signals or barrier semaphores. Data moves between devices by JAX's collectives and lax.ppermute only.
A program may use at most 64 MiB of HBM per device.

```python
import jax
import jax.numpy as jnp
from jax import lax

ORB = 16
DEGREE = 3
NX = 32
NY = 32
NZ = 1024
NCELLS = 1048576


def draw_orbitals(key, part):
    key = jax.random.fold_in(key, 11)
    keys = jax.random.split(key, 6)
    shape = (ORB, NX, NY, NZ)
    grid = (NX, NY, NZ)
    rough = jnp.clip(jax.random.normal(keys[0], shape, jnp.float32), -5.0, 5.0)
    common = 0.6
    first = jnp.clip(jax.random.normal(keys[1], grid, jnp.float32), -4.0, 4.0)
    second = jnp.clip(jax.random.normal(keys[2], grid, jnp.float32), -4.0, 4.0)
    coef_first = jnp.clip(jax.random.normal(keys[3], (ORB,), jnp.float32), -1.5, 1.5) * common
    coef_second = jnp.clip(jax.random.normal(keys[4], (ORB,), jnp.float32), -1.5, 1.5) * common
    scales = jnp.exp(jnp.log(10.0) * jax.random.uniform(keys[5], (ORB,), jnp.float32))
    growth = jnp.log(3.0)
    along_x = jnp.exp(growth * (jnp.arange(NX, dtype=jnp.float32) + 0.5) / NX)
    along_y = jnp.exp(growth * (jnp.arange(NY, dtype=jnp.float32) + 0.5) / NY)
    along_z = jnp.exp(growth * (jnp.arange(NZ, dtype=jnp.float32) + 0.5) / NZ)
    envelope = along_x[:, None, None] * along_y[None, :, None] * along_z[None, None, :]
    mixed = rough + coef_first[:, None, None, None] * first[None] + coef_second[:, None, None, None] * second[None]
    return (scales[:, None, None, None] * envelope[None] * mixed).astype(jnp.float32)


def block_scale(own_key, shape, cuts, smallest, largest):
    def one(dim, blocks):
        heights = jax.random.uniform(jax.random.fold_in(jax.random.fold_in(own_key, 6), dim), (blocks,), jnp.float32, smallest / len(cuts), largest / len(cuts))
        return jnp.repeat(jnp.exp(heights), shape[dim] // blocks).reshape((-1,) + (1,) * (len(shape) - dim - 1))

    loudness = one(*cuts[0])
    for cut in cuts[1:]:
        loudness = loudness * one(*cut)
    return loudness


def setup_inputs(seed: int = 0) -> dict:
    key_of = jax.random.split(jax.random.key(seed), 3)
    orbitals = draw_orbitals(jax.random.fold_in(key_of[2], 71), 0)
    potential = jnp.clip(2.0 * jax.random.uniform(key_of[1], (NX, NY, NZ), jnp.float32) ** block_scale(key_of[1], (NX, NY, NZ), ((0, 8), (1, 8), (2, 8)), -0.2, 0.2), 0.0, 2.0)
    return {"orbitals": orbitals, "potential": potential}


STENCIL_WEIGHTS = (-205.0 / 72.0, 8.0 / 5.0, -1.0 / 5.0, 8.0 / 315.0, -1.0 / 560.0)
FILTER_LOWER = 1.5
FILTER_UPPER = 12.0

def laplace_block(padded, width_x, width_y, width_z):

    def window(shift_x, shift_y, shift_z):
        return padded[..., 4 + shift_x:4 + shift_x + width_x, 4 + shift_y:4 + shift_y + width_y, 4 + shift_z:4 + shift_z + width_z]
    total = 3.0 * STENCIL_WEIGHTS[0] * window(0, 0, 0)
    for distance in range(1, 5):
        pairs = window(distance, 0, 0) + window(-distance, 0, 0)
        pairs = pairs + window(0, distance, 0) + window(0, -distance, 0)
        pairs = pairs + window(0, 0, distance) + window(0, 0, -distance)
        total = total + STENCIL_WEIGHTS[distance] * pairs
    return total

def hamilton(padded, field, potential):
    width_x, width_y, width_z = field.shape[-3:]
    return -0.5 * laplace_block(padded, width_x, width_y, width_z) + potential * field

def chebyshev_filter(block, apply_field):
    half_width = (FILTER_UPPER - FILTER_LOWER) / 2.0
    middle = (FILTER_UPPER + FILTER_LOWER) / 2.0
    previous = block
    current = (apply_field(block) - middle * block) / half_width
    for repeat in range(1, DEGREE):
        following = 2.0 * (apply_field(current) - middle * current) / half_width - previous
        previous, current = (current, following)
    return current

def reference(orbitals, potential):

    def apply_one(field):
        return hamilton(jnp.pad(field, 4), field, potential)

    def filter_one(field):
        return chebyshev_filter(field, apply_one)
    filtered = lax.map(filter_one, orbitals)
    flat_filtered = filtered.reshape(ORB, -1)
    gram = jnp.dot(flat_filtered.astype(jnp.float32), flat_filtered.T.astype(jnp.float32), precision=lax.Precision.HIGHEST, preferred_element_type=jnp.float32) / NCELLS
    lower_factor = jnp.linalg.cholesky(gram)
    flat_q = jax.scipy.linalg.solve_triangular(lower_factor, flat_filtered, lower=True)
    q_block = flat_q.reshape(orbitals.shape)

    def ritz_column(field):
        image = apply_one(field)
        return jnp.dot(flat_q.astype(jnp.float32), image.reshape(-1).astype(jnp.float32), precision=lax.Precision.HIGHEST, preferred_element_type=jnp.float32)
    ritz = lax.map(ritz_column, q_block).T / NCELLS
    return (q_block, ritz)
```

```python
import jax
import jax.numpy as jnp
from jax import lax
from jax.sharding import PartitionSpec as P

DEGREE = 3
STENCIL_WEIGHTS = (-205.0 / 72.0, 8.0 / 5.0, -1.0 / 5.0, 8.0 / 315.0, -1.0 / 560.0)
FILTER_LOWER = 1.5
FILTER_UPPER = 12.0


def shift_pairs(size, step):
    return [(i, i + step) for i in range(size) if 0 <= i + step < size]


def faces(value):
    width = 4
    out = []
    for axis, dim in (("gz", 3), ("gx", 1), ("gy", 2)):
        size, length = lax.axis_size(axis), value.shape[dim]
        last = lax.slice_in_dim(value, length - width, length, axis=dim)
        first = lax.slice_in_dim(value, 0, width, axis=dim)
        out.append((lax.ppermute(last, axis, shift_pairs(size, 1)), lax.ppermute(first, axis, shift_pairs(size, -1)), dim))
    return out


def hamilton(field, potential):
    lap = 3.0 * STENCIL_WEIGHTS[0] * field
    for before, after, dim in faces(field):
        padded = jnp.concatenate([before, field, after], axis=dim)
        length = field.shape[dim]
        for k in range(1, 5):
            up = lax.slice_in_dim(padded, 4 + k, 4 + k + length, axis=dim)
            down = lax.slice_in_dim(padded, 4 - k, 4 - k + length, axis=dim)
            lap = lap + STENCIL_WEIGHTS[k] * (up + down)
    return -0.5 * lap + potential * field


def inner_rows(first, second):
    return lax.dot_general(
        first, second, (((1,), (1,)), ((), ())), precision=lax.Precision.HIGHEST, preferred_element_type=jnp.float32
    )


def sum_everywhere(value):
    for axis in ("gy", "gx", "gz"):
        size, bit = lax.axis_size(axis), 1
        while bit < size:
            value = value + lax.ppermute(value, axis, [(i, i ^ bit) for i in range(size)])
            bit *= 2
    return value


def body(orbitals, potential):
    count = orbitals.shape[0]
    cells = orbitals[0].size * lax.axis_size("gx") * lax.axis_size("gy") * lax.axis_size("gz")
    half = (FILTER_UPPER - FILTER_LOWER) / 2.0
    middle = (FILTER_UPPER + FILTER_LOWER) / 2.0
    previous = orbitals
    current = (hamilton(orbitals, potential) - middle * orbitals) / half
    for _ in range(1, DEGREE):
        previous, current = current, 2.0 * (hamilton(current, potential) - middle * current) / half - previous
    image = hamilton(current, potential).reshape(count, -1)
    flat = current.reshape(count, -1)
    sums = jnp.stack([inner_rows(flat, flat), inner_rows(flat, image)]).reshape(4, 128)
    sums = sum_everywhere(sums).reshape(2, count, count) / cells
    lower = jnp.linalg.cholesky(sums[0])
    inverse = jax.scipy.linalg.solve_triangular(lower, jnp.eye(count, dtype=jnp.float32), lower=True)
    dot = lambda a, b: lax.dot_general(a, b, (((1,), (0,)), ((), ())), precision=lax.Precision.HIGHEST)
    flat_q = dot(inverse, flat)
    ritz = dot(dot(inverse, sums[1]), inverse.T)
    return (flat_q.reshape(orbitals.shape), ritz)


def solution(mesh):
    placed = (P(None, "gx", "gy", "gz"), P("gx", "gy", "gz"))
    return jax.shard_map(
        body,
        mesh=mesh,
        in_specs=placed,
        out_specs=(P(None, "gx", "gy", "gz"), P()),
        check_vma=False,
    )
```

```python
import jax
import jax.numpy as jnp
from jax import lax
from jax.sharding import PartitionSpec as P

DEGREE = 3
STENCIL_WEIGHTS = (-205.0 / 72.0, 8.0 / 5.0, -1.0 / 5.0, 8.0 / 315.0, -1.0 / 560.0)
FILTER_LOWER = 1.5
FILTER_UPPER = 12.0


def shift_pairs(size, step):
    return [(i, i + step) for i in range(size) if 0 <= i + step < size]


def faces(value):
    width = 4
    out = []
    for axis, dim in (("gz", 3), ("gx", 1), ("gy", 2)):
        size, length = lax.axis_size(axis), value.shape[dim]
        last = lax.slice_in_dim(value, length - width, length, axis=dim)
        first = lax.slice_in_dim(value, 0, width, axis=dim)
        out.append((lax.ppermute(last, axis, shift_pairs(size, 1)), lax.ppermute(first, axis, shift_pairs(size, -1)), dim))
    return out


def hamilton(field, potential):
    lap = 3.0 * STENCIL_WEIGHTS[0] * field
    for before, after, dim in faces(field):
        padded = jnp.concatenate([before, field, after], axis=dim)
        length = field.shape[dim]
        for k in range(1, 5):
            up = lax.slice_in_dim(padded, 4 + k, 4 + k + length, axis=dim)
            down = lax.slice_in_dim(padded, 4 - k, 4 - k + length, axis=dim)
            lap = lap + STENCIL_WEIGHTS[k] * (up + down)
    return -0.5 * lap + potential * field


def inner_rows(first, second):
    return lax.dot_general(
        first, second, (((1,), (1,)), ((), ())), precision=lax.Precision.HIGHEST, preferred_element_type=jnp.float32
    )


def sum_everywhere(value):
    return jnp.sum(lax.all_gather(value, ("gx", "gy", "gz"), tiled=False), axis=0)


def body(orbitals, potential):
    count = orbitals.shape[0]
    cells = orbitals[0].size * lax.axis_size("gx") * lax.axis_size("gy") * lax.axis_size("gz")
    half = (FILTER_UPPER - FILTER_LOWER) / 2.0
    middle = (FILTER_UPPER + FILTER_LOWER) / 2.0
    previous = orbitals
    current = (hamilton(orbitals, potential) - middle * orbitals) / half
    for _ in range(1, DEGREE):
        previous, current = current, 2.0 * (hamilton(current, potential) - middle * current) / half - previous
    image = hamilton(current, potential).reshape(count, -1)
    flat = current.reshape(count, -1)
    sums = jnp.stack([inner_rows(flat, flat), inner_rows(flat, image)]).reshape(4, 128)
    sums = sum_everywhere(sums).reshape(2, count, count) / cells
    lower = jnp.linalg.cholesky(sums[0])
    inverse = jax.scipy.linalg.solve_triangular(lower, jnp.eye(count, dtype=jnp.float32), lower=True)
    dot = lambda a, b: lax.dot_general(a, b, (((1,), (0,)), ((), ())), precision=lax.Precision.HIGHEST)
    flat_q = dot(inverse, flat)
    ritz = dot(dot(inverse, sums[1]), inverse.T)
    return (flat_q.reshape(orbitals.shape), ritz)


def solution(mesh):
    placed = (P(None, "gx", "gy", "gz"), P("gx", "gy", "gz"))
    return jax.shard_map(
        body,
        mesh=mesh,
        in_specs=placed,
        out_specs=(P(None, "gx", "gy", "gz"), P()),
        check_vma=False,
    )
```

```python
import functools

import jax
import jax.numpy as jnp
from jax import lax
from jax.experimental import pallas as pl
from jax.experimental.pallas import tpu as pltpu
from jax.sharding import PartitionSpec as P

WEIGHTS = (-205.0 / 72.0, 8.0 / 5.0, -1.0 / 5.0, 8.0 / 315.0, -1.0 / 560.0)
HALF = (12.0 - 1.5) / 2.0
MIDDLE = (12.0 + 1.5) / 2.0
ORB = 16
SIDE = 4
CELLS = SIDE * SIDE
LANES = 128
EXT = 16
BLOCK = CELLS * ORB
EDGE = SIDE * ORB
PAYLOAD = 2 * ORB + 8


def lane_index(rows):
    return lax.broadcasted_iota(jnp.int32, (rows, LANES), 1)


def rolled(value, amount):
    amount %= LANES
    return pltpu.roll(value, amount, 1) if amount else value


def rows_of(ref, cell):
    return ref[cell * ORB : (cell + 1) * ORB, :]


def face_masks(flags, rows):
    lane = lane_index(rows)
    even = flags[2] == 0
    upper = jnp.where(even, LANES - EXT, 0)
    lower = jnp.where(even, 0, LANES - EXT)
    first = (lane >= upper) & (lane < upper + EXT)
    second = (lane >= lower) & (lane < lower + EXT)
    return first, second


def load_kernel(flags, orbitals, potential, main, first, second):
    mask1, mask2 = face_masks(flags, ORB)
    row1, row2 = face_masks(flags, 1)
    first[...] = jnp.zeros_like(first)
    second[...] = jnp.zeros_like(second)
    for high in range(2):
        sums = [jnp.zeros((ORB, LANES), jnp.float32)] * 2 + [jnp.zeros((1, LANES), jnp.float32)] * 2
        for low in range(8):
            cell = 8 * high + low
            value = orbitals[pl.ds(cell, ORB, stride=CELLS), :]
            main[cell * ORB : (cell + 1) * ORB, :] = value
            local = potential[cell : cell + 1, :]
            parts = (
                jnp.where(mask1, value, 0.0),
                jnp.where(mask2, value, 0.0),
                jnp.where(row1, local, 0.0),
                jnp.where(row2, local, 0.0),
            )
            sums = [s + rolled(p, EXT * low) for s, p in zip(sums, parts)]
        first[high * ORB : (high + 1) * ORB, :] = sums[0]
        second[high * ORB : (high + 1) * ORB, :] = sums[1]
        first[2 * ORB + high : 2 * ORB + high + 1, :] = sums[2]
        second[2 * ORB + high : 2 * ORB + high + 1, :] = sums[3]


def pack_edge(values, send, x):
    total = values[0]
    for y in range(1, SIDE):
        total = total + rolled(values[y], 2 * EXT * y)
    send[BLOCK + x * ORB : BLOCK + (x + 1) * ORB, :] = total


def extend_kernel(flags, main, first, second, send, edge, edge_potential):
    mask1, mask2 = face_masks(flags, ORB)
    row1, row2 = face_masks(flags, 1)
    send[:BLOCK, :] = main[...]
    for x in range(SIDE):
        values = []
        for y in range(SIDE):
            cell = x * SIDE + y
            high, low = divmod(cell, 8)

            def unpack(start, size, keep1, keep2):
                one = rolled(first[start : start + size, :], -EXT * low)
                two = rolled(second[start : start + size, :], -EXT * low)
                return jnp.where(keep2, one, 0.0) + jnp.where(keep1, two, 0.0)

            value = unpack(high * ORB, ORB, mask1, mask2)
            edge[cell * ORB : (cell + 1) * ORB, :] = value
            edge_potential[cell : cell + 1, :] = unpack(2 * ORB + high, 1, row1, row2)
            values.append(value)
        pack_edge(values, send, x)


def step_kernel(scale, with_previous, flags, potential, edge_potential, send, edge, x1, x2, y1, y2, *rest):
    if with_previous:
        previous, previous_edge, out, out_edge, halo, halo_edge = rest
    else:
        out, out_edge, halo, halo_edge = rest
    for pair, (one, two) in enumerate(((x1, x2), (y1, y2))):
        even = flags[pair] == 0
        for cell in range(CELLS):
            a, b = rows_of(one, cell), rows_of(two, cell)
            halo[2 * pair, cell] = jnp.where(even, b, a)
            halo[2 * pair + 1, cell] = jnp.where(even, a, b)
        for x in range(SIDE):
            a = one[BLOCK + x * ORB : BLOCK + (x + 1) * ORB, :]
            b = two[BLOCK + x * ORB : BLOCK + (x + 1) * ORB, :]
            before, after = jnp.where(even, b, a), jnp.where(even, a, b)
            for y in range(SIDE):
                halo_edge[2 * pair, x * SIDE + y] = rolled(before, -2 * EXT * y)
                halo_edge[2 * pair + 1, x * SIDE + y] = rolled(after, -2 * EXT * y)
    lane = lane_index(ORB)
    inside = ((lane < EXT) & (flags[4] != 0)) | ((lane >= LANES - EXT) & (flags[3] != 0))

    def at(own, beyond, x, y):
        if x < 0:
            return beyond[0, (x + SIDE) * SIDE + y]
        if x >= SIDE:
            return beyond[1, (x - SIDE) * SIDE + y]
        if y < 0:
            return beyond[2, x * SIDE + y + SIDE]
        if y >= SIDE:
            return beyond[3, x * SIDE + y - SIDE]
        return rows_of(own, x * SIDE + y)

    for x in range(SIDE):
        values = []
        for y in range(SIDE):
            cell = x * SIDE + y
            rows = slice(cell * ORB, (cell + 1) * ORB)
            centre, centre_edge = send[rows, :], edge[rows, :]
            for own, beyond, here, there, local in (
                (send, halo, centre, centre_edge, potential),
                (edge, halo_edge, centre_edge, centre, edge_potential),
            ):
                total = (local[cell : cell + 1, :] - (MIDDLE + 1.5 * WEIGHTS[0])) * scale * here
                for k in range(1, 5):
                    pairs = at(own, beyond, x + k, y) + at(own, beyond, x - k, y)
                    pairs = pairs + at(own, beyond, x, y + k) + at(own, beyond, x, y - k)
                    pairs = pairs + rolled(jnp.where(lane < k, there, here), -k)
                    pairs = pairs + rolled(jnp.where(lane >= LANES - k, there, here), k)
                    total = total + (-0.5 * WEIGHTS[k] * scale) * pairs
                if own is send:
                    if with_previous:
                        total = total - previous[rows, :]
                    out[rows, :] = total
                else:
                    if with_previous:
                        total = total - previous_edge[rows, :]
                    total = jnp.where(inside, total, 0.0)
                    out_edge[rows, :] = total
                    values.append(total)
        pack_edge(values, out, x)


def dot(a, b, contract):
    return lax.dot_general(
        a, b, ((contract[:1], contract[1:]), ((), ())), precision=lax.Precision.HIGHEST, preferred_element_type=jnp.float32
    )


def sums_kernel(potential, field, edge, after_x, after_y, sums):
    lane = lane_index(ORB)
    total = jnp.zeros((ORB, 2 * ORB), jnp.float32)
    for x in range(SIDE):
        for y in range(SIDE):
            cell = x * SIDE + y
            here, there = rows_of(field, cell), rows_of(edge, cell)
            image = (0.5 * potential[cell : cell + 1, :] - 0.75 * WEIGHTS[0]) * here
            for k in range(1, 5):
                up = rows_of(field, cell + k * SIDE) if x + k < SIDE else rows_of(after_x, cell + (k - SIDE) * SIDE)
                up = up + (rows_of(field, cell + k) if y + k < SIDE else rows_of(after_y, cell + k - SIDE))
                up = up + rolled(jnp.where(lane < k, there, here), -k)
                image = image + (-0.5 * WEIGHTS[k]) * up
            total = total + dot(here, jnp.concatenate([here, image], axis=0), (1, 1))
    sums[...] = jnp.zeros_like(sums)
    sums[:, : 2 * ORB] = total


def finish_kernel(cell_total, sums, field, q_block, ritz):
    sums = sums[...] * (1.0 / cell_total)
    row = lax.broadcasted_iota(jnp.int32, (ORB, LANES), 0)
    lane = lane_index(ORB)
    work = jnp.where(lane < ORB, sums, jnp.where(lane == row + ORB, 1.0, 0.0))
    for k in range(ORB - 1):
        pivot = work[k : k + 1, :]
        factor = work[:, k : k + 1] / pivot[:, k : k + 1]
        work = work - jnp.where(row > k, factor, 0.0) * pivot
    diagonal = jnp.sum(jnp.where(lane == row, work, 0.0), axis=1, keepdims=True)
    inverse = (work * (1.0 / jnp.sqrt(diagonal)))[:, ORB : 2 * ORB]
    half = sums[:, ORB : 2 * ORB]
    part = dot(dot(inverse, half, (1, 0)), inverse, (1, 1))
    ritz[...] = part + part.T
    for cell in range(CELLS):
        q_block[pl.ds(cell, ORB, stride=CELLS), :] = dot(inverse, rows_of(field, cell), (1, 0))


def swap(value, axis, first):
    pairs = []
    for i in range(first, lax.axis_size(axis) - 1, 2):
        pairs += [(i, i + 1), (i + 1, i)]
    return lax.ppermute(value, axis, pairs)


def from_above(value, axis):
    return lax.ppermute(value, axis, [(i + 1, i) for i in range(lax.axis_size(axis) - 1)])


def exchange(value, axes, masks):
    size = 1
    for axis in axes:
        size *= lax.axis_size(axis)
    got = [lax.ppermute(value, axes, [(i, i ^ mask) for i in range(size)]) for mask in masks]
    if len(got) == 1:
        return value + got[0]
    return (value + got[0]) + (got[1] + got[2])


def sum_everywhere(value):
    if all(lax.axis_size(axis) == 8 for axis in ("gx", "gy", "gz")):
        value = exchange(value, ("gy",), (1,))
        value = exchange(value, ("gy",), (6, 2, 4))
        value = exchange(value, ("gz",), (3, 1, 2))
        value = exchange(value, ("gx",), (3, 1, 2))
        return exchange(value, ("gx", "gz"), (36, 32, 4))
    for axis in ("gy", "gx", "gz"):
        mask = 1
        while mask < lax.axis_size(axis):
            value = exchange(value, (axis,), (mask,))
            mask *= 2
    return value


def call(kernel, outs, scratch=(), smem=True):
    def run(*operands):
        specs = [pl.BlockSpec(memory_space=pltpu.VMEM)] * len(operands)
        if smem:
            specs[0] = pl.BlockSpec(memory_space=pltpu.SMEM)
        return pl.pallas_call(
            kernel,
            out_shape=[jax.ShapeDtypeStruct(shape, jnp.float32) for shape in outs],
            in_specs=specs,
            out_specs=[pl.BlockSpec(memory_space=pltpu.VMEM)] * len(outs),
            scratch_shapes=[pltpu.VMEM(shape, jnp.float32) for shape in scratch],
        )(*operands)

    return run


def body(orbitals, potential):
    at = [lax.axis_index(axis) for axis in ("gx", "gy", "gz")]
    cell_total = orbitals[0].size * lax.axis_size("gx") * lax.axis_size("gy") * lax.axis_size("gz")
    flags = jnp.stack(
        [at[0] % 2, at[1] % 2, at[2] % 2, (at[2] > 0).astype(jnp.int32), (at[2] < lax.axis_size("gz") - 1).astype(jnp.int32)]
    ).astype(jnp.int32)
    shape = orbitals.shape
    orbitals = orbitals.reshape(BLOCK, LANES)
    potential = potential.reshape(CELLS, LANES)
    block, sent = (BLOCK, LANES), (BLOCK + EDGE, LANES)
    halos = ((4, CELLS, ORB, LANES), (4, CELLS, ORB, LANES))

    main, first, second = call(load_kernel, (block, (PAYLOAD, LANES), (PAYLOAD, LANES)))(flags, orbitals, potential)
    first, second = swap(first, "gz", 0), swap(second, "gz", 1)
    field, edge, edge_potential = call(extend_kernel, (sent, block, (CELLS, LANES)))(flags, main, first, second)

    def advance(field, edge, scale, previous):
        y2, y1, x2, x1 = [swap(field, axis, first) for axis in ("gy", "gx") for first in (1, 0)]
        kernel = functools.partial(step_kernel, scale, bool(previous))
        return call(kernel, (sent, block), halos)(flags, potential, edge_potential, field, edge, x1, x2, y1, y2, *previous)

    states = [(field, edge)]
    states.append(advance(*states[0], 1.0 / HALF, ()))
    states.append(advance(*states[1], 2.0 / HALF, states[0]))
    states.append(advance(*states[2], 2.0 / HALF, states[1]))
    field, edge = states[3]
    field = field[:BLOCK]
    after_y, after_x = from_above(field, "gy"), from_above(field, "gx")
    sums = call(sums_kernel, ((ORB, LANES),), smem=False)(potential, field, edge, after_x, after_y)[0]
    sums = sum_everywhere(sums)
    q_block, ritz = call(functools.partial(finish_kernel, cell_total), (block, (ORB, ORB)), smem=False)(sums, field)
    return q_block.reshape(shape), ritz


def solution(mesh):
    placed = (P(None, "gx", "gy", "gz"), P("gx", "gy", "gz"))
    return jax.shard_map(
        body,
        mesh=mesh,
        in_specs=placed,
        out_specs=(P(None, "gx", "gy", "gz"), P()),
        check_vma=False,
    )
```

```python
import functools

import jax
import jax.numpy as jnp
from jax import lax
from jax.experimental import pallas as pl
from jax.experimental.pallas import tpu as pltpu
from jax.sharding import PartitionSpec as P

WEIGHTS = (-205.0 / 72.0, 8.0 / 5.0, -1.0 / 5.0, 8.0 / 315.0, -1.0 / 560.0)
HALF = (12.0 - 1.5) / 2.0
MIDDLE = (12.0 + 1.5) / 2.0
ORB = 16
SIDE = 4
CELLS = SIDE * SIDE
LANES = 128
EXT = 16
BLOCK = CELLS * ORB
EDGE = SIDE * ORB
PAYLOAD = 2 * ORB + 8


def lane_index(rows):
    return lax.broadcasted_iota(jnp.int32, (rows, LANES), 1)


def rolled(value, amount):
    amount %= LANES
    return pltpu.roll(value, amount, 1) if amount else value


def rows_of(ref, cell):
    return ref[cell * ORB : (cell + 1) * ORB, :]


def face_masks(flags, rows):
    lane = lane_index(rows)
    even = flags[2] == 0
    upper = jnp.where(even, LANES - EXT, 0)
    lower = jnp.where(even, 0, LANES - EXT)
    first = (lane >= upper) & (lane < upper + EXT)
    second = (lane >= lower) & (lane < lower + EXT)
    return first, second


def load_kernel(flags, orbitals, potential, main, first, second):
    mask1, mask2 = face_masks(flags, ORB)
    row1, row2 = face_masks(flags, 1)
    first[...] = jnp.zeros_like(first)
    second[...] = jnp.zeros_like(second)
    for high in range(2):
        sums = [jnp.zeros((ORB, LANES), jnp.float32)] * 2 + [jnp.zeros((1, LANES), jnp.float32)] * 2
        for low in range(8):
            cell = 8 * high + low
            value = orbitals[pl.ds(cell, ORB, stride=CELLS), :]
            main[cell * ORB : (cell + 1) * ORB, :] = value
            local = potential[cell : cell + 1, :]
            parts = (
                jnp.where(mask1, value, 0.0),
                jnp.where(mask2, value, 0.0),
                jnp.where(row1, local, 0.0),
                jnp.where(row2, local, 0.0),
            )
            sums = [s + rolled(p, EXT * low) for s, p in zip(sums, parts)]
        first[high * ORB : (high + 1) * ORB, :] = sums[0]
        second[high * ORB : (high + 1) * ORB, :] = sums[1]
        first[2 * ORB + high : 2 * ORB + high + 1, :] = sums[2]
        second[2 * ORB + high : 2 * ORB + high + 1, :] = sums[3]


def pack_edge(values, send, x):
    total = values[0]
    for y in range(1, SIDE):
        total = total + rolled(values[y], 2 * EXT * y)
    send[BLOCK + x * ORB : BLOCK + (x + 1) * ORB, :] = total


def extend_kernel(flags, main, first, second, send, edge, edge_potential):
    mask1, mask2 = face_masks(flags, ORB)
    row1, row2 = face_masks(flags, 1)
    send[:BLOCK, :] = main[...]
    for x in range(SIDE):
        values = []
        for y in range(SIDE):
            cell = x * SIDE + y
            high, low = divmod(cell, 8)

            def unpack(start, size, keep1, keep2):
                one = rolled(first[start : start + size, :], -EXT * low)
                two = rolled(second[start : start + size, :], -EXT * low)
                return jnp.where(keep2, one, 0.0) + jnp.where(keep1, two, 0.0)

            value = unpack(high * ORB, ORB, mask1, mask2)
            edge[cell * ORB : (cell + 1) * ORB, :] = value
            edge_potential[cell : cell + 1, :] = unpack(2 * ORB + high, 1, row1, row2)
            values.append(value)
        pack_edge(values, send, x)


def step_kernel(scale, with_previous, flags, potential, edge_potential, send, edge, y1, x2, y2, x1, *rest):
    if with_previous:
        previous, previous_edge, out, out_edge, halo, halo_edge = rest
    else:
        out, out_edge, halo, halo_edge = rest
    for pair, (one, two) in enumerate(((x1, x2), (y1, y2))):
        even = flags[pair] == 0
        for cell in range(CELLS):
            a, b = rows_of(one, cell), rows_of(two, cell)
            halo[2 * pair, cell] = jnp.where(even, b, a)
            halo[2 * pair + 1, cell] = jnp.where(even, a, b)
        for x in range(SIDE):
            a = one[BLOCK + x * ORB : BLOCK + (x + 1) * ORB, :]
            b = two[BLOCK + x * ORB : BLOCK + (x + 1) * ORB, :]
            before, after = jnp.where(even, b, a), jnp.where(even, a, b)
            for y in range(SIDE):
                halo_edge[2 * pair, x * SIDE + y] = rolled(before, -2 * EXT * y)
                halo_edge[2 * pair + 1, x * SIDE + y] = rolled(after, -2 * EXT * y)
    lane = lane_index(ORB)
    inside = ((lane < EXT) & (flags[4] != 0)) | ((lane >= LANES - EXT) & (flags[3] != 0))

    def at(own, beyond, x, y):
        if x < 0:
            return beyond[0, (x + SIDE) * SIDE + y]
        if x >= SIDE:
            return beyond[1, (x - SIDE) * SIDE + y]
        if y < 0:
            return beyond[2, x * SIDE + y + SIDE]
        if y >= SIDE:
            return beyond[3, x * SIDE + y - SIDE]
        return rows_of(own, x * SIDE + y)

    for x in range(SIDE):
        values = []
        for y in range(SIDE):
            cell = x * SIDE + y
            rows = slice(cell * ORB, (cell + 1) * ORB)
            centre, centre_edge = send[rows, :], edge[rows, :]
            for own, beyond, here, there, local in (
                (send, halo, centre, centre_edge, potential),
                (edge, halo_edge, centre_edge, centre, edge_potential),
            ):
                total = (local[cell : cell + 1, :] - (MIDDLE + 1.5 * WEIGHTS[0])) * scale * here
                for k in range(1, 5):
                    pairs = at(own, beyond, x + k, y) + at(own, beyond, x - k, y)
                    pairs = pairs + at(own, beyond, x, y + k) + at(own, beyond, x, y - k)
                    pairs = pairs + rolled(jnp.where(lane < k, there, here), -k)
                    pairs = pairs + rolled(jnp.where(lane >= LANES - k, there, here), k)
                    total = total + (-0.5 * WEIGHTS[k] * scale) * pairs
                if own is send:
                    if with_previous:
                        total = total - previous[rows, :]
                    out[rows, :] = total
                else:
                    if with_previous:
                        total = total - previous_edge[rows, :]
                    total = jnp.where(inside, total, 0.0)
                    out_edge[rows, :] = total
                    values.append(total)
        pack_edge(values, out, x)


def dot(a, b, contract):
    return lax.dot_general(
        a, b, ((contract[:1], contract[1:]), ((), ())), precision=lax.Precision.HIGHEST, preferred_element_type=jnp.float32
    )


def sums_kernel(potential, field, edge, after_x, after_y, sums):
    lane = lane_index(ORB)
    total = jnp.zeros((ORB, 2 * ORB), jnp.float32)
    for x in range(SIDE):
        for y in range(SIDE):
            cell = x * SIDE + y
            here, there = rows_of(field, cell), rows_of(edge, cell)
            image = (0.5 * potential[cell : cell + 1, :] - 0.75 * WEIGHTS[0]) * here
            for k in range(1, 5):
                up = rows_of(field, cell + k * SIDE) if x + k < SIDE else rows_of(after_x, cell + (k - SIDE) * SIDE)
                up = up + (rows_of(field, cell + k) if y + k < SIDE else rows_of(after_y, cell + k - SIDE))
                up = up + rolled(jnp.where(lane < k, there, here), -k)
                image = image + (-0.5 * WEIGHTS[k]) * up
            total = total + dot(here, jnp.concatenate([here, image], axis=0), (1, 1))
    sums[...] = jnp.zeros_like(sums)
    sums[:, : 2 * ORB] = total


def finish_kernel(cell_total, sums, field, q_block, ritz):
    sums = sums[...] * (1.0 / cell_total)
    row = lax.broadcasted_iota(jnp.int32, (ORB, LANES), 0)
    lane = lane_index(ORB)
    work = jnp.where(lane < ORB, sums, jnp.where(lane == row + ORB, 1.0, 0.0))
    for k in range(ORB - 1):
        pivot = work[k : k + 1, :]
        factor = work[:, k : k + 1] / pivot[:, k : k + 1]
        work = work - jnp.where(row > k, factor, 0.0) * pivot
    diagonal = jnp.sum(jnp.where(lane == row, work, 0.0), axis=1, keepdims=True)
    inverse = (work * (1.0 / jnp.sqrt(diagonal)))[:, ORB : 2 * ORB]
    half = sums[:, ORB : 2 * ORB]
    part = dot(dot(inverse, half, (1, 0)), inverse, (1, 1))
    ritz[...] = part + part.T
    for cell in range(CELLS):
        q_block[pl.ds(cell, ORB, stride=CELLS), :] = dot(inverse, rows_of(field, cell), (1, 0))


def swap(value, axis, first):
    pairs = []
    for i in range(first, lax.axis_size(axis) - 1, 2):
        pairs += [(i, i + 1), (i + 1, i)]
    return lax.ppermute(value, axis, pairs)


def from_above(value, axis):
    return lax.ppermute(value, axis, [(i + 1, i) for i in range(lax.axis_size(axis) - 1)])


def exchange(value, axes, mask):
    size = 1
    for axis in axes:
        size *= lax.axis_size(axis)
    return value + lax.ppermute(value, axes, [(i, i ^ mask) for i in range(size)])


def sum_everywhere(value):
    if all(lax.axis_size(axis) == 8 for axis in ("gx", "gy", "gz")):
        stages = (
            (("gy",), 1), (("gy",), 2), (("gy",), 6), (("gz",), 1), (("gz",), 3),
            (("gx",), 1), (("gx",), 2), (("gx",), 4), (("gx", "gz"), 36),
        )
    else:
        stages = [((axis,), 1 << bit) for axis in ("gy", "gx", "gz") for bit in range(lax.axis_size(axis).bit_length() - 1)]
    for axes, mask in stages:
        value = exchange(value, axes, mask)
    return value


def call(kernel, outs, scratch=(), smem=True):
    def run(*operands):
        specs = [pl.BlockSpec(memory_space=pltpu.VMEM)] * len(operands)
        if smem:
            specs[0] = pl.BlockSpec(memory_space=pltpu.SMEM)
        return pl.pallas_call(
            kernel,
            out_shape=[jax.ShapeDtypeStruct(shape, jnp.float32) for shape in outs],
            in_specs=specs,
            out_specs=[pl.BlockSpec(memory_space=pltpu.VMEM)] * len(outs),
            scratch_shapes=[pltpu.VMEM(shape, jnp.float32) for shape in scratch],
        )(*operands)

    return run


def body(orbitals, potential):
    at = [lax.axis_index(axis) for axis in ("gx", "gy", "gz")]
    cell_total = orbitals[0].size * lax.axis_size("gx") * lax.axis_size("gy") * lax.axis_size("gz")
    flags = jnp.stack(
        [at[0] % 2, at[1] % 2, at[2] % 2, (at[2] > 0).astype(jnp.int32), (at[2] < lax.axis_size("gz") - 1).astype(jnp.int32)]
    ).astype(jnp.int32)
    shape = orbitals.shape
    orbitals = orbitals.reshape(BLOCK, LANES)
    potential = potential.reshape(CELLS, LANES)
    block, sent = (BLOCK, LANES), (BLOCK + EDGE, LANES)
    halos = ((4, CELLS, ORB, LANES), (4, CELLS, ORB, LANES))

    main, first, second = call(load_kernel, (block, (PAYLOAD, LANES), (PAYLOAD, LANES)))(flags, orbitals, potential)
    first, second = swap(first, "gz", 0), swap(second, "gz", 1)
    field, edge, edge_potential = call(extend_kernel, (sent, block, (CELLS, LANES)))(flags, main, first, second)

    def advance(field, edge, scale, previous):
        y2, y1, x2, x1 = [swap(field, axis, first) for axis in ("gy", "gx") for first in (1, 0)]
        kernel = functools.partial(step_kernel, scale, bool(previous))
        return call(kernel, (sent, block), halos)(flags, potential, edge_potential, field, edge, y1, x2, y2, x1, *previous)

    states = [(field, edge)]
    states.append(advance(*states[0], 1.0 / HALF, ()))
    states.append(advance(*states[1], 2.0 / HALF, states[0]))
    states.append(advance(*states[2], 2.0 / HALF, states[1]))
    field, edge = states[3]
    field = field[:BLOCK]
    after_y, after_x = from_above(field, "gy"), from_above(field, "gx")
    sums = call(sums_kernel, ((ORB, LANES),), smem=False)(potential, field, edge, after_x, after_y)[0]
    sums = sum_everywhere(sums)
    q_block, ritz = call(functools.partial(finish_kernel, cell_total), (block, (ORB, ORB)), smem=False)(sums, field)
    return q_block.reshape(shape), ritz


def solution(mesh):
    placed = (P(None, "gx", "gy", "gz"), P("gx", "gy", "gz"))
    return jax.shard_map(
        body,
        mesh=mesh,
        in_specs=placed,
        out_specs=(P(None, "gx", "gy", "gz"), P()),
        check_vma=False,
    )
```

```python
import functools

import jax
import jax.numpy as jnp
from jax import lax
from jax.experimental import pallas as pl
from jax.experimental.pallas import tpu as pltpu
from jax.sharding import PartitionSpec as P

WEIGHTS = (-205.0 / 72.0, 8.0 / 5.0, -1.0 / 5.0, 8.0 / 315.0, -1.0 / 560.0)
HALF = (12.0 - 1.5) / 2.0
MIDDLE = (12.0 + 1.5) / 2.0
ORB = 16
SIDE = 4
CELLS = SIDE * SIDE
LANES = 128
EXT = 16
BLOCK = CELLS * ORB
EDGE = SIDE * ORB
PAYLOAD = 2 * ORB + 8


def lane_index(rows):
    return lax.broadcasted_iota(jnp.int32, (rows, LANES), 1)


def rolled(value, amount):
    amount %= LANES
    return pltpu.roll(value, amount, 1) if amount else value


def rows_of(ref, cell):
    return ref[cell * ORB : (cell + 1) * ORB, :]


def face_masks(flags, rows):
    lane = lane_index(rows)
    even = flags[2] == 0
    upper = jnp.where(even, LANES - EXT, 0)
    lower = jnp.where(even, 0, LANES - EXT)
    first = (lane >= upper) & (lane < upper + EXT)
    second = (lane >= lower) & (lane < lower + EXT)
    return first, second


def payload_kernel(flags, orbitals, potential, first, second):
    mask1, mask2 = face_masks(flags, ORB)
    row1, row2 = face_masks(flags, 1)
    for high in range(2):
        sums = [jnp.zeros((ORB, LANES), jnp.float32)] * 2 + [jnp.zeros((1, LANES), jnp.float32)] * 2
        for low in range(8):
            cell = 8 * high + low
            value = orbitals[pl.ds(cell, ORB, stride=CELLS), :]
            local = potential[cell : cell + 1, :]
            parts = (
                jnp.where(mask1, value, 0.0),
                jnp.where(mask2, value, 0.0),
                jnp.where(row1, local, 0.0),
                jnp.where(row2, local, 0.0),
            )
            sums = [s + rolled(p, EXT * low) for s, p in zip(sums, parts)]
        for out, value, local in ((first, sums[0], sums[2]), (second, sums[1], sums[3])):
            out[high * ORB : (high + 1) * ORB, :] = value
            out[2 * ORB + high : 2 * ORB + high + 1, :] = local
    for out in (first, second):
        out[2 * ORB + 2 :, :] = jnp.zeros((PAYLOAD - 2 * ORB - 2, LANES), jnp.float32)


def extend_kernel(flags, orbitals, first, second, field, edge_potential):
    mask1, mask2 = face_masks(flags, ORB)
    row1, row2 = face_masks(flags, 1)
    for cell in range(CELLS):
        field[cell * ORB : (cell + 1) * ORB, :] = orbitals[pl.ds(cell, ORB, stride=CELLS), :]
    for x in range(SIDE):
        total, total_potential = 0.0, 0.0
        for y in range(SIDE):
            high, low = divmod(x * SIDE + y, 8)

            def unpack(start, size, keep1, keep2):
                one = rolled(first[start : start + size, :], -EXT * low)
                two = rolled(second[start : start + size, :], -EXT * low)
                return rolled(jnp.where(keep2, one, 0.0) + jnp.where(keep1, two, 0.0), 2 * EXT * y)

            total = total + unpack(high * ORB, ORB, mask1, mask2)
            total_potential = total_potential + unpack(2 * ORB + high, 1, row1, row2)
        field[BLOCK + x * ORB : BLOCK + (x + 1) * ORB, :] = total
        edge_potential[x : x + 1, :] = total_potential


def edge_of(ref, x):
    return ref[x * ORB : (x + 1) * ORB, :]


def step_kernel(scale, with_previous, split, flags, potential, edge_potential, field, y1, x2, y2, x1, *rest):
    previous = rest[0] if with_previous else None
    out = rest[-2] if split else rest[-1]
    lane = lane_index(ORB)
    place = lane % (2 * EXT)
    lane_y = ((lane + EXT) // (2 * EXT)) % SIDE
    inside = ((place < EXT) & (flags[4] != 0)) | ((place >= EXT) & (flags[3] != 0))
    window = (lane < EXT) | (lane >= LANES - EXT)
    even_x, even_y = flags[0] == 0, flags[1] == 0
    weight = [-0.5 * scale * w for w in WEIGHTS]
    shift = MIDDLE + 1.5 * WEIGHTS[0]

    def line(get, one, two, even):
        pairs = [(get(one, i), get(two, i)) for i in range(SIDE)]
        below = [jnp.where(even, b, a) for a, b in pairs]
        above = [jnp.where(even, a, b) for a, b in pairs]
        return below + [get(field, i) for i in range(SIDE)] + above

    for y in range(SIDE):
        along = line(lambda ref, x: rows_of(ref, x * SIDE + y), x1, x2, even_x)
        for x in range(SIDE):
            cell = x * SIDE + y
            here = along[SIDE + x]
            there = rolled(edge_of(field, CELLS + x), -2 * EXT * y)
            total = (potential[cell : cell + 1, :] - shift) * scale * here
            for k in range(1, 5):
                pairs = along[SIDE + x + k] + along[SIDE + x - k]
                pairs = pairs + rolled(jnp.where(lane < k, there, here), -k)
                pairs = pairs + rolled(jnp.where(lane >= LANES - k, there, here), k)
                total = total + weight[k] * pairs
            if with_previous:
                total = total - rows_of(previous, cell)
            out[cell * ORB : (cell + 1) * ORB, :] = total
    for x in range(SIDE):
        along = line(lambda ref, y: rows_of(ref, x * SIDE + y), y1, y2, even_y)
        for y in range(SIDE):
            cell = x * SIDE + y
            total = rows_of(out, cell)
            for k in range(1, 5):
                total = total + weight[k] * (along[SIDE + y + k] + along[SIDE + y - k])
            out[cell * ORB : (cell + 1) * ORB, :] = total
    along = line(lambda ref, x: edge_of(ref, CELLS + x), x1, x2, even_x)
    for x in range(SIDE):
        here = along[SIDE + x]
        one, two = edge_of(y1, CELLS + x), edge_of(y2, CELLS + x)
        below, above = jnp.where(even_y, two, one), jnp.where(even_y, one, two)
        there = 0.0
        for y in range(SIDE):
            there = there + rolled(jnp.where(window, rows_of(field, x * SIDE + y), 0.0), 2 * EXT * y)
        total = (edge_potential[x : x + 1, :] - shift) * scale * here
        for k in range(1, 5):
            pairs = along[SIDE + x + k] + along[SIDE + x - k]
            pairs = pairs + rolled(jnp.where(lane_y < k, above, here), -2 * EXT * k)
            pairs = pairs + rolled(jnp.where(lane_y >= SIDE - k, below, here), 2 * EXT * k)
            pairs = pairs + rolled(jnp.where(place < k, there, here), -k)
            pairs = pairs + rolled(jnp.where(place >= 2 * EXT - k, there, here), k)
            total = total + weight[k] * pairs
        if with_previous:
            total = total - edge_of(previous, CELLS + x)
        total = jnp.where(inside, total, 0.0)
        if split:
            rest[-1][x * ORB : (x + 1) * ORB, :] = total
        else:
            out[BLOCK + x * ORB : BLOCK + (x + 1) * ORB, :] = total


def dot(a, b, contract):
    return lax.dot_general(
        a, b, ((contract[:1], contract[1:]), ((), ())), precision=lax.Precision.HIGHEST, preferred_element_type=jnp.float32
    )


def sums_kernel(potential, field, edge, after_x, after_y, sums):
    lane = lane_index(ORB)
    here_all, image_all = [], []
    for x in range(SIDE):
        for y in range(SIDE):
            cell = x * SIDE + y
            here, there = rows_of(field, cell), rolled(edge_of(edge, x), -2 * EXT * y)
            image = (0.5 * potential[cell : cell + 1, :] - 0.75 * WEIGHTS[0]) * here
            for k in range(1, 5):
                up = rows_of(field, cell + k * SIDE) if x + k < SIDE else rows_of(after_x, cell + (k - SIDE) * SIDE)
                up = up + (rows_of(field, cell + k) if y + k < SIDE else rows_of(after_y, cell + k - SIDE))
                up = up + rolled(jnp.where(lane < k, there, here), -k)
                image = image + (-0.5 * WEIGHTS[k]) * up
            here_all.append(here)
            image_all.append(image)
    here = jnp.concatenate(here_all, axis=1)
    image = jnp.concatenate(image_all, axis=1)
    sums[...] = jnp.zeros_like(sums)
    sums[:, : 2 * ORB] = dot(here, jnp.concatenate([here, image], axis=0), (1, 1))


def finish_kernel(cell_total, sums, field, q_block, ritz):
    sums = sums[...] * (1.0 / cell_total)
    row = lax.broadcasted_iota(jnp.int32, (ORB, LANES), 0)
    lane = lane_index(ORB)
    work = jnp.where(lane < ORB, sums, jnp.where(lane == row + ORB, 1.0, 0.0))
    for k in range(ORB - 1):
        pivot = work[k : k + 1, :]
        factor = work[:, k : k + 1] / pivot[:, k : k + 1]
        work = work - jnp.where(row > k, factor, 0.0) * pivot
    diagonal = jnp.sum(jnp.where(lane == row, work, 0.0), axis=1, keepdims=True)
    inverse = (work * (1.0 / jnp.sqrt(diagonal)))[:, ORB : 2 * ORB]
    half = sums[:, ORB : 2 * ORB]
    part = dot(dot(inverse, half, (1, 0)), inverse, (1, 1))
    ritz[...] = part + part.T
    for cell in range(CELLS):
        q_block[pl.ds(cell, ORB, stride=CELLS), :] = dot(inverse, rows_of(field, cell), (1, 0))


def swap(value, axis, first):
    pairs = []
    for i in range(first, lax.axis_size(axis) - 1, 2):
        pairs += [(i, i + 1), (i + 1, i)]
    return lax.ppermute(value, axis, pairs)


def from_above(value, axis):
    return lax.ppermute(value, axis, [(i + 1, i) for i in range(lax.axis_size(axis) - 1)])


def exchange(value, axes, mask):
    size = 1
    for axis in axes:
        size *= lax.axis_size(axis)
    return value + lax.ppermute(value, axes, [(i, i ^ mask) for i in range(size)])


def sum_everywhere(value):
    if all(lax.axis_size(axis) == 8 for axis in ("gx", "gy", "gz")):
        stages = (
            (("gy",), 1), (("gy",), 2), (("gy",), 6), (("gz",), 1), (("gz",), 3),
            (("gx",), 1), (("gx",), 2), (("gx",), 4), (("gx", "gz"), 36),
        )
    else:
        stages = [((axis,), 1 << bit) for axis in ("gy", "gx", "gz") for bit in range(lax.axis_size(axis).bit_length() - 1)]
    for axes, mask in stages:
        value = exchange(value, axes, mask)
    return value


def call(kernel, outs, smem=True):
    def run(*operands):
        specs = [pl.BlockSpec(memory_space=pltpu.VMEM)] * len(operands)
        if smem:
            specs[0] = pl.BlockSpec(memory_space=pltpu.SMEM)
        return pl.pallas_call(
            kernel,
            out_shape=[jax.ShapeDtypeStruct(shape, jnp.float32) for shape in outs],
            in_specs=specs,
            out_specs=[pl.BlockSpec(memory_space=pltpu.VMEM)] * len(outs),
            compiler_params=pltpu.CompilerParams(vmem_limit_bytes=8 * 1024 * 1024),
        )(*operands)

    return run


def body(orbitals, potential):
    at = [lax.axis_index(axis) for axis in ("gx", "gy", "gz")]
    cell_total = orbitals[0].size * lax.axis_size("gx") * lax.axis_size("gy") * lax.axis_size("gz")
    flags = jnp.stack(
        [at[0] % 2, at[1] % 2, at[2] % 2, (at[2] > 0).astype(jnp.int32), (at[2] < lax.axis_size("gz") - 1).astype(jnp.int32)]
    ).astype(jnp.int32)
    shape = orbitals.shape
    orbitals = orbitals.reshape(BLOCK, LANES)
    potential = potential.reshape(CELLS, LANES)
    block, edge, sent = (BLOCK, LANES), (EDGE, LANES), (BLOCK + EDGE, LANES)

    first, second = call(payload_kernel, ((PAYLOAD, LANES),) * 2)(flags, orbitals, potential)
    second, first = swap(second, "gz", 1), swap(first, "gz", 0)
    field, edge_potential = call(extend_kernel, (sent, (8, LANES)))(flags, orbitals, first, second)

    def advance(field, scale, previous, split):
        y2, y1, x2, x1 = [swap(field, axis, first) for axis in ("gy", "gx") for first in (1, 0)]
        kernel = functools.partial(step_kernel, scale, bool(previous), split)
        outs = (block, edge) if split else (sent,)
        return call(kernel, outs)(flags, potential, edge_potential, field, y1, x2, y2, x1, *previous)

    (field1,) = advance(field, 1.0 / HALF, (), False)
    (field2,) = advance(field1, 2.0 / HALF, (field,), False)
    field, edge = advance(field2, 2.0 / HALF, (field1,), True)
    after_y, after_x = from_above(field, "gy"), from_above(field, "gx")
    sums = call(sums_kernel, ((ORB, LANES),), smem=False)(potential, field, edge, after_x, after_y)[0]
    sums = sum_everywhere(sums)
    q_block, ritz = call(functools.partial(finish_kernel, cell_total), (block, (ORB, ORB)), smem=False)(sums, field)
    return q_block.reshape(shape), ritz


def solution(mesh):
    placed = (P(None, "gx", "gy", "gz"), P("gx", "gy", "gz"))
    return jax.shard_map(
        body,
        mesh=mesh,
        in_specs=placed,
        out_specs=(P(None, "gx", "gy", "gz"), P()),
        check_vma=False,
    )
```

```python
import functools

import jax
import jax.numpy as jnp
from jax import lax
from jax.experimental import pallas as pl
from jax.experimental.pallas import tpu as pltpu
from jax.sharding import PartitionSpec as P

WEIGHTS = (-205.0 / 72.0, 8.0 / 5.0, -1.0 / 5.0, 8.0 / 315.0, -1.0 / 560.0)
HALF = (12.0 - 1.5) / 2.0
MIDDLE = (12.0 + 1.5) / 2.0
ORB = 16
SIDE = 4
CELLS = SIDE * SIDE
LANES = 128
EXT = 16
BLOCK = CELLS * ORB
EDGE = SIDE * ORB
PAYLOAD = 2 * ORB + 8


def lane_index(rows):
    return lax.broadcasted_iota(jnp.int32, (rows, LANES), 1)


def rolled(value, amount):
    amount %= LANES
    return pltpu.roll(value, amount, 1) if amount else value


def rows_of(ref, cell):
    return ref[cell * ORB : (cell + 1) * ORB, :]


def face_masks(flags, rows):
    lane = lane_index(rows)
    even = flags[2] == 0
    upper = jnp.where(even, LANES - EXT, 0)
    lower = jnp.where(even, 0, LANES - EXT)
    first = (lane >= upper) & (lane < upper + EXT)
    second = (lane >= lower) & (lane < lower + EXT)
    return first, second


def payload_kernel(flags, orbitals, potential, first, second):
    mask1, mask2 = face_masks(flags, ORB)
    row1, row2 = face_masks(flags, 1)
    for high in range(2):
        sums = [jnp.zeros((ORB, LANES), jnp.float32)] * 2 + [jnp.zeros((1, LANES), jnp.float32)] * 2
        for low in range(8):
            cell = 8 * high + low
            value = orbitals[pl.ds(cell, ORB, stride=CELLS), :]
            local = potential[cell : cell + 1, :]
            parts = (
                jnp.where(mask1, value, 0.0),
                jnp.where(mask2, value, 0.0),
                jnp.where(row1, local, 0.0),
                jnp.where(row2, local, 0.0),
            )
            sums = [s + rolled(p, EXT * low) for s, p in zip(sums, parts)]
        for out, value, local in ((first, sums[0], sums[2]), (second, sums[1], sums[3])):
            out[high * ORB : (high + 1) * ORB, :] = value
            out[2 * ORB + high : 2 * ORB + high + 1, :] = local
    for out in (first, second):
        out[2 * ORB + 2 :, :] = jnp.zeros((PAYLOAD - 2 * ORB - 2, LANES), jnp.float32)


def extend_kernel(flags, orbitals, second, first, field, edge_potential):
    mask1, mask2 = face_masks(flags, ORB)
    row1, row2 = face_masks(flags, 1)
    for cell in range(CELLS):
        field[cell * ORB : (cell + 1) * ORB, :] = orbitals[pl.ds(cell, ORB, stride=CELLS), :]
    for x in range(SIDE):
        total, total_potential = 0.0, 0.0
        for y in range(SIDE):
            high, low = divmod(x * SIDE + y, 8)

            def unpack(start, size, keep1, keep2):
                one = rolled(first[start : start + size, :], -EXT * low)
                two = rolled(second[start : start + size, :], -EXT * low)
                return rolled(jnp.where(keep2, one, 0.0) + jnp.where(keep1, two, 0.0), 2 * EXT * y)

            total = total + unpack(high * ORB, ORB, mask1, mask2)
            total_potential = total_potential + unpack(2 * ORB + high, 1, row1, row2)
        field[BLOCK + x * ORB : BLOCK + (x + 1) * ORB, :] = total
        edge_potential[x : x + 1, :] = total_potential


def edge_of(ref, x):
    return ref[x * ORB : (x + 1) * ORB, :]


def step_kernel(scale, with_previous, split, flags, potential, edge_potential, field, y1, x2, y2, x1, *rest):
    previous = rest[0] if with_previous else None
    out = rest[-2] if split else rest[-1]
    lane = lane_index(ORB)
    place = lane % (2 * EXT)
    lane_y = ((lane + EXT) // (2 * EXT)) % SIDE
    inside = ((place < EXT) & (flags[4] != 0)) | ((place >= EXT) & (flags[3] != 0))
    window = (lane < EXT) | (lane >= LANES - EXT)
    even_x, even_y = flags[0] == 0, flags[1] == 0
    weight = [-0.5 * scale * w for w in WEIGHTS]
    shift = MIDDLE + 1.5 * WEIGHTS[0]

    def line(get, one, two, even):
        pairs = [(get(one, i), get(two, i)) for i in range(SIDE)]
        below = [jnp.where(even, b, a) for a, b in pairs]
        above = [jnp.where(even, a, b) for a, b in pairs]
        return below + [get(field, i) for i in range(SIDE)] + above

    for y in range(SIDE):
        along = line(lambda ref, x: rows_of(ref, x * SIDE + y), x1, x2, even_x)
        for x in range(SIDE):
            cell = x * SIDE + y
            here = along[SIDE + x]
            there = rolled(edge_of(field, CELLS + x), -2 * EXT * y)
            total = (potential[cell : cell + 1, :] - shift) * scale * here
            for k in range(1, 5):
                pairs = along[SIDE + x + k] + along[SIDE + x - k]
                pairs = pairs + rolled(jnp.where(lane < k, there, here), -k)
                pairs = pairs + rolled(jnp.where(lane >= LANES - k, there, here), k)
                total = total + weight[k] * pairs
            if with_previous:
                total = total - rows_of(previous, cell)
            out[cell * ORB : (cell + 1) * ORB, :] = total
    for x in range(SIDE):
        along = line(lambda ref, y: rows_of(ref, x * SIDE + y), y1, y2, even_y)
        for y in range(SIDE):
            cell = x * SIDE + y
            total = rows_of(out, cell)
            for k in range(1, 5):
                total = total + weight[k] * (along[SIDE + y + k] + along[SIDE + y - k])
            out[cell * ORB : (cell + 1) * ORB, :] = total
    along = line(lambda ref, x: edge_of(ref, CELLS + x), x1, x2, even_x)
    for x in range(SIDE):
        here = along[SIDE + x]
        one, two = edge_of(y1, CELLS + x), edge_of(y2, CELLS + x)
        below, above = jnp.where(even_y, two, one), jnp.where(even_y, one, two)
        there = 0.0
        for y in range(SIDE):
            there = there + rolled(jnp.where(window, rows_of(field, x * SIDE + y), 0.0), 2 * EXT * y)
        total = (edge_potential[x : x + 1, :] - shift) * scale * here
        for k in range(1, 5):
            pairs = along[SIDE + x + k] + along[SIDE + x - k]
            pairs = pairs + rolled(jnp.where(lane_y < k, above, here), -2 * EXT * k)
            pairs = pairs + rolled(jnp.where(lane_y >= SIDE - k, below, here), 2 * EXT * k)
            pairs = pairs + rolled(jnp.where(place < k, there, here), -k)
            pairs = pairs + rolled(jnp.where(place >= 2 * EXT - k, there, here), k)
            total = total + weight[k] * pairs
        if with_previous:
            total = total - edge_of(previous, CELLS + x)
        total = jnp.where(inside, total, 0.0)
        if split:
            rest[-1][x * ORB : (x + 1) * ORB, :] = total
        else:
            out[BLOCK + x * ORB : BLOCK + (x + 1) * ORB, :] = total


def dot(a, b, contract):
    return lax.dot_general(
        a, b, ((contract[:1], contract[1:]), ((), ())), precision=lax.Precision.HIGHEST, preferred_element_type=jnp.float32
    )


def sums_kernel(potential, field, edge, after_y, after_x, sums):
    lane = lane_index(ORB)
    here_all, image_all = [], []
    for x in range(SIDE):
        for y in range(SIDE):
            cell = x * SIDE + y
            here, there = rows_of(field, cell), rolled(edge_of(edge, x), -2 * EXT * y)
            image = (0.5 * potential[cell : cell + 1, :] - 0.75 * WEIGHTS[0]) * here
            for k in range(1, 5):
                up = rows_of(field, cell + k * SIDE) if x + k < SIDE else rows_of(after_x, cell + (k - SIDE) * SIDE)
                up = up + (rows_of(field, cell + k) if y + k < SIDE else rows_of(after_y, cell + k - SIDE))
                up = up + rolled(jnp.where(lane < k, there, here), -k)
                image = image + (-0.5 * WEIGHTS[k]) * up
            here_all.append(here)
            image_all.append(image)
    here = jnp.concatenate(here_all, axis=1)
    image = jnp.concatenate(image_all, axis=1)
    sums[...] = jnp.zeros_like(sums)
    sums[:, : 2 * ORB] = dot(here, jnp.concatenate([here, image], axis=0), (1, 1))


def finish_kernel(cell_total, sums, field, q_block, ritz):
    sums = sums[...] * (1.0 / cell_total)
    row = lax.broadcasted_iota(jnp.int32, (ORB, LANES), 0)
    lane = lane_index(ORB)
    work = jnp.where(lane < ORB, sums, jnp.where(lane == row + ORB, 1.0, 0.0))
    for k in range(ORB - 1):
        pivot = work[k : k + 1, :]
        factor = work[:, k : k + 1] / pivot[:, k : k + 1]
        work = work - jnp.where(row > k, factor, 0.0) * pivot
    diagonal = jnp.sum(jnp.where(lane == row, work, 0.0), axis=1, keepdims=True)
    inverse = (work * (1.0 / jnp.sqrt(diagonal)))[:, ORB : 2 * ORB]
    half = sums[:, ORB : 2 * ORB]
    part = dot(dot(inverse, half, (1, 0)), inverse, (1, 1))
    ritz[...] = part + part.T
    for cell in range(CELLS):
        q_block[pl.ds(cell, ORB, stride=CELLS), :] = dot(inverse, rows_of(field, cell), (1, 0))


def swap(value, axis, first):
    pairs = []
    for i in range(first, lax.axis_size(axis) - 1, 2):
        pairs += [(i, i + 1), (i + 1, i)]
    return lax.ppermute(value, axis, pairs)


def from_above(value, axis):
    return lax.ppermute(value, axis, [(i + 1, i) for i in range(lax.axis_size(axis) - 1)])


def exchange(value, axes, mask):
    size = 1
    for axis in axes:
        size *= lax.axis_size(axis)
    return value + lax.ppermute(value, axes, [(i, i ^ mask) for i in range(size)])


def sum_everywhere(value):
    if all(lax.axis_size(axis) == 8 for axis in ("gx", "gy", "gz")):
        value = lax.psum(value, "gy")
        stages = (
            (("gz",), 1), (("gz",), 3),
            (("gx",), 1), (("gx",), 2), (("gx",), 4), (("gx", "gz"), 36),
        )
    else:
        stages = [((axis,), 1 << bit) for axis in ("gy", "gx", "gz") for bit in range(lax.axis_size(axis).bit_length() - 1)]
    for axes, mask in stages:
        value = exchange(value, axes, mask)
    return value


def call(kernel, outs, smem=True):
    def run(*operands):
        specs = [pl.BlockSpec(memory_space=pltpu.VMEM)] * len(operands)
        if smem:
            specs[0] = pl.BlockSpec(memory_space=pltpu.SMEM)
        return pl.pallas_call(
            kernel,
            out_shape=[jax.ShapeDtypeStruct(shape, jnp.float32) for shape in outs],
            in_specs=specs,
            out_specs=[pl.BlockSpec(memory_space=pltpu.VMEM)] * len(outs),
            compiler_params=pltpu.CompilerParams(vmem_limit_bytes=8 * 1024 * 1024),
        )(*operands)

    return run


def body(orbitals, potential):
    at = [lax.axis_index(axis) for axis in ("gx", "gy", "gz")]
    cell_total = orbitals[0].size * lax.axis_size("gx") * lax.axis_size("gy") * lax.axis_size("gz")
    flags = jnp.stack(
        [at[0] % 2, at[1] % 2, at[2] % 2, (at[2] > 0).astype(jnp.int32), (at[2] < lax.axis_size("gz") - 1).astype(jnp.int32)]
    ).astype(jnp.int32)
    shape = orbitals.shape
    orbitals = orbitals.reshape(BLOCK, LANES)
    potential = potential.reshape(CELLS, LANES)
    block, edge, sent = (BLOCK, LANES), (EDGE, LANES), (BLOCK + EDGE, LANES)

    first, second = call(payload_kernel, ((PAYLOAD, LANES),) * 2)(flags, orbitals, potential)
    second, first = swap(second, "gz", 1), swap(first, "gz", 0)
    field, edge_potential = call(extend_kernel, (sent, (8, LANES)))(flags, orbitals, second, first)

    def advance(field, scale, previous, split):
        y2, y1, x2, x1 = [swap(field, axis, first) for axis in ("gy", "gx") for first in (1, 0)]
        kernel = functools.partial(step_kernel, scale, bool(previous), split)
        outs = (block, edge) if split else (sent,)
        return call(kernel, outs)(flags, potential, edge_potential, field, y1, x2, y2, x1, *previous)

    (field1,) = advance(field, 1.0 / HALF, (), False)
    (field2,) = advance(field1, 2.0 / HALF, (field,), False)
    field, edge = advance(field2, 2.0 / HALF, (field1,), True)
    after_y, after_x = from_above(field, "gy"), from_above(field, "gx")
    sums = call(sums_kernel, ((ORB, LANES),), smem=False)(potential, field, edge, after_y, after_x)[0]
    sums = sum_everywhere(sums)
    q_block, ritz = call(functools.partial(finish_kernel, cell_total), (block, (ORB, ORB)), smem=False)(sums, field)
    return q_block.reshape(shape), ritz


def solution(mesh):
    placed = (P(None, "gx", "gy", "gz"), P("gx", "gy", "gz"))
    return jax.shard_map(
        body,
        mesh=mesh,
        in_specs=placed,
        out_specs=(P(None, "gx", "gy", "gz"), P()),
        check_vma=False,
    )
```

```python
import functools

import jax
import jax.numpy as jnp
from jax import lax
from jax.experimental import pallas as pl
from jax.experimental.pallas import tpu as pltpu
from jax.sharding import PartitionSpec as P

WEIGHTS = (-205.0 / 72.0, 8.0 / 5.0, -1.0 / 5.0, 8.0 / 315.0, -1.0 / 560.0)
HALF = (12.0 - 1.5) / 2.0
MIDDLE = (12.0 + 1.5) / 2.0
ORB = 16
SIDE = 4
CELLS = SIDE * SIDE
LANES = 128
EXT = 16
BLOCK = CELLS * ORB
EDGE = SIDE * ORB
PAYLOAD = 2 * ORB + 8


def lane_index(rows):
    return lax.broadcasted_iota(jnp.int32, (rows, LANES), 1)


def rolled(value, amount):
    amount %= LANES
    return pltpu.roll(value, amount, 1) if amount else value


def rows_of(ref, cell):
    return ref[cell * ORB : (cell + 1) * ORB, :]


def face_masks(flags, rows):
    lane = lane_index(rows)
    even = flags[2] == 0
    upper = jnp.where(even, LANES - EXT, 0)
    lower = jnp.where(even, 0, LANES - EXT)
    first = (lane >= upper) & (lane < upper + EXT)
    second = (lane >= lower) & (lane < lower + EXT)
    return first, second


def payload_kernel(flags, orbitals, potential, first, second):
    mask1, mask2 = face_masks(flags, ORB)
    row1, row2 = face_masks(flags, 1)
    for high in range(2):
        sums = [jnp.zeros((ORB, LANES), jnp.float32)] * 2 + [jnp.zeros((1, LANES), jnp.float32)] * 2
        for low in range(8):
            cell = 8 * high + low
            value = orbitals[pl.ds(cell, ORB, stride=CELLS), :]
            local = potential[cell : cell + 1, :]
            parts = (
                jnp.where(mask1, value, 0.0),
                jnp.where(mask2, value, 0.0),
                jnp.where(row1, local, 0.0),
                jnp.where(row2, local, 0.0),
            )
            sums = [s + rolled(p, EXT * low) for s, p in zip(sums, parts)]
        for out, value, local in ((first, sums[0], sums[2]), (second, sums[1], sums[3])):
            out[high * ORB : (high + 1) * ORB, :] = value
            out[2 * ORB + high : 2 * ORB + high + 1, :] = local
    for out in (first, second):
        out[2 * ORB + 2 :, :] = jnp.zeros((PAYLOAD - 2 * ORB - 2, LANES), jnp.float32)


def extend_kernel(flags, orbitals, second, first, field, edge_potential):
    mask1, mask2 = face_masks(flags, ORB)
    row1, row2 = face_masks(flags, 1)
    for cell in range(CELLS):
        field[cell * ORB : (cell + 1) * ORB, :] = orbitals[pl.ds(cell, ORB, stride=CELLS), :]
    for x in range(SIDE):
        total, total_potential = 0.0, 0.0
        for y in range(SIDE):
            high, low = divmod(x * SIDE + y, 8)

            def unpack(start, size, keep1, keep2):
                one = rolled(first[start : start + size, :], -EXT * low)
                two = rolled(second[start : start + size, :], -EXT * low)
                return rolled(jnp.where(keep2, one, 0.0) + jnp.where(keep1, two, 0.0), 2 * EXT * y)

            total = total + unpack(high * ORB, ORB, mask1, mask2)
            total_potential = total_potential + unpack(2 * ORB + high, 1, row1, row2)
        field[BLOCK + x * ORB : BLOCK + (x + 1) * ORB, :] = total
        edge_potential[x : x + 1, :] = total_potential


def edge_of(ref, x):
    return ref[x * ORB : (x + 1) * ORB, :]


def step_kernel(scale, with_previous, split, flags, potential, edge_potential, field, y1, x2, y2, x1, *rest):
    previous = rest[0] if with_previous else None
    out = rest[-2] if split else rest[-1]
    lane = lane_index(ORB)
    place = lane % (2 * EXT)
    lane_y = ((lane + EXT) // (2 * EXT)) % SIDE
    inside = ((place < EXT) & (flags[4] != 0)) | ((place >= EXT) & (flags[3] != 0))
    window = (lane < EXT) | (lane >= LANES - EXT)
    even_x, even_y = flags[0] == 0, flags[1] == 0
    weight = [-0.5 * scale * w for w in WEIGHTS]
    shift = MIDDLE + 1.5 * WEIGHTS[0]

    def line(get, one, two, even):
        pairs = [(get(one, i), get(two, i)) for i in range(SIDE)]
        below = [jnp.where(even, b, a) for a, b in pairs]
        above = [jnp.where(even, a, b) for a, b in pairs]
        return below + [get(field, i) for i in range(SIDE)] + above

    for y in range(SIDE):
        along = line(lambda ref, x: rows_of(ref, x * SIDE + y), x1, x2, even_x)
        for x in range(SIDE):
            cell = x * SIDE + y
            here = along[SIDE + x]
            there = rolled(edge_of(field, CELLS + x), -2 * EXT * y)
            total = (potential[cell : cell + 1, :] - shift) * scale * here
            for k in range(1, 5):
                pairs = along[SIDE + x + k] + along[SIDE + x - k]
                pairs = pairs + rolled(jnp.where(lane < k, there, here), -k)
                pairs = pairs + rolled(jnp.where(lane >= LANES - k, there, here), k)
                total = total + weight[k] * pairs
            if with_previous:
                total = total - rows_of(previous, cell)
            out[cell * ORB : (cell + 1) * ORB, :] = total
    for x in range(SIDE):
        along = line(lambda ref, y: rows_of(ref, x * SIDE + y), y1, y2, even_y)
        for y in range(SIDE):
            cell = x * SIDE + y
            total = rows_of(out, cell)
            for k in range(1, 5):
                total = total + weight[k] * (along[SIDE + y + k] + along[SIDE + y - k])
            out[cell * ORB : (cell + 1) * ORB, :] = total
    along = line(lambda ref, x: edge_of(ref, CELLS + x), x1, x2, even_x)
    for x in range(SIDE):
        here = along[SIDE + x]
        one, two = edge_of(y1, CELLS + x), edge_of(y2, CELLS + x)
        below, above = jnp.where(even_y, two, one), jnp.where(even_y, one, two)
        there = 0.0
        for y in range(SIDE):
            there = there + rolled(jnp.where(window, rows_of(field, x * SIDE + y), 0.0), 2 * EXT * y)
        total = (edge_potential[x : x + 1, :] - shift) * scale * here
        for k in range(1, 5):
            pairs = along[SIDE + x + k] + along[SIDE + x - k]
            pairs = pairs + rolled(jnp.where(lane_y < k, above, here), -2 * EXT * k)
            pairs = pairs + rolled(jnp.where(lane_y >= SIDE - k, below, here), 2 * EXT * k)
            pairs = pairs + rolled(jnp.where(place < k, there, here), -k)
            pairs = pairs + rolled(jnp.where(place >= 2 * EXT - k, there, here), k)
            total = total + weight[k] * pairs
        if with_previous:
            total = total - edge_of(previous, CELLS + x)
        total = jnp.where(inside, total, 0.0)
        if split:
            rest[-1][x * ORB : (x + 1) * ORB, :] = total
        else:
            out[BLOCK + x * ORB : BLOCK + (x + 1) * ORB, :] = total


def dot(a, b, contract):
    return lax.dot_general(
        a, b, ((contract[:1], contract[1:]), ((), ())), precision=lax.Precision.HIGHEST, preferred_element_type=jnp.float32
    )


def sums_kernel(potential, field, edge, after_y, after_x, sums):
    lane = lane_index(ORB)
    here_all, image_all = [], []
    for x in range(SIDE):
        for y in range(SIDE):
            cell = x * SIDE + y
            here, there = rows_of(field, cell), rolled(edge_of(edge, x), -2 * EXT * y)
            image = (0.5 * potential[cell : cell + 1, :] - 0.75 * WEIGHTS[0]) * here
            for k in range(1, 5):
                up = rows_of(field, cell + k * SIDE) if x + k < SIDE else rows_of(after_x, cell + (k - SIDE) * SIDE)
                up = up + (rows_of(field, cell + k) if y + k < SIDE else rows_of(after_y, cell + k - SIDE))
                up = up + rolled(jnp.where(lane < k, there, here), -k)
                image = image + (-0.5 * WEIGHTS[k]) * up
            here_all.append(here)
            image_all.append(image)
    here = jnp.concatenate(here_all, axis=1)
    image = jnp.concatenate(image_all, axis=1)
    sums[...] = jnp.zeros_like(sums)
    sums[:, : 2 * ORB] = dot(here, jnp.concatenate([here, image], axis=0), (1, 1))


def finish_kernel(cell_total, sums, field, q_block, ritz):
    sums = sums[...] * (1.0 / cell_total)
    row = lax.broadcasted_iota(jnp.int32, (ORB, LANES), 0)
    lane = lane_index(ORB)
    work = jnp.where(lane < ORB, sums, jnp.where(lane == row + ORB, 1.0, 0.0))
    for k in range(ORB - 1):
        pivot = work[k : k + 1, :]
        factor = work[:, k : k + 1] / pivot[:, k : k + 1]
        work = work - jnp.where(row > k, factor, 0.0) * pivot
    diagonal = jnp.sum(jnp.where(lane == row, work, 0.0), axis=1, keepdims=True)
    inverse = (work * (1.0 / jnp.sqrt(diagonal)))[:, ORB : 2 * ORB]
    half = sums[:, ORB : 2 * ORB]
    part = dot(dot(inverse, half, (1, 0)), inverse, (1, 1))
    ritz[...] = part + part.T
    for cell in range(CELLS):
        q_block[pl.ds(cell, ORB, stride=CELLS), :] = dot(inverse, rows_of(field, cell), (1, 0))


def swap(value, axis, first):
    pairs = []
    for i in range(first, lax.axis_size(axis) - 1, 2):
        pairs += [(i, i + 1), (i + 1, i)]
    return lax.ppermute(value, axis, pairs)


def from_above(value, axis):
    return lax.ppermute(value, axis, [(i + 1, i) for i in range(lax.axis_size(axis) - 1)])


def exchange(value, axes, mask):
    size = 1
    for axis in axes:
        size *= lax.axis_size(axis)
    return value + lax.ppermute(value, axes, [(i, i ^ mask) for i in range(size)])


def sum_everywhere(value):
    if all(lax.axis_size(axis) == 8 for axis in ("gx", "gy", "gz")):
        value = lax.psum(lax.psum(value, "gy"), "gx")
        stages = (
            (("gz",), 1), (("gz",), 3),
            (("gx", "gz"), 36),
        )
    else:
        stages = [((axis,), 1 << bit) for axis in ("gy", "gx", "gz") for bit in range(lax.axis_size(axis).bit_length() - 1)]
    for axes, mask in stages:
        value = exchange(value, axes, mask)
    return value


def call(kernel, outs, smem=True):
    def run(*operands):
        specs = [pl.BlockSpec(memory_space=pltpu.VMEM)] * len(operands)
        if smem:
            specs[0] = pl.BlockSpec(memory_space=pltpu.SMEM)
        return pl.pallas_call(
            kernel,
            out_shape=[jax.ShapeDtypeStruct(shape, jnp.float32) for shape in outs],
            in_specs=specs,
            out_specs=[pl.BlockSpec(memory_space=pltpu.VMEM)] * len(outs),
            compiler_params=pltpu.CompilerParams(vmem_limit_bytes=8 * 1024 * 1024),
        )(*operands)

    return run


def body(orbitals, potential):
    at = [lax.axis_index(axis) for axis in ("gx", "gy", "gz")]
    cell_total = orbitals[0].size * lax.axis_size("gx") * lax.axis_size("gy") * lax.axis_size("gz")
    flags = jnp.stack(
        [at[0] % 2, at[1] % 2, at[2] % 2, (at[2] > 0).astype(jnp.int32), (at[2] < lax.axis_size("gz") - 1).astype(jnp.int32)]
    ).astype(jnp.int32)
    shape = orbitals.shape
    orbitals = orbitals.reshape(BLOCK, LANES)
    potential = potential.reshape(CELLS, LANES)
    block, edge, sent = (BLOCK, LANES), (EDGE, LANES), (BLOCK + EDGE, LANES)

    first, second = call(payload_kernel, ((PAYLOAD, LANES),) * 2)(flags, orbitals, potential)
    second, first = swap(second, "gz", 1), swap(first, "gz", 0)
    field, edge_potential = call(extend_kernel, (sent, (8, LANES)))(flags, orbitals, second, first)

    def advance(field, scale, previous, split):
        y2, y1, x2, x1 = [swap(field, axis, first) for axis in ("gy", "gx") for first in (1, 0)]
        kernel = functools.partial(step_kernel, scale, bool(previous), split)
        outs = (block, edge) if split else (sent,)
        return call(kernel, outs)(flags, potential, edge_potential, field, y1, x2, y2, x1, *previous)

    (field1,) = advance(field, 1.0 / HALF, (), False)
    (field2,) = advance(field1, 2.0 / HALF, (field,), False)
    field, edge = advance(field2, 2.0 / HALF, (field1,), True)
    after_y, after_x = from_above(field, "gy"), from_above(field, "gx")
    sums = call(sums_kernel, ((ORB, LANES),), smem=False)(potential, field, edge, after_y, after_x)[0]
    sums = sum_everywhere(sums)
    q_block, ritz = call(functools.partial(finish_kernel, cell_total), (block, (ORB, ORB)), smem=False)(sums, field)
    return q_block.reshape(shape), ritz


def solution(mesh):
    placed = (P(None, "gx", "gy", "gz"), P("gx", "gy", "gz"))
    return jax.shard_map(
        body,
        mesh=mesh,
        in_specs=placed,
        out_specs=(P(None, "gx", "gy", "gz"), P()),
        check_vma=False,
    )
```

```python
import functools

import jax
import jax.numpy as jnp
from jax import lax
from jax.experimental import pallas as pl
from jax.experimental.pallas import tpu as pltpu
from jax.sharding import PartitionSpec as P

WEIGHTS = (-205.0 / 72.0, 8.0 / 5.0, -1.0 / 5.0, 8.0 / 315.0, -1.0 / 560.0)
HALF = (12.0 - 1.5) / 2.0
MIDDLE = (12.0 + 1.5) / 2.0
ORB = 16
SIDE = 4
CELLS = SIDE * SIDE
LANES = 128
EXT = 16
BLOCK = CELLS * ORB
EDGE = SIDE * ORB
PAYLOAD = 2 * ORB + 8


def lane_index(rows):
    return lax.broadcasted_iota(jnp.int32, (rows, LANES), 1)


def rolled(value, amount):
    amount %= LANES
    return pltpu.roll(value, amount, 1) if amount else value


def rows_of(ref, cell):
    return ref[cell * ORB : (cell + 1) * ORB, :]


def face_masks(flags, rows):
    lane = lane_index(rows)
    even = flags[2] == 0
    upper = jnp.where(even, LANES - EXT, 0)
    lower = jnp.where(even, 0, LANES - EXT)
    first = (lane >= upper) & (lane < upper + EXT)
    second = (lane >= lower) & (lane < lower + EXT)
    return first, second


def payload_kernel(flags, orbitals, potential, first, second):
    mask1, mask2 = face_masks(flags, ORB)
    row1, row2 = face_masks(flags, 1)
    for high in range(2):
        sums = [jnp.zeros((ORB, LANES), jnp.float32)] * 2 + [jnp.zeros((1, LANES), jnp.float32)] * 2
        for low in range(8):
            cell = 8 * high + low
            value = orbitals[pl.ds(cell, ORB, stride=CELLS), :]
            local = potential[cell : cell + 1, :]
            parts = (
                jnp.where(mask1, value, 0.0),
                jnp.where(mask2, value, 0.0),
                jnp.where(row1, local, 0.0),
                jnp.where(row2, local, 0.0),
            )
            sums = [s + rolled(p, EXT * low) for s, p in zip(sums, parts)]
        for out, value, local in ((first, sums[0], sums[2]), (second, sums[1], sums[3])):
            out[high * ORB : (high + 1) * ORB, :] = value
            out[2 * ORB + high : 2 * ORB + high + 1, :] = local
    for out in (first, second):
        out[2 * ORB + 2 :, :] = jnp.zeros((PAYLOAD - 2 * ORB - 2, LANES), jnp.float32)


def extend_kernel(flags, orbitals, second, first, field, edge_potential):
    mask1, mask2 = face_masks(flags, ORB)
    row1, row2 = face_masks(flags, 1)
    for cell in range(CELLS):
        field[cell * ORB : (cell + 1) * ORB, :] = orbitals[pl.ds(cell, ORB, stride=CELLS), :]
    for x in range(SIDE):
        total, total_potential = 0.0, 0.0
        for y in range(SIDE):
            high, low = divmod(x * SIDE + y, 8)

            def unpack(start, size, keep1, keep2):
                one = rolled(first[start : start + size, :], -EXT * low)
                two = rolled(second[start : start + size, :], -EXT * low)
                return rolled(jnp.where(keep2, one, 0.0) + jnp.where(keep1, two, 0.0), 2 * EXT * y)

            total = total + unpack(high * ORB, ORB, mask1, mask2)
            total_potential = total_potential + unpack(2 * ORB + high, 1, row1, row2)
        field[BLOCK + x * ORB : BLOCK + (x + 1) * ORB, :] = total
        edge_potential[x : x + 1, :] = total_potential


def edge_of(ref, x):
    return ref[x * ORB : (x + 1) * ORB, :]


def step_kernel(scale, with_previous, split, flags, potential, edge_potential, field, y1, x2, y2, x1, *rest):
    previous = rest[0] if with_previous else None
    out = rest[-2] if split else rest[-1]
    lane = lane_index(ORB)
    place = lane % (2 * EXT)
    lane_y = ((lane + EXT) // (2 * EXT)) % SIDE
    inside = ((place < EXT) & (flags[4] != 0)) | ((place >= EXT) & (flags[3] != 0))
    window = (lane < EXT) | (lane >= LANES - EXT)
    even_x, even_y = flags[0] == 0, flags[1] == 0
    weight = [-0.5 * scale * w for w in WEIGHTS]
    shift = MIDDLE + 1.5 * WEIGHTS[0]

    def line(get, one, two, even):
        pairs = [(get(one, i), get(two, i)) for i in range(SIDE)]
        below = [jnp.where(even, b, a) for a, b in pairs]
        above = [jnp.where(even, a, b) for a, b in pairs]
        return below + [get(field, i) for i in range(SIDE)] + above

    for y in range(SIDE):
        along = line(lambda ref, x: rows_of(ref, x * SIDE + y), x1, x2, even_x)
        for x in range(SIDE):
            cell = x * SIDE + y
            here = along[SIDE + x]
            there = rolled(edge_of(field, CELLS + x), -2 * EXT * y)
            total = (potential[cell : cell + 1, :] - shift) * scale * here
            for k in range(1, 5):
                pairs = along[SIDE + x + k] + along[SIDE + x - k]
                pairs = pairs + rolled(jnp.where(lane < k, there, here), -k)
                pairs = pairs + rolled(jnp.where(lane >= LANES - k, there, here), k)
                total = total + weight[k] * pairs
            if with_previous:
                total = total - rows_of(previous, cell)
            out[cell * ORB : (cell + 1) * ORB, :] = total
    for x in range(SIDE):
        along = line(lambda ref, y: rows_of(ref, x * SIDE + y), y1, y2, even_y)
        for y in range(SIDE):
            cell = x * SIDE + y
            total = rows_of(out, cell)
            for k in range(1, 5):
                total = total + weight[k] * (along[SIDE + y + k] + along[SIDE + y - k])
            out[cell * ORB : (cell + 1) * ORB, :] = total
    along = line(lambda ref, x: edge_of(ref, CELLS + x), x1, x2, even_x)
    for x in range(SIDE):
        here = along[SIDE + x]
        one, two = edge_of(y1, CELLS + x), edge_of(y2, CELLS + x)
        below, above = jnp.where(even_y, two, one), jnp.where(even_y, one, two)
        there = 0.0
        for y in range(SIDE):
            there = there + rolled(jnp.where(window, rows_of(field, x * SIDE + y), 0.0), 2 * EXT * y)
        total = (edge_potential[x : x + 1, :] - shift) * scale * here
        for k in range(1, 5):
            pairs = along[SIDE + x + k] + along[SIDE + x - k]
            pairs = pairs + rolled(jnp.where(lane_y < k, above, here), -2 * EXT * k)
            pairs = pairs + rolled(jnp.where(lane_y >= SIDE - k, below, here), 2 * EXT * k)
            pairs = pairs + rolled(jnp.where(place < k, there, here), -k)
            pairs = pairs + rolled(jnp.where(place >= 2 * EXT - k, there, here), k)
            total = total + weight[k] * pairs
        if with_previous:
            total = total - edge_of(previous, CELLS + x)
        total = jnp.where(inside, total, 0.0)
        if split:
            rest[-1][x * ORB : (x + 1) * ORB, :] = total
        else:
            out[BLOCK + x * ORB : BLOCK + (x + 1) * ORB, :] = total


def dot(a, b, contract):
    return lax.dot_general(
        a, b, ((contract[:1], contract[1:]), ((), ())), precision=lax.Precision.HIGHEST, preferred_element_type=jnp.float32
    )


def sums_kernel(potential, field, edge, after_y, after_x, sums):
    lane = lane_index(ORB)
    here_all, image_all = [], []
    for x in range(SIDE):
        for y in range(SIDE):
            cell = x * SIDE + y
            here, there = rows_of(field, cell), rolled(edge_of(edge, x), -2 * EXT * y)
            image = (0.5 * potential[cell : cell + 1, :] - 0.75 * WEIGHTS[0]) * here
            for k in range(1, 5):
                up = rows_of(field, cell + k * SIDE) if x + k < SIDE else rows_of(after_x, cell + (k - SIDE) * SIDE)
                up = up + (rows_of(field, cell + k) if y + k < SIDE else rows_of(after_y, cell + k - SIDE))
                up = up + rolled(jnp.where(lane < k, there, here), -k)
                image = image + (-0.5 * WEIGHTS[k]) * up
            here_all.append(here)
            image_all.append(image)
    here = jnp.concatenate(here_all, axis=1)
    image = jnp.concatenate(image_all, axis=1)
    sums[...] = jnp.zeros_like(sums)
    sums[:, : 2 * ORB] = dot(here, jnp.concatenate([here, image], axis=0), (1, 1))


def finish_kernel(cell_total, sums, field, q_block, ritz):
    sums = sums[...] * (1.0 / cell_total)
    row = lax.broadcasted_iota(jnp.int32, (ORB, LANES), 0)
    lane = lane_index(ORB)
    work = jnp.where(lane < ORB, sums, jnp.where(lane == row + ORB, 1.0, 0.0))
    for k in range(ORB - 1):
        pivot = work[k : k + 1, :]
        factor = work[:, k : k + 1] / pivot[:, k : k + 1]
        work = work - jnp.where(row > k, factor, 0.0) * pivot
    diagonal = jnp.sum(jnp.where(lane == row, work, 0.0), axis=1, keepdims=True)
    inverse = (work * (1.0 / jnp.sqrt(diagonal)))[:, ORB : 2 * ORB]
    half = sums[:, ORB : 2 * ORB]
    part = dot(dot(inverse, half, (1, 0)), inverse, (1, 1))
    ritz[...] = part + part.T
    for cell in range(CELLS):
        q_block[pl.ds(cell, ORB, stride=CELLS), :] = dot(inverse, rows_of(field, cell), (1, 0))


def swap(value, axis, first):
    pairs = []
    for i in range(first, lax.axis_size(axis) - 1, 2):
        pairs += [(i, i + 1), (i + 1, i)]
    return lax.ppermute(value, axis, pairs)


def from_above(value, axis):
    return lax.ppermute(value, axis, [(i + 1, i) for i in range(lax.axis_size(axis) - 1)])


def exchange(value, axes, mask):
    size = 1
    for axis in axes:
        size *= lax.axis_size(axis)
    return value + lax.ppermute(value, axes, [(i, i ^ mask) for i in range(size)])


def sum_everywhere(value):
    if all(lax.axis_size(axis) == 8 for axis in ("gx", "gy", "gz")):
        value = lax.psum(value, "gy")
        value = lax.psum(value, "gz", axis_index_groups=[[0, 1, 2, 3], [4, 5, 6, 7]])
        stages = (
            (("gx",), 1), (("gx",), 2), (("gx",), 4), (("gx", "gz"), 36),
        )
    else:
        stages = [((axis,), 1 << bit) for axis in ("gy", "gx", "gz") for bit in range(lax.axis_size(axis).bit_length() - 1)]
    for axes, mask in stages:
        value = exchange(value, axes, mask)
    return value


def call(kernel, outs, smem=True):
    def run(*operands):
        specs = [pl.BlockSpec(memory_space=pltpu.VMEM)] * len(operands)
        if smem:
            specs[0] = pl.BlockSpec(memory_space=pltpu.SMEM)
        return pl.pallas_call(
            kernel,
            out_shape=[jax.ShapeDtypeStruct(shape, jnp.float32) for shape in outs],
            in_specs=specs,
            out_specs=[pl.BlockSpec(memory_space=pltpu.VMEM)] * len(outs),
            compiler_params=pltpu.CompilerParams(vmem_limit_bytes=8 * 1024 * 1024),
        )(*operands)

    return run


def body(orbitals, potential):
    at = [lax.axis_index(axis) for axis in ("gx", "gy", "gz")]
    cell_total = orbitals[0].size * lax.axis_size("gx") * lax.axis_size("gy") * lax.axis_size("gz")
    flags = jnp.stack(
        [at[0] % 2, at[1] % 2, at[2] % 2, (at[2] > 0).astype(jnp.int32), (at[2] < lax.axis_size("gz") - 1).astype(jnp.int32)]
    ).astype(jnp.int32)
    shape = orbitals.shape
    orbitals = orbitals.reshape(BLOCK, LANES)
    potential = potential.reshape(CELLS, LANES)
    block, edge, sent = (BLOCK, LANES), (EDGE, LANES), (BLOCK + EDGE, LANES)

    first, second = call(payload_kernel, ((PAYLOAD, LANES),) * 2)(flags, orbitals, potential)
    second, first = swap(second, "gz", 1), swap(first, "gz", 0)
    field, edge_potential = call(extend_kernel, (sent, (8, LANES)))(flags, orbitals, second, first)

    def advance(field, scale, previous, split):
        y2, y1, x2, x1 = [swap(field, axis, first) for axis in ("gy", "gx") for first in (1, 0)]
        kernel = functools.partial(step_kernel, scale, bool(previous), split)
        outs = (block, edge) if split else (sent,)
        return call(kernel, outs)(flags, potential, edge_potential, field, y1, x2, y2, x1, *previous)

    (field1,) = advance(field, 1.0 / HALF, (), False)
    (field2,) = advance(field1, 2.0 / HALF, (field,), False)
    field, edge = advance(field2, 2.0 / HALF, (field1,), True)
    after_y, after_x = from_above(field, "gy"), from_above(field, "gx")
    sums = call(sums_kernel, ((ORB, LANES),), smem=False)(potential, field, edge, after_y, after_x)[0]
    sums = sum_everywhere(sums)
    q_block, ritz = call(functools.partial(finish_kernel, cell_total), (block, (ORB, ORB)), smem=False)(sums, field)
    return q_block.reshape(shape), ritz


def solution(mesh):
    placed = (P(None, "gx", "gy", "gz"), P("gx", "gy", "gz"))
    return jax.shard_map(
        body,
        mesh=mesh,
        in_specs=placed,
        out_specs=(P(None, "gx", "gy", "gz"), P()),
        check_vma=False,
    )
```

```python
import functools

import jax
import jax.numpy as jnp
from jax import lax
from jax.experimental import pallas as pl
from jax.experimental.pallas import tpu as pltpu
from jax.sharding import PartitionSpec as P

WEIGHTS = (-205.0 / 72.0, 8.0 / 5.0, -1.0 / 5.0, 8.0 / 315.0, -1.0 / 560.0)
HALF = (12.0 - 1.5) / 2.0
MIDDLE = (12.0 + 1.5) / 2.0
ORB = 16
SIDE = 4
CELLS = SIDE * SIDE
LANES = 128
EXT = 16
BLOCK = CELLS * ORB
EDGE = SIDE * ORB
PAYLOAD = 2 * ORB + 8


def lane_index(rows):
    return lax.broadcasted_iota(jnp.int32, (rows, LANES), 1)


def rolled(value, amount):
    amount %= LANES
    return pltpu.roll(value, amount, 1) if amount else value


def rows_of(ref, cell):
    return ref[cell * ORB : (cell + 1) * ORB, :]


def face_masks(flags, rows):
    lane = lane_index(rows)
    even = flags[2] == 0
    upper = jnp.where(even, LANES - EXT, 0)
    lower = jnp.where(even, 0, LANES - EXT)
    first = (lane >= upper) & (lane < upper + EXT)
    second = (lane >= lower) & (lane < lower + EXT)
    return first, second


def payload_kernel(flags, orbitals, potential, first, second):
    mask1, mask2 = face_masks(flags, ORB)
    row1, row2 = face_masks(flags, 1)
    for high in range(2):
        sums = [jnp.zeros((ORB, LANES), jnp.float32)] * 2 + [jnp.zeros((1, LANES), jnp.float32)] * 2
        for low in range(8):
            cell = 8 * high + low
            value = orbitals[pl.ds(cell, ORB, stride=CELLS), :]
            local = potential[cell : cell + 1, :]
            parts = (
                jnp.where(mask1, value, 0.0),
                jnp.where(mask2, value, 0.0),
                jnp.where(row1, local, 0.0),
                jnp.where(row2, local, 0.0),
            )
            sums = [s + rolled(p, EXT * low) for s, p in zip(sums, parts)]
        for out, value, local in ((first, sums[0], sums[2]), (second, sums[1], sums[3])):
            out[high * ORB : (high + 1) * ORB, :] = value
            out[2 * ORB + high : 2 * ORB + high + 1, :] = local
    for out in (first, second):
        out[2 * ORB + 2 :, :] = jnp.zeros((PAYLOAD - 2 * ORB - 2, LANES), jnp.float32)


def extend_kernel(flags, orbitals, second, first, field, edge_potential):
    mask1, mask2 = face_masks(flags, ORB)
    row1, row2 = face_masks(flags, 1)
    for cell in range(CELLS):
        field[cell * ORB : (cell + 1) * ORB, :] = orbitals[pl.ds(cell, ORB, stride=CELLS), :]
    for x in range(SIDE):
        total, total_potential = 0.0, 0.0
        for y in range(SIDE):
            high, low = divmod(x * SIDE + y, 8)

            def unpack(start, size, keep1, keep2):
                one = rolled(first[start : start + size, :], -EXT * low)
                two = rolled(second[start : start + size, :], -EXT * low)
                return rolled(jnp.where(keep2, one, 0.0) + jnp.where(keep1, two, 0.0), 2 * EXT * y)

            total = total + unpack(high * ORB, ORB, mask1, mask2)
            total_potential = total_potential + unpack(2 * ORB + high, 1, row1, row2)
        field[BLOCK + x * ORB : BLOCK + (x + 1) * ORB, :] = total
        edge_potential[x : x + 1, :] = total_potential


def edge_of(ref, x):
    return ref[x * ORB : (x + 1) * ORB, :]


def step_kernel(scale, with_previous, split, flags, potential, edge_potential, field, y1, x2, y2, x1, *rest):
    previous = rest[0] if with_previous else None
    out = rest[-2] if split else rest[-1]
    lane = lane_index(ORB)
    place = lane % (2 * EXT)
    lane_y = ((lane + EXT) // (2 * EXT)) % SIDE
    inside = ((place < EXT) & (flags[4] != 0)) | ((place >= EXT) & (flags[3] != 0))
    window = (lane < EXT) | (lane >= LANES - EXT)
    even_x, even_y = flags[0] == 0, flags[1] == 0
    weight = [-0.5 * scale * w for w in WEIGHTS]
    shift = MIDDLE + 1.5 * WEIGHTS[0]

    def line(get, one, two, even):
        pairs = [(get(one, i), get(two, i)) for i in range(SIDE)]
        below = [jnp.where(even, b, a) for a, b in pairs]
        above = [jnp.where(even, a, b) for a, b in pairs]
        return below + [get(field, i) for i in range(SIDE)] + above

    for y in range(SIDE):
        along = line(lambda ref, x: rows_of(ref, x * SIDE + y), x1, x2, even_x)
        for x in range(SIDE):
            cell = x * SIDE + y
            here = along[SIDE + x]
            there = rolled(edge_of(field, CELLS + x), -2 * EXT * y)
            total = (potential[cell : cell + 1, :] - shift) * scale * here
            for k in range(1, 5):
                pairs = along[SIDE + x + k] + along[SIDE + x - k]
                pairs = pairs + rolled(jnp.where(lane < k, there, here), -k)
                pairs = pairs + rolled(jnp.where(lane >= LANES - k, there, here), k)
                total = total + weight[k] * pairs
            if with_previous:
                total = total - rows_of(previous, cell)
            out[cell * ORB : (cell + 1) * ORB, :] = total
    for x in range(SIDE):
        along = line(lambda ref, y: rows_of(ref, x * SIDE + y), y1, y2, even_y)
        for y in range(SIDE):
            cell = x * SIDE + y
            total = rows_of(out, cell)
            for k in range(1, 5):
                total = total + weight[k] * (along[SIDE + y + k] + along[SIDE + y - k])
            out[cell * ORB : (cell + 1) * ORB, :] = total
    along = line(lambda ref, x: edge_of(ref, CELLS + x), x1, x2, even_x)
    for x in range(SIDE):
        here = along[SIDE + x]
        one, two = edge_of(y1, CELLS + x), edge_of(y2, CELLS + x)
        below, above = jnp.where(even_y, two, one), jnp.where(even_y, one, two)
        there = 0.0
        for y in range(SIDE):
            there = there + rolled(jnp.where(window, rows_of(field, x * SIDE + y), 0.0), 2 * EXT * y)
        total = (edge_potential[x : x + 1, :] - shift) * scale * here
        for k in range(1, 5):
            pairs = along[SIDE + x + k] + along[SIDE + x - k]
            pairs = pairs + rolled(jnp.where(lane_y < k, above, here), -2 * EXT * k)
            pairs = pairs + rolled(jnp.where(lane_y >= SIDE - k, below, here), 2 * EXT * k)
            pairs = pairs + rolled(jnp.where(place < k, there, here), -k)
            pairs = pairs + rolled(jnp.where(place >= 2 * EXT - k, there, here), k)
            total = total + weight[k] * pairs
        if with_previous:
            total = total - edge_of(previous, CELLS + x)
        total = jnp.where(inside, total, 0.0)
        if split:
            rest[-1][x * ORB : (x + 1) * ORB, :] = total
        else:
            out[BLOCK + x * ORB : BLOCK + (x + 1) * ORB, :] = total


def dot(a, b, contract):
    return lax.dot_general(
        a, b, ((contract[:1], contract[1:]), ((), ())), precision=lax.Precision.HIGHEST, preferred_element_type=jnp.float32
    )


def sums_kernel(potential, field, edge, after_y, after_x, sums):
    lane = lane_index(ORB)
    here_all, image_all = [], []
    for x in range(SIDE):
        for y in range(SIDE):
            cell = x * SIDE + y
            here, there = rows_of(field, cell), rolled(edge_of(edge, x), -2 * EXT * y)
            image = (0.5 * potential[cell : cell + 1, :] - 0.75 * WEIGHTS[0]) * here
            for k in range(1, 5):
                up = rows_of(field, cell + k * SIDE) if x + k < SIDE else rows_of(after_x, cell + (k - SIDE) * SIDE)
                up = up + (rows_of(field, cell + k) if y + k < SIDE else rows_of(after_y, cell + k - SIDE))
                up = up + rolled(jnp.where(lane < k, there, here), -k)
                image = image + (-0.5 * WEIGHTS[k]) * up
            here_all.append(here)
            image_all.append(image)
    here = jnp.concatenate(here_all, axis=1)
    image = jnp.concatenate(image_all, axis=1)
    sums[...] = jnp.zeros_like(sums)
    sums[:, : 2 * ORB] = dot(here, jnp.concatenate([here, image], axis=0), (1, 1))


def finish_kernel(cell_total, sums, field, q_block, ritz):
    sums = sums[...] * (1.0 / cell_total)
    row = lax.broadcasted_iota(jnp.int32, (ORB, LANES), 0)
    lane = lane_index(ORB)
    work = jnp.where(lane < ORB, sums, jnp.where(lane == row + ORB, 1.0, 0.0))
    for k in range(ORB - 1):
        pivot = work[k : k + 1, :]
        factor = work[:, k : k + 1] / pivot[:, k : k + 1]
        work = work - jnp.where(row > k, factor, 0.0) * pivot
    diagonal = jnp.sum(jnp.where(lane == row, work, 0.0), axis=1, keepdims=True)
    inverse = (work * (1.0 / jnp.sqrt(diagonal)))[:, ORB : 2 * ORB]
    half = sums[:, ORB : 2 * ORB]
    part = dot(dot(inverse, half, (1, 0)), inverse, (1, 1))
    ritz[...] = part + part.T
    for cell in range(CELLS):
        q_block[pl.ds(cell, ORB, stride=CELLS), :] = dot(inverse, rows_of(field, cell), (1, 0))


def swap(value, axis, first):
    pairs = []
    for i in range(first, lax.axis_size(axis) - 1, 2):
        pairs += [(i, i + 1), (i + 1, i)]
    return lax.ppermute(value, axis, pairs)


def from_above(value, axis):
    return lax.ppermute(value, axis, [(i + 1, i) for i in range(lax.axis_size(axis) - 1)])


def sum_everywhere(value):
    if all(lax.axis_size(axis) == 8 for axis in ("gx", "gy", "gz")):
        fours = [[0, 1, 2, 3], [4, 5, 6, 7]]
        value = lax.psum(value, "gy")
        value = lax.psum(value, "gz", axis_index_groups=fours)
        value = lax.psum(value, "gx", axis_index_groups=fours)
        rings = [[8 * gx + gz, 8 * gx + 32 + gz, 8 * gx + gz + 4, 8 * gx + 32 + gz + 4] for gx in range(4) for gz in range(4)]
        return lax.psum(value, ("gx", "gz"), axis_index_groups=rings)
    return lax.psum(value, ("gx", "gy", "gz"))


def call(kernel, outs, smem=True):
    def run(*operands):
        specs = [pl.BlockSpec(memory_space=pltpu.VMEM)] * len(operands)
        if smem:
            specs[0] = pl.BlockSpec(memory_space=pltpu.SMEM)
        return pl.pallas_call(
            kernel,
            out_shape=[jax.ShapeDtypeStruct(shape, jnp.float32) for shape in outs],
            in_specs=specs,
            out_specs=[pl.BlockSpec(memory_space=pltpu.VMEM)] * len(outs),
            compiler_params=pltpu.CompilerParams(vmem_limit_bytes=8 * 1024 * 1024),
        )(*operands)

    return run


def body(orbitals, potential):
    at = [lax.axis_index(axis) for axis in ("gx", "gy", "gz")]
    cell_total = orbitals[0].size * lax.axis_size("gx") * lax.axis_size("gy") * lax.axis_size("gz")
    flags = jnp.stack(
        [at[0] % 2, at[1] % 2, at[2] % 2, (at[2] > 0).astype(jnp.int32), (at[2] < lax.axis_size("gz") - 1).astype(jnp.int32)]
    ).astype(jnp.int32)
    shape = orbitals.shape
    orbitals = orbitals.reshape(BLOCK, LANES)
    potential = potential.reshape(CELLS, LANES)
    block, edge, sent = (BLOCK, LANES), (EDGE, LANES), (BLOCK + EDGE, LANES)

    first, second = call(payload_kernel, ((PAYLOAD, LANES),) * 2)(flags, orbitals, potential)
    second, first = swap(second, "gz", 1), swap(first, "gz", 0)
    field, edge_potential = call(extend_kernel, (sent, (8, LANES)))(flags, orbitals, second, first)

    def advance(field, scale, previous, split):
        y2, y1, x2, x1 = [swap(field, axis, first) for axis in ("gy", "gx") for first in (1, 0)]
        kernel = functools.partial(step_kernel, scale, bool(previous), split)
        outs = (block, edge) if split else (sent,)
        return call(kernel, outs)(flags, potential, edge_potential, field, y1, x2, y2, x1, *previous)

    (field1,) = advance(field, 1.0 / HALF, (), False)
    (field2,) = advance(field1, 2.0 / HALF, (field,), False)
    field, edge = advance(field2, 2.0 / HALF, (field1,), True)
    after_y, after_x = from_above(field, "gy"), from_above(field, "gx")
    sums = call(sums_kernel, ((ORB, LANES),), smem=False)(potential, field, edge, after_y, after_x)[0]
    sums = sum_everywhere(sums)
    q_block, ritz = call(functools.partial(finish_kernel, cell_total), (block, (ORB, ORB)), smem=False)(sums, field)
    return q_block.reshape(shape), ritz


def solution(mesh):
    placed = (P(None, "gx", "gy", "gz"), P("gx", "gy", "gz"))
    return jax.shard_map(
        body,
        mesh=mesh,
        in_specs=placed,
        out_specs=(P(None, "gx", "gy", "gz"), P()),
        check_vma=False,
    )
```

```python
import functools

import jax
import jax.numpy as jnp
from jax import lax
from jax.experimental import pallas as pl
from jax.experimental.pallas import tpu as pltpu
from jax.sharding import PartitionSpec as P

WEIGHTS = (-205.0 / 72.0, 8.0 / 5.0, -1.0 / 5.0, 8.0 / 315.0, -1.0 / 560.0)
HALF = (12.0 - 1.5) / 2.0
MIDDLE = (12.0 + 1.5) / 2.0
ORB = 16
SIDE = 4
CELLS = SIDE * SIDE
LANES = 128
EXT = 16
BLOCK = CELLS * ORB
EDGE = SIDE * ORB
PAYLOAD = 2 * ORB + 8


def lane_index(rows):
    return lax.broadcasted_iota(jnp.int32, (rows, LANES), 1)


def rolled(value, amount):
    amount %= LANES
    return pltpu.roll(value, amount, 1) if amount else value


def rows_of(ref, cell):
    return ref[cell * ORB : (cell + 1) * ORB, :]


def face_masks(flags, rows):
    lane = lane_index(rows)
    even = flags[2] == 0
    upper = jnp.where(even, LANES - EXT, 0)
    lower = jnp.where(even, 0, LANES - EXT)
    first = (lane >= upper) & (lane < upper + EXT)
    second = (lane >= lower) & (lane < lower + EXT)
    return first, second


def payload_kernel(flags, orbitals, potential, first, second):
    mask1, mask2 = face_masks(flags, ORB)
    row1, row2 = face_masks(flags, 1)
    even = flags[2] == 0
    for high in range(2):
        sums = [jnp.zeros((ORB, LANES), jnp.float32)] * 2 + [jnp.zeros((1, LANES), jnp.float32)] * 2
        for low in range(8):
            cell = 8 * high + low
            value = orbitals[pl.ds(cell, ORB, stride=CELLS), :]
            local = potential[cell : cell + 1, :]
            parts = (
                jnp.where(mask1, value, 0.0),
                jnp.where(mask2, value, 0.0),
                jnp.where(row1, local, 0.0),
                jnp.where(row2, local, 0.0),
            )
            sums = [s + rolled(p, EXT * low) for s, p in zip(sums, parts)]
        low_slot = jnp.where(even, 0.0, 1.0)
        for out, base, value, local in (
            (first, 0, sums[0], sums[2]),
            (second, 0, sums[1] * low_slot, sums[3] * low_slot),
            (second, PAYLOAD, sums[1] * (1.0 - low_slot), sums[3] * (1.0 - low_slot)),
        ):
            out[base + high * ORB : base + (high + 1) * ORB, :] = value
            out[base + 2 * ORB + high : base + 2 * ORB + high + 1, :] = local
    for out, base in ((first, 0), (second, 0), (second, PAYLOAD)):
        out[base + 2 * ORB + 2 : base + PAYLOAD, :] = jnp.zeros((PAYLOAD - 2 * ORB - 2, LANES), jnp.float32)


def extend_kernel(flags, orbitals, second, first, field, edge_potential):
    mask1, mask2 = face_masks(flags, ORB)
    row1, row2 = face_masks(flags, 1)
    even = flags[2] == 0
    real = jnp.where(even, flags[3], flags[4]) != 0
    mask1, row1 = mask1 & real, row1 & real
    for cell in range(CELLS):
        field[cell * ORB : (cell + 1) * ORB, :] = orbitals[pl.ds(cell, ORB, stride=CELLS), :]
    for x in range(SIDE):
        total, total_potential = 0.0, 0.0
        for y in range(SIDE):
            high, low = divmod(x * SIDE + y, 8)

            def unpack(start, size, keep1, keep2):
                one = rolled(first[start : start + size, :], -EXT * low)
                two = jnp.where(even, second[start : start + size, :], second[PAYLOAD + start : PAYLOAD + start + size, :])
                two = rolled(two, -EXT * low)
                return rolled(jnp.where(keep2, one, 0.0) + jnp.where(keep1, two, 0.0), 2 * EXT * y)

            total = total + unpack(high * ORB, ORB, mask1, mask2)
            total_potential = total_potential + unpack(2 * ORB + high, 1, row1, row2)
        field[BLOCK + x * ORB : BLOCK + (x + 1) * ORB, :] = total
        edge_potential[x : x + 1, :] = total_potential


def edge_of(ref, x):
    return ref[x * ORB : (x + 1) * ORB, :]


def step_kernel(scale, with_previous, split, flags, potential, edge_potential, field, y1, x2, y2, x1, *rest):
    previous = rest[0] if with_previous else None
    out = rest[-2] if split else rest[-1]
    lane = lane_index(ORB)
    place = lane % (2 * EXT)
    lane_y = ((lane + EXT) // (2 * EXT)) % SIDE
    inside = ((place < EXT) & (flags[4] != 0)) | ((place >= EXT) & (flags[3] != 0))
    window = (lane < EXT) | (lane >= LANES - EXT)
    even_x, even_y = flags[0] == 0, flags[1] == 0
    weight = [-0.5 * scale * w for w in WEIGHTS]
    shift = MIDDLE + 1.5 * WEIGHTS[0]

    def line(get, one, two, even):
        pairs = [(get(one, i), get(two, i)) for i in range(SIDE)]
        below = [jnp.where(even, b, a) for a, b in pairs]
        above = [jnp.where(even, a, b) for a, b in pairs]
        return below + [get(field, i) for i in range(SIDE)] + above

    for y in range(SIDE):
        along = line(lambda ref, x: rows_of(ref, x * SIDE + y), x1, x2, even_x)
        for x in range(SIDE):
            cell = x * SIDE + y
            here = along[SIDE + x]
            there = rolled(edge_of(field, CELLS + x), -2 * EXT * y)
            total = (potential[cell : cell + 1, :] - shift) * scale * here
            for k in range(1, 5):
                pairs = along[SIDE + x + k] + along[SIDE + x - k]
                pairs = pairs + rolled(jnp.where(lane < k, there, here), -k)
                pairs = pairs + rolled(jnp.where(lane >= LANES - k, there, here), k)
                total = total + weight[k] * pairs
            if with_previous:
                total = total - rows_of(previous, cell)
            out[cell * ORB : (cell + 1) * ORB, :] = total
    for x in range(SIDE):
        along = line(lambda ref, y: rows_of(ref, x * SIDE + y), y1, y2, even_y)
        for y in range(SIDE):
            cell = x * SIDE + y
            total = rows_of(out, cell)
            for k in range(1, 5):
                total = total + weight[k] * (along[SIDE + y + k] + along[SIDE + y - k])
            out[cell * ORB : (cell + 1) * ORB, :] = total
    along = line(lambda ref, x: edge_of(ref, CELLS + x), x1, x2, even_x)
    for x in range(SIDE):
        here = along[SIDE + x]
        one, two = edge_of(y1, CELLS + x), edge_of(y2, CELLS + x)
        below, above = jnp.where(even_y, two, one), jnp.where(even_y, one, two)
        there = 0.0
        for y in range(SIDE):
            there = there + rolled(jnp.where(window, rows_of(field, x * SIDE + y), 0.0), 2 * EXT * y)
        total = (edge_potential[x : x + 1, :] - shift) * scale * here
        for k in range(1, 5):
            pairs = along[SIDE + x + k] + along[SIDE + x - k]
            pairs = pairs + rolled(jnp.where(lane_y < k, above, here), -2 * EXT * k)
            pairs = pairs + rolled(jnp.where(lane_y >= SIDE - k, below, here), 2 * EXT * k)
            pairs = pairs + rolled(jnp.where(place < k, there, here), -k)
            pairs = pairs + rolled(jnp.where(place >= 2 * EXT - k, there, here), k)
            total = total + weight[k] * pairs
        if with_previous:
            total = total - edge_of(previous, CELLS + x)
        total = jnp.where(inside, total, 0.0)
        if split:
            rest[-1][x * ORB : (x + 1) * ORB, :] = total
        else:
            out[BLOCK + x * ORB : BLOCK + (x + 1) * ORB, :] = total


def dot(a, b, contract):
    return lax.dot_general(
        a, b, ((contract[:1], contract[1:]), ((), ())), precision=lax.Precision.HIGHEST, preferred_element_type=jnp.float32
    )


def sums_kernel(potential, field, edge, after_y, after_x, sums):
    lane = lane_index(ORB)
    here_all, image_all = [], []
    for x in range(SIDE):
        for y in range(SIDE):
            cell = x * SIDE + y
            here, there = rows_of(field, cell), rolled(edge_of(edge, x), -2 * EXT * y)
            image = (0.5 * potential[cell : cell + 1, :] - 0.75 * WEIGHTS[0]) * here
            for k in range(1, 5):
                up = rows_of(field, cell + k * SIDE) if x + k < SIDE else rows_of(after_x, cell + (k - SIDE) * SIDE)
                up = up + (rows_of(field, cell + k) if y + k < SIDE else rows_of(after_y, cell + k - SIDE))
                up = up + rolled(jnp.where(lane < k, there, here), -k)
                image = image + (-0.5 * WEIGHTS[k]) * up
            here_all.append(here)
            image_all.append(image)
    here = jnp.concatenate(here_all, axis=1)
    image = jnp.concatenate(image_all, axis=1)
    sums[...] = jnp.zeros_like(sums)
    sums[:, : 2 * ORB] = dot(here, jnp.concatenate([here, image], axis=0), (1, 1))


def finish_kernel(cell_total, sums, field, q_block, ritz):
    sums = sums[...] * (1.0 / cell_total)
    row = lax.broadcasted_iota(jnp.int32, (ORB, LANES), 0)
    lane = lane_index(ORB)
    work = jnp.where(lane < ORB, sums, jnp.where(lane == row + ORB, 1.0, 0.0))
    for k in range(ORB - 1):
        pivot = work[k : k + 1, :]
        factor = work[:, k : k + 1] / pivot[:, k : k + 1]
        work = work - jnp.where(row > k, factor, 0.0) * pivot
    diagonal = jnp.sum(jnp.where(lane == row, work, 0.0), axis=1, keepdims=True)
    inverse = (work * (1.0 / jnp.sqrt(diagonal)))[:, ORB : 2 * ORB]
    half = sums[:, ORB : 2 * ORB]
    part = dot(dot(inverse, half, (1, 0)), inverse, (1, 1))
    ritz[...] = part + part.T
    for cell in range(CELLS):
        q_block[pl.ds(cell, ORB, stride=CELLS), :] = dot(inverse, rows_of(field, cell), (1, 0))


def swap(value, axis, first):
    pairs = []
    for i in range(first, lax.axis_size(axis) - 1, 2):
        pairs += [(i, i + 1), (i + 1, i)]
    return lax.ppermute(value, axis, pairs)


def from_above(value, axis):
    return lax.ppermute(value, axis, [(i + 1, i) for i in range(lax.axis_size(axis) - 1)])


def sum_everywhere(value):
    if all(lax.axis_size(axis) == 8 for axis in ("gx", "gy", "gz")):
        fours = [[0, 1, 2, 3], [4, 5, 6, 7]]
        value = value + lax.ppermute(value, "gy", [(i, i ^ 1) for i in range(8)])
        value = lax.psum(value, "gy", axis_index_groups=[[0, 2, 4, 6], [1, 3, 5, 7]])
        value = lax.psum(value, "gz", axis_index_groups=fours)
        value = lax.psum(value, "gx", axis_index_groups=fours)
        rings = [[8 * gx + gz, 8 * gx + 32 + gz, 8 * gx + gz + 4, 8 * gx + 32 + gz + 4] for gx in range(4) for gz in range(4)]
        return lax.psum(value, ("gx", "gz"), axis_index_groups=rings)
    return lax.psum(value, ("gx", "gy", "gz"))


def call(kernel, outs, smem=True):
    def run(*operands):
        specs = [pl.BlockSpec(memory_space=pltpu.VMEM)] * len(operands)
        if smem:
            specs[0] = pl.BlockSpec(memory_space=pltpu.SMEM)
        return pl.pallas_call(
            kernel,
            out_shape=[jax.ShapeDtypeStruct(shape, jnp.float32) for shape in outs],
            in_specs=specs,
            out_specs=[pl.BlockSpec(memory_space=pltpu.VMEM)] * len(outs),
            compiler_params=pltpu.CompilerParams(vmem_limit_bytes=8 * 1024 * 1024),
        )(*operands)

    return run


def body(orbitals, potential):
    at = [lax.axis_index(axis) for axis in ("gx", "gy", "gz")]
    cell_total = orbitals[0].size * lax.axis_size("gx") * lax.axis_size("gy") * lax.axis_size("gz")
    flags = jnp.stack(
        [at[0] % 2, at[1] % 2, at[2] % 2, (at[2] > 0).astype(jnp.int32), (at[2] < lax.axis_size("gz") - 1).astype(jnp.int32)]
    ).astype(jnp.int32)
    shape = orbitals.shape
    orbitals = orbitals.reshape(BLOCK, LANES)
    potential = potential.reshape(CELLS, LANES)
    block, edge, sent = (BLOCK, LANES), (EDGE, LANES), (BLOCK + EDGE, LANES)

    first, second = call(payload_kernel, ((PAYLOAD, LANES), (2 * PAYLOAD, LANES)))(flags, orbitals, potential)
    deep = lax.axis_size("gz")
    first = swap(first, "gz", 0)
    second = lax.psum(second, "gz", axis_index_groups=[[i, (i + 1) % deep] for i in range(1, deep, 2)])
    field, edge_potential = call(extend_kernel, (sent, (8, LANES)))(flags, orbitals, second, first)

    def advance(field, scale, previous, split):
        y2, y1, x2, x1 = [swap(field, axis, first) for axis in ("gy", "gx") for first in (1, 0)]
        kernel = functools.partial(step_kernel, scale, bool(previous), split)
        outs = (block, edge) if split else (sent,)
        return call(kernel, outs)(flags, potential, edge_potential, field, y1, x2, y2, x1, *previous)

    (field1,) = advance(field, 1.0 / HALF, (), False)
    (field2,) = advance(field1, 2.0 / HALF, (field,), False)
    field, edge = advance(field2, 2.0 / HALF, (field1,), True)
    after_y, after_x = from_above(field, "gy"), from_above(field, "gx")
    sums = call(sums_kernel, ((ORB, LANES),), smem=False)(potential, field, edge, after_y, after_x)[0]
    sums = sum_everywhere(sums)
    q_block, ritz = call(functools.partial(finish_kernel, cell_total), (block, (ORB, ORB)), smem=False)(sums, field)
    return q_block.reshape(shape), ritz


def solution(mesh):
    placed = (P(None, "gx", "gy", "gz"), P("gx", "gy", "gz"))
    return jax.shard_map(
        body,
        mesh=mesh,
        in_specs=placed,
        out_specs=(P(None, "gx", "gy", "gz"), P()),
        check_vma=False,
    )
```

```python
import functools

import jax
import jax.numpy as jnp
from jax import lax
from jax.experimental import pallas as pl
from jax.experimental.pallas import tpu as pltpu
from jax.sharding import PartitionSpec as P

WEIGHTS = (-205.0 / 72.0, 8.0 / 5.0, -1.0 / 5.0, 8.0 / 315.0, -1.0 / 560.0)
HALF = (12.0 - 1.5) / 2.0
MIDDLE = (12.0 + 1.5) / 2.0
ORB = 16
SIDE = 4
CELLS = SIDE * SIDE
LANES = 128
EXT = 16
BLOCK = CELLS * ORB
EDGE = SIDE * ORB
PAYLOAD = 2 * ORB + 8


def lane_index(rows):
    return lax.broadcasted_iota(jnp.int32, (rows, LANES), 1)


def rolled(value, amount):
    amount %= LANES
    return pltpu.roll(value, amount, 1) if amount else value


def rows_of(ref, cell):
    return ref[cell * ORB : (cell + 1) * ORB, :]


def face_masks(flags, rows):
    lane = lane_index(rows)
    even = flags[2] == 0
    upper = jnp.where(even, LANES - EXT, 0)
    lower = jnp.where(even, 0, LANES - EXT)
    first = (lane >= upper) & (lane < upper + EXT)
    second = (lane >= lower) & (lane < lower + EXT)
    return first, second


def payload_kernel(flags, orbitals, potential, first, second):
    mask1, mask2 = face_masks(flags, ORB)
    row1, row2 = face_masks(flags, 1)
    for high in range(2):
        sums = [jnp.zeros((ORB, LANES), jnp.float32)] * 2 + [jnp.zeros((1, LANES), jnp.float32)] * 2
        for low in range(8):
            cell = 8 * high + low
            value = orbitals[pl.ds(cell, ORB, stride=CELLS), :]
            local = potential[cell : cell + 1, :]
            parts = (
                jnp.where(mask1, value, 0.0),
                jnp.where(mask2, value, 0.0),
                jnp.where(row1, local, 0.0),
                jnp.where(row2, local, 0.0),
            )
            sums = [s + rolled(p, EXT * low) for s, p in zip(sums, parts)]
        for out, value, local in ((first, sums[0], sums[2]), (second, sums[1], sums[3])):
            out[high * ORB : (high + 1) * ORB, :] = value
            out[2 * ORB + high : 2 * ORB + high + 1, :] = local
    for out in (first, second):
        out[2 * ORB + 2 :, :] = jnp.zeros((PAYLOAD - 2 * ORB - 2, LANES), jnp.float32)


def extend_kernel(flags, orbitals, second, first, field, edge_potential):
    mask1, mask2 = face_masks(flags, ORB)
    row1, row2 = face_masks(flags, 1)
    for cell in range(CELLS):
        field[cell * ORB : (cell + 1) * ORB, :] = orbitals[pl.ds(cell, ORB, stride=CELLS), :]
    for x in range(SIDE):
        total, total_potential = 0.0, 0.0
        for y in range(SIDE):
            high, low = divmod(x * SIDE + y, 8)

            def unpack(start, size, keep1, keep2):
                one = rolled(first[start : start + size, :], -EXT * low)
                two = rolled(second[start : start + size, :], -EXT * low)
                return rolled(jnp.where(keep2, one, 0.0) + jnp.where(keep1, two, 0.0), 2 * EXT * y)

            total = total + unpack(high * ORB, ORB, mask1, mask2)
            total_potential = total_potential + unpack(2 * ORB + high, 1, row1, row2)
        field[BLOCK + x * ORB : BLOCK + (x + 1) * ORB, :] = total
        edge_potential[x : x + 1, :] = total_potential


def edge_of(ref, x):
    return ref[x * ORB : (x + 1) * ORB, :]


def step_kernel(scale, with_previous, split, flags, potential, edge_potential, field, y1, x2, y2, x1, *rest):
    previous = rest[0] if with_previous else None
    out = rest[-2] if split else rest[-1]
    lane = lane_index(ORB)
    place = lane % (2 * EXT)
    lane_y = ((lane + EXT) // (2 * EXT)) % SIDE
    inside = ((place < EXT) & (flags[4] != 0)) | ((place >= EXT) & (flags[3] != 0))
    window = (lane < EXT) | (lane >= LANES - EXT)
    even_x, even_y = flags[0] == 0, flags[1] == 0
    weight = [-0.5 * scale * w for w in WEIGHTS]
    shift = MIDDLE + 1.5 * WEIGHTS[0]

    def line(get, one, two, even):
        pairs = [(get(one, i), get(two, i)) for i in range(SIDE)]
        below = [jnp.where(even, b, a) for a, b in pairs]
        above = [jnp.where(even, a, b) for a, b in pairs]
        return below + [get(field, i) for i in range(SIDE)] + above

    for y in range(SIDE):
        along = line(lambda ref, x: rows_of(ref, x * SIDE + y), x1, x2, even_x)
        for x in range(SIDE):
            cell = x * SIDE + y
            here = along[SIDE + x]
            there = rolled(edge_of(field, CELLS + x), -2 * EXT * y)
            total = (potential[cell : cell + 1, :] - shift) * scale * here
            for k in range(1, 5):
                pairs = along[SIDE + x + k] + along[SIDE + x - k]
                pairs = pairs + rolled(jnp.where(lane < k, there, here), -k)
                pairs = pairs + rolled(jnp.where(lane >= LANES - k, there, here), k)
                total = total + weight[k] * pairs
            if with_previous:
                total = total - rows_of(previous, cell)
            out[cell * ORB : (cell + 1) * ORB, :] = total
    for x in range(SIDE):
        along = line(lambda ref, y: rows_of(ref, x * SIDE + y), y1, y2, even_y)
        for y in range(SIDE):
            cell = x * SIDE + y
            total = rows_of(out, cell)
            for k in range(1, 5):
                total = total + weight[k] * (along[SIDE + y + k] + along[SIDE + y - k])
            out[cell * ORB : (cell + 1) * ORB, :] = total
    along = line(lambda ref, x: edge_of(ref, CELLS + x), x1, x2, even_x)
    for x in range(SIDE):
        here = along[SIDE + x]
        one, two = edge_of(y1, CELLS + x), edge_of(y2, CELLS + x)
        below, above = jnp.where(even_y, two, one), jnp.where(even_y, one, two)
        there = 0.0
        for y in range(SIDE):
            there = there + rolled(jnp.where(window, rows_of(field, x * SIDE + y), 0.0), 2 * EXT * y)
        total = (edge_potential[x : x + 1, :] - shift) * scale * here
        for k in range(1, 5):
            pairs = along[SIDE + x + k] + along[SIDE + x - k]
            pairs = pairs + rolled(jnp.where(lane_y < k, above, here), -2 * EXT * k)
            pairs = pairs + rolled(jnp.where(lane_y >= SIDE - k, below, here), 2 * EXT * k)
            pairs = pairs + rolled(jnp.where(place < k, there, here), -k)
            pairs = pairs + rolled(jnp.where(place >= 2 * EXT - k, there, here), k)
            total = total + weight[k] * pairs
        if with_previous:
            total = total - edge_of(previous, CELLS + x)
        total = jnp.where(inside, total, 0.0)
        if split:
            rest[-1][x * ORB : (x + 1) * ORB, :] = total
        else:
            out[BLOCK + x * ORB : BLOCK + (x + 1) * ORB, :] = total


def dot(a, b, contract):
    return lax.dot_general(
        a, b, ((contract[:1], contract[1:]), ((), ())), precision=lax.Precision.HIGHEST, preferred_element_type=jnp.float32
    )


def sums_kernel(flags, potential, field, edge, after_y, beside_x, sums):
    lane = lane_index(ORB)
    up = flags[1] == 0
    along_x = {}
    for y in range(SIDE):
        rows = [rows_of(ref, x * SIDE + y) for ref in (field, beside_x) for x in range(SIDE)]
        line = [jnp.where(up, rows[start + i], rows[start + SIDE - 1 - i]) for start in (0, SIDE) for i in range(SIDE)]
        terms = [sum(-0.5 * WEIGHTS[k] * line[i + k] for k in range(1, 5)) for i in range(SIDE)]
        for x in range(SIDE):
            along_x[x, y] = jnp.where(up, terms[x], terms[SIDE - 1 - x])
    here_all, image_all = [], []
    for x in range(SIDE):
        for y in range(SIDE):
            cell = x * SIDE + y
            here, there = rows_of(field, cell), rolled(edge_of(edge, x), -2 * EXT * y)
            image = (0.5 * potential[cell : cell + 1, :] - 0.75 * WEIGHTS[0]) * here + along_x[x, y]
            for k in range(1, 5):
                above = rows_of(field, cell + k) if y + k < SIDE else rows_of(after_y, cell + k - SIDE)
                above = above + rolled(jnp.where(lane < k, there, here), -k)
                image = image + (-0.5 * WEIGHTS[k]) * above
            here_all.append(here)
            image_all.append(image)
    here = jnp.concatenate(here_all, axis=1)
    image = jnp.concatenate(image_all, axis=1)
    sums[...] = jnp.zeros_like(sums)
    sums[:, : 2 * ORB] = dot(here, jnp.concatenate([here, image], axis=0), (1, 1))


def finish_kernel(cell_total, sums, field, q_block, ritz):
    sums = sums[...] * (1.0 / cell_total)
    row = lax.broadcasted_iota(jnp.int32, (ORB, LANES), 0)
    lane = lane_index(ORB)
    work = jnp.where(lane < ORB, sums, jnp.where(lane == row + ORB, 1.0, 0.0))
    for k in range(ORB - 1):
        pivot = work[k : k + 1, :]
        factor = work[:, k : k + 1] / pivot[:, k : k + 1]
        work = work - jnp.where(row > k, factor, 0.0) * pivot
    diagonal = jnp.sum(jnp.where(lane == row, work, 0.0), axis=1, keepdims=True)
    inverse = (work * (1.0 / jnp.sqrt(diagonal)))[:, ORB : 2 * ORB]
    half = sums[:, ORB : 2 * ORB]
    part = dot(dot(inverse, half, (1, 0)), inverse, (1, 1))
    ritz[...] = part + part.T
    for cell in range(CELLS):
        q_block[pl.ds(cell, ORB, stride=CELLS), :] = dot(inverse, rows_of(field, cell), (1, 0))


def swap(value, axis, first):
    pairs = []
    for i in range(first, lax.axis_size(axis) - 1, 2):
        pairs += [(i, i + 1), (i + 1, i)]
    return lax.ppermute(value, axis, pairs)


def swap_x(value, turn):
    deep, wide = lax.axis_size("gx"), lax.axis_size("gy")
    pairs = []
    for j in range(wide):
        for i in range((turn + j) % 2, deep - 1, 2):
            pairs += [(i * wide + j, (i + 1) * wide + j), ((i + 1) * wide + j, i * wide + j)]
    return lax.ppermute(value, ("gx", "gy"), pairs)


def one_side_x(value):
    deep, wide = lax.axis_size("gx"), lax.axis_size("gy")
    pairs = []
    for j in range(wide):
        for i in range(deep - 1):
            low, high = i * wide + j, (i + 1) * wide + j
            pairs.append((low, high) if j % 2 else (high, low))
    return lax.ppermute(value, ("gx", "gy"), pairs)


def from_above(value, axis):
    return lax.ppermute(value, axis, [(i + 1, i) for i in range(lax.axis_size(axis) - 1)])


def sum_everywhere(value):
    if all(lax.axis_size(axis) == 8 for axis in ("gx", "gy", "gz")):
        fours = [[0, 1, 2, 3], [4, 5, 6, 7]]
        value = value + lax.ppermute(value, "gy", [(i, i ^ 1) for i in range(8)])
        value = lax.psum(value, "gy", axis_index_groups=[[0, 2, 4, 6], [1, 3, 5, 7]])
        value = lax.psum(value, "gz", axis_index_groups=fours)
        value = lax.psum(value, "gx", axis_index_groups=fours)
        rings = [[8 * gx + gz, 8 * gx + 32 + gz, 8 * gx + gz + 4, 8 * gx + 32 + gz + 4] for gx in range(4) for gz in range(4)]
        return lax.psum(value, ("gx", "gz"), axis_index_groups=rings)
    return lax.psum(value, ("gx", "gy", "gz"))


def call(kernel, outs, smem=True):
    def run(*operands):
        specs = [pl.BlockSpec(memory_space=pltpu.VMEM)] * len(operands)
        if smem:
            specs[0] = pl.BlockSpec(memory_space=pltpu.SMEM)
        return pl.pallas_call(
            kernel,
            out_shape=[jax.ShapeDtypeStruct(shape, jnp.float32) for shape in outs],
            in_specs=specs,
            out_specs=[pl.BlockSpec(memory_space=pltpu.VMEM)] * len(outs),
            compiler_params=pltpu.CompilerParams(vmem_limit_bytes=8 * 1024 * 1024),
        )(*operands)

    return run


def body(orbitals, potential):
    at = [lax.axis_index(axis) for axis in ("gx", "gy", "gz")]
    cell_total = orbitals[0].size * lax.axis_size("gx") * lax.axis_size("gy") * lax.axis_size("gz")
    flags = jnp.stack(
        [(at[0] + at[1]) % 2, at[1] % 2, at[2] % 2, (at[2] > 0).astype(jnp.int32), (at[2] < lax.axis_size("gz") - 1).astype(jnp.int32)]
    ).astype(jnp.int32)
    shape = orbitals.shape
    orbitals = orbitals.reshape(BLOCK, LANES)
    potential = potential.reshape(CELLS, LANES)
    block, edge, sent = (BLOCK, LANES), (EDGE, LANES), (BLOCK + EDGE, LANES)

    first, second = call(payload_kernel, ((PAYLOAD, LANES),) * 2)(flags, orbitals, potential)
    second, first = swap(second, "gz", 1), swap(first, "gz", 0)
    field, edge_potential = call(extend_kernel, (sent, (8, LANES)))(flags, orbitals, second, first)

    def advance(field, scale, previous, split):
        y2, y1, x2, x1 = swap(field, "gy", 1), swap(field, "gy", 0), swap_x(field, 1), swap_x(field, 0)
        kernel = functools.partial(step_kernel, scale, bool(previous), split)
        outs = (block, edge) if split else (sent,)
        return call(kernel, outs)(flags, potential, edge_potential, field, y1, x2, y2, x1, *previous)

    (field1,) = advance(field, 1.0 / HALF, (), False)
    (field2,) = advance(field1, 2.0 / HALF, (field,), False)
    field, edge = advance(field2, 2.0 / HALF, (field1,), True)
    after_y, beside_x = from_above(field, "gy"), one_side_x(field)
    sums = call(sums_kernel, ((ORB, LANES),))(flags, potential, field, edge, after_y, beside_x)[0]
    sums = sum_everywhere(sums)
    q_block, ritz = call(functools.partial(finish_kernel, cell_total), (block, (ORB, ORB)), smem=False)(sums, field)
    return q_block.reshape(shape), ritz


def solution(mesh):
    placed = (P(None, "gx", "gy", "gz"), P("gx", "gy", "gz"))
    return jax.shard_map(
        body,
        mesh=mesh,
        in_specs=placed,
        out_specs=(P(None, "gx", "gy", "gz"), P()),
        check_vma=False,
    )
```

```python
import functools

import jax
import jax.numpy as jnp
from jax import lax
from jax.experimental import pallas as pl
from jax.experimental.pallas import tpu as pltpu
from jax.sharding import PartitionSpec as P

WEIGHTS = (-205.0 / 72.0, 8.0 / 5.0, -1.0 / 5.0, 8.0 / 315.0, -1.0 / 560.0)
HALF = (12.0 - 1.5) / 2.0
MIDDLE = (12.0 + 1.5) / 2.0
ORB = 16
SIDE = 4
CELLS = SIDE * SIDE
LANES = 128
EXT = 16
BLOCK = CELLS * ORB
EDGE = SIDE * ORB
PAYLOAD = 2 * ORB + 8


def lane_index(rows):
    return lax.broadcasted_iota(jnp.int32, (rows, LANES), 1)


def rolled(value, amount):
    amount %= LANES
    return pltpu.roll(value, amount, 1) if amount else value


def rows_of(ref, cell):
    return ref[cell * ORB : (cell + 1) * ORB, :]


def face_masks(flags, rows):
    lane = lane_index(rows)
    even = flags[2] == 0
    upper = jnp.where(even, LANES - EXT, 0)
    lower = jnp.where(even, 0, LANES - EXT)
    first = (lane >= upper) & (lane < upper + EXT)
    second = (lane >= lower) & (lane < lower + EXT)
    return first, second


def payload_kernel(flags, orbitals, potential, first, second):
    mask1, mask2 = face_masks(flags, ORB)
    row1, row2 = face_masks(flags, 1)
    for high in range(2):
        sums = [jnp.zeros((ORB, LANES), jnp.float32)] * 2 + [jnp.zeros((1, LANES), jnp.float32)] * 2
        for low in range(8):
            cell = 8 * high + low
            value = orbitals[pl.ds(cell, ORB, stride=CELLS), :]
            local = potential[cell : cell + 1, :]
            parts = (
                jnp.where(mask1, value, 0.0),
                jnp.where(mask2, value, 0.0),
                jnp.where(row1, local, 0.0),
                jnp.where(row2, local, 0.0),
            )
            sums = [s + rolled(p, EXT * low) for s, p in zip(sums, parts)]
        for out, value, local in ((first, sums[0], sums[2]), (second, sums[1], sums[3])):
            out[high * ORB : (high + 1) * ORB, :] = value
            out[2 * ORB + high : 2 * ORB + high + 1, :] = local
    for out in (first, second):
        out[2 * ORB + 2 :, :] = jnp.zeros((PAYLOAD - 2 * ORB - 2, LANES), jnp.float32)


def extend_kernel(flags, orbitals, second, first, field, edge_potential):
    mask1, mask2 = face_masks(flags, ORB)
    row1, row2 = face_masks(flags, 1)
    for cell in range(CELLS):
        field[cell * ORB : (cell + 1) * ORB, :] = orbitals[pl.ds(cell, ORB, stride=CELLS), :]
    for x in range(SIDE):
        total, total_potential = 0.0, 0.0
        for y in range(SIDE):
            high, low = divmod(x * SIDE + y, 8)

            def unpack(start, size, keep1, keep2):
                one = rolled(first[start : start + size, :], -EXT * low)
                two = rolled(second[start : start + size, :], -EXT * low)
                return rolled(jnp.where(keep2, one, 0.0) + jnp.where(keep1, two, 0.0), 2 * EXT * y)

            total = total + unpack(high * ORB, ORB, mask1, mask2)
            total_potential = total_potential + unpack(2 * ORB + high, 1, row1, row2)
        field[BLOCK + x * ORB : BLOCK + (x + 1) * ORB, :] = total
        edge_potential[x : x + 1, :] = total_potential


def edge_of(ref, x):
    return ref[x * ORB : (x + 1) * ORB, :]


def sides(is_above, get):
    layers = [get(i) for i in range(SIDE)]
    return [jnp.where(is_above, 0.0, v) for v in layers], [jnp.where(is_above, v, 0.0) for v in layers]


def block_kernel(scale, with_previous, flags, potential, field, *rest):
    previous = rest[0] if with_previous else None
    y2, x1, out = rest[-3:]
    lane = lane_index(ORB)
    weight = [-0.5 * scale * w for w in WEIGHTS]
    shift = MIDDLE + 1.5 * WEIGHTS[0]
    for y in range(SIDE):
        below, above = sides(flags[0] == 0, lambda x: rows_of(x1, x * SIDE + y))
        along = below + [rows_of(field, x * SIDE + y) for x in range(SIDE)] + above
        for x in range(SIDE):
            cell = x * SIDE + y
            here = along[SIDE + x]
            there = rolled(edge_of(field, CELLS + x), -2 * EXT * y)
            total = (potential[cell : cell + 1, :] - shift) * scale * here
            for k in range(1, 5):
                pairs = along[SIDE + x + k] + along[SIDE + x - k]
                pairs = pairs + rolled(jnp.where(lane < k, there, here), -k)
                pairs = pairs + rolled(jnp.where(lane >= LANES - k, there, here), k)
                total = total + weight[k] * pairs
            if with_previous:
                total = total - rows_of(previous, cell)
            out[cell * ORB : (cell + 1) * ORB, :] = total
    for x in range(SIDE):
        below, above = sides(flags[1] != 0, lambda y: rows_of(y2, x * SIDE + y))
        along = below + [rows_of(field, x * SIDE + y) for y in range(SIDE)] + above
        for y in range(SIDE):
            cell = x * SIDE + y
            total = rows_of(out, cell)
            for k in range(1, 5):
                total = total + weight[k] * (along[SIDE + y + k] + along[SIDE + y - k])
            out[cell * ORB : (cell + 1) * ORB, :] = total


def join_kernel(scale, with_previous, split, flags, edge_potential, part, field, y1, x2, y2, x1, *rest):
    previous = rest[0] if with_previous else None
    out = rest[-2] if split else rest[-1]
    lane = lane_index(ORB)
    place = lane % (2 * EXT)
    lane_y = ((lane + EXT) // (2 * EXT)) % SIDE
    inside = ((place < EXT) & (flags[4] != 0)) | ((place >= EXT) & (flags[3] != 0))
    window = (lane < EXT) | (lane >= LANES - EXT)
    even_x, even_y = flags[0] == 0, flags[1] == 0
    weight = [-0.5 * scale * w for w in WEIGHTS]
    shift = MIDDLE + 1.5 * WEIGHTS[0]

    def face_terms(below, above, i):
        terms = [weight[k] * above[i + k - SIDE] for k in range(SIDE - i, 5)]
        return sum(terms + [weight[k] * below[i - k + SIDE] for k in range(i + 1, 5)])

    for y in range(SIDE):
        below, above = sides(flags[0] != 0, lambda x: rows_of(x2, x * SIDE + y))
        for x in range(SIDE):
            cell = x * SIDE + y
            out[cell * ORB : (cell + 1) * ORB, :] = rows_of(part, cell) + face_terms(below, above, x)
    for x in range(SIDE):
        below, above = sides(even_y, lambda y: rows_of(y1, x * SIDE + y))
        for y in range(SIDE):
            cell = x * SIDE + y
            out[cell * ORB : (cell + 1) * ORB, :] = rows_of(out, cell) + face_terms(below, above, y)
    pairs = [(edge_of(x1, CELLS + x), edge_of(x2, CELLS + x)) for x in range(SIDE)]
    along = [jnp.where(even_x, b, a) for a, b in pairs]
    along = along + [edge_of(field, CELLS + x) for x in range(SIDE)] + [jnp.where(even_x, a, b) for a, b in pairs]
    for x in range(SIDE):
        here = along[SIDE + x]
        one, two = edge_of(y1, CELLS + x), edge_of(y2, CELLS + x)
        below, above = jnp.where(even_y, two, one), jnp.where(even_y, one, two)
        there = 0.0
        for y in range(SIDE):
            there = there + rolled(jnp.where(window, rows_of(field, x * SIDE + y), 0.0), 2 * EXT * y)
        total = (edge_potential[x : x + 1, :] - shift) * scale * here
        for k in range(1, 5):
            terms = along[SIDE + x + k] + along[SIDE + x - k]
            terms = terms + rolled(jnp.where(lane_y < k, above, here), -2 * EXT * k)
            terms = terms + rolled(jnp.where(lane_y >= SIDE - k, below, here), 2 * EXT * k)
            terms = terms + rolled(jnp.where(place < k, there, here), -k)
            terms = terms + rolled(jnp.where(place >= 2 * EXT - k, there, here), k)
            total = total + weight[k] * terms
        if with_previous:
            total = total - edge_of(previous, CELLS + x)
        total = jnp.where(inside, total, 0.0)
        if split:
            rest[-1][x * ORB : (x + 1) * ORB, :] = total
        else:
            out[BLOCK + x * ORB : BLOCK + (x + 1) * ORB, :] = total


def dot(a, b, contract):
    return lax.dot_general(
        a, b, ((contract[:1], contract[1:]), ((), ())), precision=lax.Precision.HIGHEST, preferred_element_type=jnp.float32
    )


def sums_kernel(flags, potential, field, edge, after_y, beside_x, sums):
    lane = lane_index(ORB)
    up = flags[1] == 0
    along_x = {}
    for y in range(SIDE):
        rows = [rows_of(ref, x * SIDE + y) for ref in (field, beside_x) for x in range(SIDE)]
        line = [jnp.where(up, rows[start + i], rows[start + SIDE - 1 - i]) for start in (0, SIDE) for i in range(SIDE)]
        terms = [sum(-0.5 * WEIGHTS[k] * line[i + k] for k in range(1, 5)) for i in range(SIDE)]
        for x in range(SIDE):
            along_x[x, y] = jnp.where(up, terms[x], terms[SIDE - 1 - x])
    here_all, image_all = [], []
    for x in range(SIDE):
        for y in range(SIDE):
            cell = x * SIDE + y
            here, there = rows_of(field, cell), rolled(edge_of(edge, x), -2 * EXT * y)
            image = (0.5 * potential[cell : cell + 1, :] - 0.75 * WEIGHTS[0]) * here + along_x[x, y]
            for k in range(1, 5):
                above = rows_of(field, cell + k) if y + k < SIDE else rows_of(after_y, cell + k - SIDE)
                above = above + rolled(jnp.where(lane < k, there, here), -k)
                image = image + (-0.5 * WEIGHTS[k]) * above
            here_all.append(here)
            image_all.append(image)
    here = jnp.concatenate(here_all, axis=1)
    image = jnp.concatenate(image_all, axis=1)
    sums[...] = jnp.zeros_like(sums)
    sums[:, : 2 * ORB] = dot(here, jnp.concatenate([here, image], axis=0), (1, 1))


def finish_kernel(cell_total, sums, field, q_block, ritz):
    sums = sums[...] * (1.0 / cell_total)
    row = lax.broadcasted_iota(jnp.int32, (ORB, LANES), 0)
    lane = lane_index(ORB)
    work = jnp.where(lane < ORB, sums, jnp.where(lane == row + ORB, 1.0, 0.0))
    for k in range(ORB - 1):
        pivot = work[k : k + 1, :]
        factor = work[:, k : k + 1] / pivot[:, k : k + 1]
        work = work - jnp.where(row > k, factor, 0.0) * pivot
    diagonal = jnp.sum(jnp.where(lane == row, work, 0.0), axis=1, keepdims=True)
    inverse = (work * (1.0 / jnp.sqrt(diagonal)))[:, ORB : 2 * ORB]
    half = sums[:, ORB : 2 * ORB]
    part = dot(dot(inverse, half, (1, 0)), inverse, (1, 1))
    ritz[...] = part + part.T
    for cell in range(CELLS):
        q_block[pl.ds(cell, ORB, stride=CELLS), :] = dot(inverse, rows_of(field, cell), (1, 0))


def swap(value, axis, first):
    pairs = []
    for i in range(first, lax.axis_size(axis) - 1, 2):
        pairs += [(i, i + 1), (i + 1, i)]
    return lax.ppermute(value, axis, pairs)


def swap_x(value, turn):
    deep, wide = lax.axis_size("gx"), lax.axis_size("gy")
    pairs = []
    for j in range(wide):
        for i in range((turn + j) % 2, deep - 1, 2):
            pairs += [(i * wide + j, (i + 1) * wide + j), ((i + 1) * wide + j, i * wide + j)]
    return lax.ppermute(value, ("gx", "gy"), pairs)


def one_side_x(value):
    deep, wide = lax.axis_size("gx"), lax.axis_size("gy")
    pairs = []
    for j in range(wide):
        for i in range(deep - 1):
            low, high = i * wide + j, (i + 1) * wide + j
            pairs.append((low, high) if j % 2 else (high, low))
    return lax.ppermute(value, ("gx", "gy"), pairs)


def from_above(value, axis):
    return lax.ppermute(value, axis, [(i + 1, i) for i in range(lax.axis_size(axis) - 1)])


def sum_everywhere(value):
    if all(lax.axis_size(axis) == 8 for axis in ("gx", "gy", "gz")):
        fours = [[0, 1, 2, 3], [4, 5, 6, 7]]
        value = value + lax.ppermute(value, "gy", [(i, i ^ 1) for i in range(8)])
        value = lax.psum(value, "gy", axis_index_groups=[[0, 2, 4, 6], [1, 3, 5, 7]])
        value = lax.psum(value, "gz", axis_index_groups=fours)
        value = lax.psum(value, "gx", axis_index_groups=fours)
        rings = [[8 * gx + gz, 8 * gx + 32 + gz, 8 * gx + gz + 4, 8 * gx + 32 + gz + 4] for gx in range(4) for gz in range(4)]
        return lax.psum(value, ("gx", "gz"), axis_index_groups=rings)
    return lax.psum(value, ("gx", "gy", "gz"))


def call(kernel, outs, smem=True):
    def run(*operands):
        specs = [pl.BlockSpec(memory_space=pltpu.VMEM)] * len(operands)
        if smem:
            specs[0] = pl.BlockSpec(memory_space=pltpu.SMEM)
        return pl.pallas_call(
            kernel,
            out_shape=[jax.ShapeDtypeStruct(shape, jnp.float32) for shape in outs],
            in_specs=specs,
            out_specs=[pl.BlockSpec(memory_space=pltpu.VMEM)] * len(outs),
            compiler_params=pltpu.CompilerParams(vmem_limit_bytes=8 * 1024 * 1024),
        )(*operands)

    return run


def body(orbitals, potential):
    at = [lax.axis_index(axis) for axis in ("gx", "gy", "gz")]
    cell_total = orbitals[0].size * lax.axis_size("gx") * lax.axis_size("gy") * lax.axis_size("gz")
    flags = jnp.stack(
        [(at[0] + at[1]) % 2, at[1] % 2, at[2] % 2, (at[2] > 0).astype(jnp.int32), (at[2] < lax.axis_size("gz") - 1).astype(jnp.int32)]
    ).astype(jnp.int32)
    shape = orbitals.shape
    orbitals = orbitals.reshape(BLOCK, LANES)
    potential = potential.reshape(CELLS, LANES)
    block, edge, sent = (BLOCK, LANES), (EDGE, LANES), (BLOCK + EDGE, LANES)

    first, second = call(payload_kernel, ((PAYLOAD, LANES),) * 2)(flags, orbitals, potential)
    second, first = swap(second, "gz", 1), swap(first, "gz", 0)
    field, edge_potential = call(extend_kernel, (sent, (8, LANES)))(flags, orbitals, second, first)

    def advance(field, scale, previous, split):
        y2, y1, x2, x1 = swap(field, "gy", 1), swap(field, "gy", 0), swap_x(field, 1), swap_x(field, 0)
        kernel = functools.partial(block_kernel, scale, bool(previous))
        (part,) = call(kernel, (block,))(flags, potential, field, *previous, y2, x1)
        kernel = functools.partial(join_kernel, scale, bool(previous), split)
        outs = (block, edge) if split else (sent,)
        return call(kernel, outs)(flags, edge_potential, part, field, y1, x2, y2, x1, *previous)

    (field1,) = advance(field, 1.0 / HALF, (), False)
    (field2,) = advance(field1, 2.0 / HALF, (field,), False)
    field, edge = advance(field2, 2.0 / HALF, (field1,), True)
    after_y, beside_x = from_above(field, "gy"), one_side_x(field)
    sums = call(sums_kernel, ((ORB, LANES),))(flags, potential, field, edge, after_y, beside_x)[0]
    sums = sum_everywhere(sums)
    q_block, ritz = call(functools.partial(finish_kernel, cell_total), (block, (ORB, ORB)), smem=False)(sums, field)
    return q_block.reshape(shape), ritz


def solution(mesh):
    placed = (P(None, "gx", "gy", "gz"), P("gx", "gy", "gz"))
    return jax.shard_map(
        body,
        mesh=mesh,
        in_specs=placed,
        out_specs=(P(None, "gx", "gy", "gz"), P()),
        check_vma=False,
    )
```

```python
import functools

import jax
import jax.numpy as jnp
from jax import lax
from jax.experimental import pallas as pl
from jax.experimental.pallas import tpu as pltpu
from jax.sharding import PartitionSpec as P

WEIGHTS = (-205.0 / 72.0, 8.0 / 5.0, -1.0 / 5.0, 8.0 / 315.0, -1.0 / 560.0)
HALF = (12.0 - 1.5) / 2.0
MIDDLE = (12.0 + 1.5) / 2.0
ORB = 16
SIDE = 4
CELLS = SIDE * SIDE
LANES = 128
EXT = 16
BLOCK = CELLS * ORB
EDGE = SIDE * ORB
PAYLOAD = 2 * ORB + 8


def lane_index(rows):
    return lax.broadcasted_iota(jnp.int32, (rows, LANES), 1)


def rolled(value, amount):
    amount %= LANES
    return pltpu.roll(value, amount, 1) if amount else value


def rows_of(ref, cell):
    return ref[cell * ORB : (cell + 1) * ORB, :]


def face_masks(flags, rows):
    lane = lane_index(rows)
    even = flags[2] == 0
    upper = jnp.where(even, LANES - EXT, 0)
    lower = jnp.where(even, 0, LANES - EXT)
    first = (lane >= upper) & (lane < upper + EXT)
    second = (lane >= lower) & (lane < lower + EXT)
    return first, second


def payload_kernel(flags, orbitals, potential, first, second):
    mask1, mask2 = face_masks(flags, ORB)
    row1, row2 = face_masks(flags, 1)
    for high in range(2):
        sums = [jnp.zeros((ORB, LANES), jnp.float32)] * 2 + [jnp.zeros((1, LANES), jnp.float32)] * 2
        for low in range(8):
            cell = 8 * high + low
            value = orbitals[pl.ds(cell, ORB, stride=CELLS), :]
            local = potential[cell : cell + 1, :]
            parts = (
                jnp.where(mask1, value, 0.0),
                jnp.where(mask2, value, 0.0),
                jnp.where(row1, local, 0.0),
                jnp.where(row2, local, 0.0),
            )
            sums = [s + rolled(p, EXT * low) for s, p in zip(sums, parts)]
        for out, value, local in ((first, sums[0], sums[2]), (second, sums[1], sums[3])):
            out[high * ORB : (high + 1) * ORB, :] = value
            out[2 * ORB + high : 2 * ORB + high + 1, :] = local
    for out in (first, second):
        out[2 * ORB + 2 :, :] = jnp.zeros((PAYLOAD - 2 * ORB - 2, LANES), jnp.float32)


def extend_kernel(flags, orbitals, second, first, field, edge_potential):
    mask1, mask2 = face_masks(flags, ORB)
    row1, row2 = face_masks(flags, 1)
    for cell in range(CELLS):
        field[cell * ORB : (cell + 1) * ORB, :] = orbitals[pl.ds(cell, ORB, stride=CELLS), :]
    for x in range(SIDE):
        total, total_potential = 0.0, 0.0
        for y in range(SIDE):
            high, low = divmod(x * SIDE + y, 8)

            def unpack(start, size, keep1, keep2):
                one = rolled(first[start : start + size, :], -EXT * low)
                two = rolled(second[start : start + size, :], -EXT * low)
                return rolled(jnp.where(keep2, one, 0.0) + jnp.where(keep1, two, 0.0), 2 * EXT * y)

            total = total + unpack(high * ORB, ORB, mask1, mask2)
            total_potential = total_potential + unpack(2 * ORB + high, 1, row1, row2)
        field[BLOCK + x * ORB : BLOCK + (x + 1) * ORB, :] = total
        edge_potential[x : x + 1, :] = total_potential


def edge_of(ref, x):
    return ref[x * ORB : (x + 1) * ORB, :]


def sides(is_above, get):
    layers = [get(i) for i in range(SIDE)]
    return [jnp.where(is_above, 0.0, v) for v in layers], [jnp.where(is_above, v, 0.0) for v in layers]


def block_kernel(scale, with_previous, flags, potential, field, *rest):
    previous = rest[0] if with_previous else None
    y2, x1, out = rest[-3:]
    lane = lane_index(ORB)
    weight = [-0.5 * scale * w for w in WEIGHTS]
    shift = MIDDLE + 1.5 * WEIGHTS[0]
    for y in range(SIDE):
        below, above = sides(flags[0] == 0, lambda x: rows_of(x1, x * SIDE + y))
        along = below + [rows_of(field, x * SIDE + y) for x in range(SIDE)] + above
        for x in range(SIDE):
            cell = x * SIDE + y
            here = along[SIDE + x]
            there = rolled(edge_of(field, CELLS + x), -2 * EXT * y)
            total = (potential[cell : cell + 1, :] - shift) * scale * here
            for k in range(1, 5):
                pairs = along[SIDE + x + k] + along[SIDE + x - k]
                pairs = pairs + rolled(jnp.where(lane < k, there, here), -k)
                pairs = pairs + rolled(jnp.where(lane >= LANES - k, there, here), k)
                total = total + weight[k] * pairs
            if with_previous:
                total = total - rows_of(previous, cell)
            out[cell * ORB : (cell + 1) * ORB, :] = total
    for x in range(SIDE):
        below, above = sides(flags[1] != 0, lambda y: rows_of(y2, x * SIDE + y))
        along = below + [rows_of(field, x * SIDE + y) for y in range(SIDE)] + above
        for y in range(SIDE):
            cell = x * SIDE + y
            total = rows_of(out, cell)
            for k in range(1, 5):
                total = total + weight[k] * (along[SIDE + y + k] + along[SIDE + y - k])
            out[cell * ORB : (cell + 1) * ORB, :] = total


def join_kernel(scale, with_previous, split, flags, edge_potential, part, field, y1, x2, y2, x1, *rest):
    previous = rest[0] if with_previous else None
    out = rest[-2] if split else rest[-1]
    lane = lane_index(ORB)
    place = lane % (2 * EXT)
    lane_y = ((lane + EXT) // (2 * EXT)) % SIDE
    inside = ((place < EXT) & (flags[4] != 0)) | ((place >= EXT) & (flags[3] != 0))
    window = (lane < EXT) | (lane >= LANES - EXT)
    even_x, even_y = flags[0] == 0, flags[1] == 0
    weight = [-0.5 * scale * w for w in WEIGHTS]
    shift = MIDDLE + 1.5 * WEIGHTS[0]

    def face_terms(below, above, i):
        terms = [weight[k] * above[i + k - SIDE] for k in range(SIDE - i, 5)]
        return sum(terms + [weight[k] * below[i - k + SIDE] for k in range(i + 1, 5)])

    for y in range(SIDE):
        below, above = sides(flags[0] != 0, lambda x: rows_of(x2, x * SIDE + y))
        for x in range(SIDE):
            cell = x * SIDE + y
            out[cell * ORB : (cell + 1) * ORB, :] = rows_of(part, cell) + face_terms(below, above, x)
    for x in range(SIDE):
        below, above = sides(even_y, lambda y: rows_of(y1, x * SIDE + y))
        for y in range(SIDE):
            cell = x * SIDE + y
            out[cell * ORB : (cell + 1) * ORB, :] = rows_of(out, cell) + face_terms(below, above, y)
    pairs = [(edge_of(x1, CELLS + x), edge_of(x2, CELLS + x)) for x in range(SIDE)]
    along = [jnp.where(even_x, b, a) for a, b in pairs]
    along = along + [edge_of(field, CELLS + x) for x in range(SIDE)] + [jnp.where(even_x, a, b) for a, b in pairs]
    for x in range(SIDE):
        here = along[SIDE + x]
        one, two = edge_of(y1, CELLS + x), edge_of(y2, CELLS + x)
        below, above = jnp.where(even_y, two, one), jnp.where(even_y, one, two)
        there = 0.0
        for y in range(SIDE):
            there = there + rolled(jnp.where(window, rows_of(field, x * SIDE + y), 0.0), 2 * EXT * y)
        total = (edge_potential[x : x + 1, :] - shift) * scale * here
        for k in range(1, 5):
            terms = along[SIDE + x + k] + along[SIDE + x - k]
            terms = terms + rolled(jnp.where(lane_y < k, above, here), -2 * EXT * k)
            terms = terms + rolled(jnp.where(lane_y >= SIDE - k, below, here), 2 * EXT * k)
            terms = terms + rolled(jnp.where(place < k, there, here), -k)
            terms = terms + rolled(jnp.where(place >= 2 * EXT - k, there, here), k)
            total = total + weight[k] * terms
        if with_previous:
            total = total - edge_of(previous, CELLS + x)
        total = jnp.where(inside, total, 0.0)
        if split:
            rest[-1][x * ORB : (x + 1) * ORB, :] = total
        else:
            out[BLOCK + x * ORB : BLOCK + (x + 1) * ORB, :] = total


def dot(a, b, contract):
    return lax.dot_general(
        a, b, ((contract[:1], contract[1:]), ((), ())), precision=lax.Precision.HIGHEST, preferred_element_type=jnp.float32
    )


def image_kernel(flags, potential, field, edge, out):
    lane = lane_index(ORB)
    up = flags[1] == 0
    weight = [-0.5 * w for w in WEIGHTS]
    for x in range(SIDE):
        for y in range(SIDE):
            cell = x * SIDE + y
            here, there = rows_of(field, cell), rolled(edge_of(edge, x), -2 * EXT * y)
            total = (0.5 * potential[cell : cell + 1, :] + 1.5 * weight[0]) * here
            above = sum([weight[k] * rows_of(field, cell + k * SIDE) for k in range(1, SIDE - x)], jnp.zeros_like(here))
            below = sum([weight[k] * rows_of(field, cell - k * SIDE) for k in range(1, x + 1)], jnp.zeros_like(here))
            total = total + jnp.where(up, above, below)
            for k in range(1, 5):
                pair = rolled(jnp.where(lane < k, there, here), -k)
                if y + k < SIDE:
                    pair = pair + rows_of(field, cell + k)
                total = total + weight[k] * pair
            out[cell * ORB : (cell + 1) * ORB, :] = total


def group_of(rows):
    return lax.broadcasted_iota(jnp.int32, (rows, LANES), 0) // 4


def sums_kernel(flags, part, field, after_y, beside_x, sums, wide):
    up = flags[1] == 0
    weight = [-0.5 * w for w in WEIGHTS]
    here_all, image_all = [], []
    for x in range(SIDE):
        for y in range(SIDE):
            cell = x * SIDE + y
            above = sum(weight[k] * rows_of(beside_x, cell + (k - SIDE) * SIDE) for k in range(SIDE - x, 5))
            below = sum(weight[k] * rows_of(beside_x, cell + (SIDE - k) * SIDE) for k in range(x + 1, 5))
            image = rows_of(part, cell) + jnp.where(up, above, below)
            image = image + sum(weight[k] * rows_of(after_y, cell + k - SIDE) for k in range(SIDE - y, 5))
            here_all.append(rows_of(field, cell))
            image_all.append(image)
    here = jnp.concatenate(here_all, axis=1)
    image = jnp.concatenate(image_all, axis=1)
    wide[...] = jnp.zeros_like(wide)
    wide[:, : 2 * ORB] = dot(here, jnp.concatenate([here, image], axis=0), (1, 1))
    value, group = wide[...], group_of(ORB)
    wide[...] = sum(jnp.where(group == g, rolled(value, 2 * ORB * g), 0.0) for g in range(4))
    sums[...] = (wide[0:4, :] + wide[4:8, :]) + (wide[8:12, :] + wide[12:16, :])


def finish_kernel(cell_total, sums, field, q_block, ritz, wide):
    for g in range(4):
        wide[4 * g : 4 * g + 4, :] = sums[...]
    value, group = wide[...], group_of(ORB)
    sums = sum(jnp.where(group == g, rolled(value, -2 * ORB * g), 0.0) for g in range(4)) * (1.0 / cell_total)
    row = lax.broadcasted_iota(jnp.int32, (ORB, LANES), 0)
    lane = lane_index(ORB)
    work = jnp.where(lane < ORB, sums, jnp.where(lane == row + ORB, 1.0, 0.0))
    for k in range(ORB - 1):
        pivot = work[k : k + 1, :]
        factor = work[:, k : k + 1] / pivot[:, k : k + 1]
        work = work - jnp.where(row > k, factor, 0.0) * pivot
    diagonal = jnp.sum(jnp.where(lane == row, work, 0.0), axis=1, keepdims=True)
    inverse = (work * (1.0 / jnp.sqrt(diagonal)))[:, ORB : 2 * ORB]
    half = sums[:, ORB : 2 * ORB]
    part = dot(dot(inverse, half, (1, 0)), inverse, (1, 1))
    ritz[...] = part + part.T
    for cell in range(CELLS):
        q_block[pl.ds(cell, ORB, stride=CELLS), :] = dot(inverse, rows_of(field, cell), (1, 0))


def swap(value, axis, first):
    pairs = []
    for i in range(first, lax.axis_size(axis) - 1, 2):
        pairs += [(i, i + 1), (i + 1, i)]
    return lax.ppermute(value, axis, pairs)


def swap_x(value, turn):
    deep, wide = lax.axis_size("gx"), lax.axis_size("gy")
    pairs = []
    for j in range(wide):
        for i in range((turn + j) % 2, deep - 1, 2):
            pairs += [(i * wide + j, (i + 1) * wide + j), ((i + 1) * wide + j, i * wide + j)]
    return lax.ppermute(value, ("gx", "gy"), pairs)


def one_side_x(value):
    deep, wide = lax.axis_size("gx"), lax.axis_size("gy")
    pairs = []
    for j in range(wide):
        for i in range(deep - 1):
            low, high = i * wide + j, (i + 1) * wide + j
            pairs.append((low, high) if j % 2 else (high, low))
    return lax.ppermute(value, ("gx", "gy"), pairs)


def from_above(value, axis):
    return lax.ppermute(value, axis, [(i + 1, i) for i in range(lax.axis_size(axis) - 1)])


def sum_everywhere(value):
    if all(lax.axis_size(axis) == 8 for axis in ("gx", "gy", "gz")):
        fours = [[0, 1, 2, 3], [4, 5, 6, 7]]
        value = value + lax.ppermute(value, "gy", [(i, i ^ 1) for i in range(8)])
        value = lax.psum(value, "gy", axis_index_groups=[[0, 2, 4, 6], [1, 3, 5, 7]])
        value = lax.psum(value, "gz", axis_index_groups=fours)
        value = lax.psum(value, "gx", axis_index_groups=fours)
        rings = [[8 * gx + gz, 8 * gx + 32 + gz, 8 * gx + gz + 4, 8 * gx + 32 + gz + 4] for gx in range(4) for gz in range(4)]
        return lax.psum(value, ("gx", "gz"), axis_index_groups=rings)
    return lax.psum(value, ("gx", "gy", "gz"))


def call(kernel, outs, smem=True, scratch=()):
    def run(*operands):
        specs = [pl.BlockSpec(memory_space=pltpu.VMEM)] * len(operands)
        if smem:
            specs[0] = pl.BlockSpec(memory_space=pltpu.SMEM)
        return pl.pallas_call(
            kernel,
            out_shape=[jax.ShapeDtypeStruct(shape, jnp.float32) for shape in outs],
            in_specs=specs,
            out_specs=[pl.BlockSpec(memory_space=pltpu.VMEM)] * len(outs),
            scratch_shapes=[pltpu.VMEM(shape, jnp.float32) for shape in scratch],
            compiler_params=pltpu.CompilerParams(vmem_limit_bytes=8 * 1024 * 1024),
        )(*operands)

    return run


def body(orbitals, potential):
    at = [lax.axis_index(axis) for axis in ("gx", "gy", "gz")]
    cell_total = orbitals[0].size * lax.axis_size("gx") * lax.axis_size("gy") * lax.axis_size("gz")
    flags = jnp.stack(
        [(at[0] + at[1]) % 2, at[1] % 2, at[2] % 2, (at[2] > 0).astype(jnp.int32), (at[2] < lax.axis_size("gz") - 1).astype(jnp.int32)]
    ).astype(jnp.int32)
    shape = orbitals.shape
    orbitals = orbitals.reshape(BLOCK, LANES)
    potential = potential.reshape(CELLS, LANES)
    block, edge, sent = (BLOCK, LANES), (EDGE, LANES), (BLOCK + EDGE, LANES)

    first, second = call(payload_kernel, ((PAYLOAD, LANES),) * 2)(flags, orbitals, potential)
    second, first = swap(second, "gz", 1), swap(first, "gz", 0)
    field, edge_potential = call(extend_kernel, (sent, (8, LANES)))(flags, orbitals, second, first)

    def advance(field, scale, previous, split):
        y2, y1, x2, x1 = swap(field, "gy", 1), swap(field, "gy", 0), swap_x(field, 1), swap_x(field, 0)
        kernel = functools.partial(block_kernel, scale, bool(previous))
        (part,) = call(kernel, (block,))(flags, potential, field, *previous, y2, x1)
        kernel = functools.partial(join_kernel, scale, bool(previous), split)
        outs = (block, edge) if split else (sent,)
        return call(kernel, outs)(flags, edge_potential, part, field, y1, x2, y2, x1, *previous)

    (field1,) = advance(field, 1.0 / HALF, (), False)
    (field2,) = advance(field1, 2.0 / HALF, (field,), False)
    field, edge = advance(field2, 2.0 / HALF, (field1,), True)
    after_y, beside_x = from_above(field, "gy"), one_side_x(field)
    (part,) = call(image_kernel, (block,))(flags, potential, field, edge)
    wide = (ORB, LANES)
    (sums,) = call(sums_kernel, ((4, LANES),), scratch=(wide,))(flags, part, field, after_y, beside_x)
    sums = sum_everywhere(sums)
    q_block, ritz = call(functools.partial(finish_kernel, cell_total), (block, (ORB, ORB)), False, (wide,))(sums, field)
    return q_block.reshape(shape), ritz


def solution(mesh):
    placed = (P(None, "gx", "gy", "gz"), P("gx", "gy", "gz"))
    return jax.shard_map(
        body,
        mesh=mesh,
        in_specs=placed,
        out_specs=(P(None, "gx", "gy", "gz"), P()),
        check_vma=False,
    )
```

```python
import functools

import jax
import jax.numpy as jnp
from jax import lax
from jax.experimental import pallas as pl
from jax.experimental.pallas import tpu as pltpu
from jax.sharding import PartitionSpec as P

WEIGHTS = (-205.0 / 72.0, 8.0 / 5.0, -1.0 / 5.0, 8.0 / 315.0, -1.0 / 560.0)
HALF = (12.0 - 1.5) / 2.0
MIDDLE = (12.0 + 1.5) / 2.0
ORB = 16
SIDE = 4
CELLS = SIDE * SIDE
LANES = 128
EXT = 16
BLOCK = CELLS * ORB
EDGE = SIDE * ORB
PAYLOAD = 2 * ORB + 8


def lane_index(rows):
    return lax.broadcasted_iota(jnp.int32, (rows, LANES), 1)


def rolled(value, amount):
    amount %= LANES
    return pltpu.roll(value, amount, 1) if amount else value


def rows_of(ref, cell):
    return ref[cell * ORB : (cell + 1) * ORB, :]


def face_masks(flags, rows):
    lane = lane_index(rows)
    even = flags[2] == 0
    upper = jnp.where(even, LANES - EXT, 0)
    lower = jnp.where(even, 0, LANES - EXT)
    first = (lane >= upper) & (lane < upper + EXT)
    second = (lane >= lower) & (lane < lower + EXT)
    return first, second


def payload_kernel(flags, orbitals, potential, first, second):
    mask1, mask2 = face_masks(flags, ORB)
    row1, row2 = face_masks(flags, 1)
    for high in range(2):
        sums = [jnp.zeros((ORB, LANES), jnp.float32)] * 2 + [jnp.zeros((1, LANES), jnp.float32)] * 2
        for low in range(8):
            cell = 8 * high + low
            value = orbitals[pl.ds(cell, ORB, stride=CELLS), :]
            local = potential[cell : cell + 1, :]
            parts = (
                jnp.where(mask1, value, 0.0),
                jnp.where(mask2, value, 0.0),
                jnp.where(row1, local, 0.0),
                jnp.where(row2, local, 0.0),
            )
            sums = [s + rolled(p, EXT * low) for s, p in zip(sums, parts)]
        for out, value, local in ((first, sums[0], sums[2]), (second, sums[1], sums[3])):
            out[high * ORB : (high + 1) * ORB, :] = value
            out[2 * ORB + high : 2 * ORB + high + 1, :] = local
    for out in (first, second):
        out[2 * ORB + 2 :, :] = jnp.zeros((PAYLOAD - 2 * ORB - 2, LANES), jnp.float32)


def extend_kernel(flags, orbitals, second, first, field, edge_potential):
    mask1, mask2 = face_masks(flags, ORB)
    row1, row2 = face_masks(flags, 1)
    for cell in range(CELLS):
        field[cell * ORB : (cell + 1) * ORB, :] = orbitals[pl.ds(cell, ORB, stride=CELLS), :]
    for x in range(SIDE):
        total, total_potential = 0.0, 0.0
        for y in range(SIDE):
            high, low = divmod(x * SIDE + y, 8)

            def unpack(start, size, keep1, keep2):
                one = rolled(first[start : start + size, :], -EXT * low)
                two = rolled(second[start : start + size, :], -EXT * low)
                return rolled(jnp.where(keep2, one, 0.0) + jnp.where(keep1, two, 0.0), 2 * EXT * y)

            total = total + unpack(high * ORB, ORB, mask1, mask2)
            total_potential = total_potential + unpack(2 * ORB + high, 1, row1, row2)
        field[BLOCK + x * ORB : BLOCK + (x + 1) * ORB, :] = total
        edge_potential[x : x + 1, :] = total_potential


def edge_of(ref, x):
    return ref[x * ORB : (x + 1) * ORB, :]


def sides(is_above, get):
    layers = [get(i) for i in range(SIDE)]
    return [jnp.where(is_above, 0.0, v) for v in layers], [jnp.where(is_above, v, 0.0) for v in layers]


def block_kernel(scale, with_previous, flags, potential, field, *rest):
    previous = rest[0] if with_previous else None
    y2, x1, out = rest[-3:]
    lane = lane_index(ORB)
    weight = [-0.5 * scale * w for w in WEIGHTS]
    shift = MIDDLE + 1.5 * WEIGHTS[0]
    for y in range(SIDE):
        below, above = sides(flags[0] == 0, lambda x: rows_of(x1, x * SIDE + y))
        along = below + [rows_of(field, x * SIDE + y) for x in range(SIDE)] + above
        for x in range(SIDE):
            cell = x * SIDE + y
            here = along[SIDE + x]
            there = rolled(edge_of(field, CELLS + x), -2 * EXT * y)
            total = (potential[cell : cell + 1, :] - shift) * scale * here
            for k in range(1, 5):
                pairs = along[SIDE + x + k] + along[SIDE + x - k]
                pairs = pairs + rolled(jnp.where(lane < k, there, here), -k)
                pairs = pairs + rolled(jnp.where(lane >= LANES - k, there, here), k)
                total = total + weight[k] * pairs
            if with_previous:
                total = total - rows_of(previous, cell)
            out[cell * ORB : (cell + 1) * ORB, :] = total
    for x in range(SIDE):
        below, above = sides(flags[1] != 0, lambda y: rows_of(y2, x * SIDE + y))
        along = below + [rows_of(field, x * SIDE + y) for y in range(SIDE)] + above
        for y in range(SIDE):
            cell = x * SIDE + y
            total = rows_of(out, cell)
            for k in range(1, 5):
                total = total + weight[k] * (along[SIDE + y + k] + along[SIDE + y - k])
            out[cell * ORB : (cell + 1) * ORB, :] = total


def join_kernel(scale, with_previous, split, flags, edge_potential, part, field, y1, x2, y2, x1, *rest):
    previous = rest[0] if with_previous else None
    out = rest[-2] if split else rest[-1]
    lane = lane_index(ORB)
    place = lane % (2 * EXT)
    lane_y = ((lane + EXT) // (2 * EXT)) % SIDE
    inside = ((place < EXT) & (flags[4] != 0)) | ((place >= EXT) & (flags[3] != 0))
    window = (lane < EXT) | (lane >= LANES - EXT)
    even_x, even_y = flags[0] == 0, flags[1] == 0
    weight = [-0.5 * scale * w for w in WEIGHTS]
    shift = MIDDLE + 1.5 * WEIGHTS[0]

    def face_terms(below, above, i):
        terms = [weight[k] * above[i + k - SIDE] for k in range(SIDE - i, 5)]
        return sum(terms + [weight[k] * below[i - k + SIDE] for k in range(i + 1, 5)])

    for y in range(SIDE):
        below, above = sides(flags[0] != 0, lambda x: rows_of(x2, x * SIDE + y))
        for x in range(SIDE):
            cell = x * SIDE + y
            out[cell * ORB : (cell + 1) * ORB, :] = rows_of(part, cell) + face_terms(below, above, x)
    for x in range(SIDE):
        below, above = sides(even_y, lambda y: rows_of(y1, x * SIDE + y))
        for y in range(SIDE):
            cell = x * SIDE + y
            out[cell * ORB : (cell + 1) * ORB, :] = rows_of(out, cell) + face_terms(below, above, y)
    pairs = [(edge_of(x1, CELLS + x), edge_of(x2, CELLS + x)) for x in range(SIDE)]
    along = [jnp.where(even_x, b, a) for a, b in pairs]
    along = along + [edge_of(field, CELLS + x) for x in range(SIDE)] + [jnp.where(even_x, a, b) for a, b in pairs]
    for x in range(SIDE):
        here = along[SIDE + x]
        one, two = edge_of(y1, CELLS + x), edge_of(y2, CELLS + x)
        below, above = jnp.where(even_y, two, one), jnp.where(even_y, one, two)
        there = 0.0
        for y in range(SIDE):
            there = there + rolled(jnp.where(window, rows_of(field, x * SIDE + y), 0.0), 2 * EXT * y)
        total = (edge_potential[x : x + 1, :] - shift) * scale * here
        for k in range(1, 5):
            terms = along[SIDE + x + k] + along[SIDE + x - k]
            terms = terms + rolled(jnp.where(lane_y < k, above, here), -2 * EXT * k)
            terms = terms + rolled(jnp.where(lane_y >= SIDE - k, below, here), 2 * EXT * k)
            terms = terms + rolled(jnp.where(place < k, there, here), -k)
            terms = terms + rolled(jnp.where(place >= 2 * EXT - k, there, here), k)
            total = total + weight[k] * terms
        if with_previous:
            total = total - edge_of(previous, CELLS + x)
        total = jnp.where(inside, total, 0.0)
        if split:
            rest[-1][x * ORB : (x + 1) * ORB, :] = total
        else:
            out[BLOCK + x * ORB : BLOCK + (x + 1) * ORB, :] = total


def dot(a, b, contract):
    return lax.dot_general(
        a, b, ((contract[:1], contract[1:]), ((), ())), precision=lax.Precision.HIGHEST, preferred_element_type=jnp.float32
    )


def image_kernel(flags, potential, field, edge, out):
    lane = lane_index(ORB)
    up = flags[1] == 0
    weight = [-0.5 * w for w in WEIGHTS]
    for x in range(SIDE):
        for y in range(SIDE):
            cell = x * SIDE + y
            here, there = rows_of(field, cell), rolled(edge_of(edge, x), -2 * EXT * y)
            total = (0.5 * potential[cell : cell + 1, :] + 1.5 * weight[0]) * here
            above = sum([weight[k] * rows_of(field, cell + k * SIDE) for k in range(1, SIDE - x)], jnp.zeros_like(here))
            below = sum([weight[k] * rows_of(field, cell - k * SIDE) for k in range(1, x + 1)], jnp.zeros_like(here))
            total = total + jnp.where(up, above, below)
            for k in range(1, 5):
                pair = rolled(jnp.where(lane < k, there, here), -k)
                if y + k < SIDE:
                    pair = pair + rows_of(field, cell + k)
                total = total + weight[k] * pair
            out[cell * ORB : (cell + 1) * ORB, :] = total


def group_of(rows):
    return lax.broadcasted_iota(jnp.int32, (rows, LANES), 0) // 4


def sums_kernel(flags, part, field, after_y, beside_x, sums, wide):
    up = flags[1] == 0
    weight = [-0.5 * w for w in WEIGHTS]
    here_all, image_all = [], []
    for x in range(SIDE):
        for y in range(SIDE):
            cell = x * SIDE + y
            above = sum(weight[k] * rows_of(beside_x, cell + (k - SIDE) * SIDE) for k in range(SIDE - x, 5))
            below = sum(weight[k] * rows_of(beside_x, cell + (SIDE - k) * SIDE) for k in range(x + 1, 5))
            image = rows_of(part, cell) + jnp.where(up, above, below)
            image = image + sum(weight[k] * rows_of(after_y, cell + k - SIDE) for k in range(SIDE - y, 5))
            here_all.append(rows_of(field, cell))
            image_all.append(image)
    here = jnp.concatenate(here_all, axis=1)
    image = jnp.concatenate(image_all, axis=1)
    wide[...] = jnp.zeros_like(wide)
    wide[:, : 2 * ORB] = dot(here, jnp.concatenate([here, image], axis=0), (1, 1))
    value, group = wide[...], group_of(ORB)
    wide[...] = sum(jnp.where(group == g, rolled(value, 2 * ORB * g), 0.0) for g in range(4))
    sums[...] = (wide[0:4, :] + wide[4:8, :]) + (wide[8:12, :] + wide[12:16, :])


def finish_kernel(cell_total, sums, field, q_block, ritz, wide):
    for g in range(4):
        wide[4 * g : 4 * g + 4, :] = sums[...]
    value, group = wide[...], group_of(ORB)
    sums = sum(jnp.where(group == g, rolled(value, -2 * ORB * g), 0.0) for g in range(4)) * (1.0 / cell_total)
    row = lax.broadcasted_iota(jnp.int32, (ORB, LANES), 0)
    lane = lane_index(ORB)
    work = jnp.where(lane < ORB, sums, jnp.where(lane == row + ORB, 1.0, 0.0))
    for k in range(ORB - 1):
        pivot = work[k : k + 1, :]
        factor = work[:, k : k + 1] / pivot[:, k : k + 1]
        work = work - jnp.where(row > k, factor, 0.0) * pivot
    diagonal = jnp.sum(jnp.where(lane == row, work, 0.0), axis=1, keepdims=True)
    inverse = (work * (1.0 / jnp.sqrt(diagonal)))[:, ORB : 2 * ORB]
    half = sums[:, ORB : 2 * ORB]
    part = dot(dot(inverse, half, (1, 0)), inverse, (1, 1))
    ritz[...] = part + part.T
    for cell in range(CELLS):
        q_block[pl.ds(cell, ORB, stride=CELLS), :] = dot(inverse, rows_of(field, cell), (1, 0))


def swap(value, axis, first):
    pairs = []
    for i in range(first, lax.axis_size(axis) - 1, 2):
        pairs += [(i, i + 1), (i + 1, i)]
    return lax.ppermute(value, axis, pairs)


def swap_x(value, turn):
    deep, wide = lax.axis_size("gx"), lax.axis_size("gy")
    pairs = []
    for j in range(wide):
        for i in range((turn + j) % 2, deep - 1, 2):
            pairs += [(i * wide + j, (i + 1) * wide + j), ((i + 1) * wide + j, i * wide + j)]
    return lax.ppermute(value, ("gx", "gy"), pairs)


def one_side_x(value):
    deep, wide = lax.axis_size("gx"), lax.axis_size("gy")
    pairs = []
    for j in range(wide):
        for i in range(deep - 1):
            low, high = i * wide + j, (i + 1) * wide + j
            pairs.append((low, high) if j % 2 else (high, low))
    return lax.ppermute(value, ("gx", "gy"), pairs)


def from_above(value, axis):
    return lax.ppermute(value, axis, [(i + 1, i) for i in range(lax.axis_size(axis) - 1)])


def ring_groups(odd_core, stage):
    at = lambda gx, gy, gz: (gx * 8 + gy) * 8 + gz
    four, eight, cores = range(4), range(8), range(odd_core, 8, 2)
    if stage == "y":
        return [[at(gx, 2 * i + odd_core, gz) for i in four] for gx in eight for gz in eight]
    if stage == "x":
        return [[at(gx, gy, 4 * h + i) for i in four] for gx in eight for gy in cores for h in range(2)]
    if stage == "z":
        return [[at(4 * h + i, gy, gz) for i in four] for gy in cores for gz in eight for h in range(2)]
    return [[at(gx + 4 * j, gy, gz + 4 * h) for h in range(2) for j in range(2)] for gx in four for gy in cores for gz in four]


def sum_everywhere(value):
    axes = ("gx", "gy", "gz")
    if all(lax.axis_size(axis) == 8 for axis in axes):
        value = value + lax.ppermute(value, "gy", [(i, i ^ 1) for i in range(8)])
        for stages in (("y", "x"), ("x", "y"), ("z", "apart"), ("apart", "z")):
            groups = [group for core in range(2) for group in ring_groups(core, stages[core])]
            value = lax.psum(value, axes, axis_index_groups=groups)
        return value
    return lax.psum(value, axes)


def call(kernel, outs, smem=True, scratch=()):
    def run(*operands):
        specs = [pl.BlockSpec(memory_space=pltpu.VMEM)] * len(operands)
        if smem:
            specs[0] = pl.BlockSpec(memory_space=pltpu.SMEM)
        return pl.pallas_call(
            kernel,
            out_shape=[jax.ShapeDtypeStruct(shape, jnp.float32) for shape in outs],
            in_specs=specs,
            out_specs=[pl.BlockSpec(memory_space=pltpu.VMEM)] * len(outs),
            scratch_shapes=[pltpu.VMEM(shape, jnp.float32) for shape in scratch],
            compiler_params=pltpu.CompilerParams(vmem_limit_bytes=8 * 1024 * 1024),
        )(*operands)

    return run


def body(orbitals, potential):
    at = [lax.axis_index(axis) for axis in ("gx", "gy", "gz")]
    cell_total = orbitals[0].size * lax.axis_size("gx") * lax.axis_size("gy") * lax.axis_size("gz")
    flags = jnp.stack(
        [(at[0] + at[1]) % 2, at[1] % 2, at[2] % 2, (at[2] > 0).astype(jnp.int32), (at[2] < lax.axis_size("gz") - 1).astype(jnp.int32)]
    ).astype(jnp.int32)
    shape = orbitals.shape
    orbitals = orbitals.reshape(BLOCK, LANES)
    potential = potential.reshape(CELLS, LANES)
    block, edge, sent = (BLOCK, LANES), (EDGE, LANES), (BLOCK + EDGE, LANES)

    first, second = call(payload_kernel, ((PAYLOAD, LANES),) * 2)(flags, orbitals, potential)
    second, first = swap(second, "gz", 1), swap(first, "gz", 0)
    field, edge_potential = call(extend_kernel, (sent, (8, LANES)))(flags, orbitals, second, first)

    def advance(field, scale, previous, split):
        y2, y1, x2, x1 = swap(field, "gy", 1), swap(field, "gy", 0), swap_x(field, 1), swap_x(field, 0)
        kernel = functools.partial(block_kernel, scale, bool(previous))
        (part,) = call(kernel, (block,))(flags, potential, field, *previous, y2, x1)
        kernel = functools.partial(join_kernel, scale, bool(previous), split)
        outs = (block, edge) if split else (sent,)
        return call(kernel, outs)(flags, edge_potential, part, field, y1, x2, y2, x1, *previous)

    (field1,) = advance(field, 1.0 / HALF, (), False)
    (field2,) = advance(field1, 2.0 / HALF, (field,), False)
    field, edge = advance(field2, 2.0 / HALF, (field1,), True)
    after_y, beside_x = from_above(field, "gy"), one_side_x(field)
    (part,) = call(image_kernel, (block,))(flags, potential, field, edge)
    wide = (ORB, LANES)
    (sums,) = call(sums_kernel, ((4, LANES),), scratch=(wide,))(flags, part, field, after_y, beside_x)
    sums = sum_everywhere(sums)
    q_block, ritz = call(functools.partial(finish_kernel, cell_total), (block, (ORB, ORB)), False, (wide,))(sums, field)
    return q_block.reshape(shape), ritz


def solution(mesh):
    placed = (P(None, "gx", "gy", "gz"), P("gx", "gy", "gz"))
    return jax.shard_map(
        body,
        mesh=mesh,
        in_specs=placed,
        out_specs=(P(None, "gx", "gy", "gz"), P()),
        check_vma=False,
    )
```

```python
import functools

import jax
import jax.numpy as jnp
from jax import lax
from jax.experimental import pallas as pl
from jax.experimental.pallas import tpu as pltpu
from jax.sharding import PartitionSpec as P

WEIGHTS = (-205.0 / 72.0, 8.0 / 5.0, -1.0 / 5.0, 8.0 / 315.0, -1.0 / 560.0)
HALF = (12.0 - 1.5) / 2.0
MIDDLE = (12.0 + 1.5) / 2.0
ORB = 16
SIDE = 4
CELLS = SIDE * SIDE
LANES = 128
EXT = 16
BLOCK = CELLS * ORB
EDGE = SIDE * ORB
PAYLOAD = 2 * ORB + 8


def lane_index(rows):
    return lax.broadcasted_iota(jnp.int32, (rows, LANES), 1)


def rolled(value, amount):
    amount %= LANES
    return pltpu.roll(value, amount, 1) if amount else value


def rows_of(ref, cell):
    return ref[cell * ORB : (cell + 1) * ORB, :]


def face_masks(flags, rows):
    lane = lane_index(rows)
    even = flags[2] == 0
    upper = jnp.where(even, LANES - EXT, 0)
    lower = jnp.where(even, 0, LANES - EXT)
    first = (lane >= upper) & (lane < upper + EXT)
    second = (lane >= lower) & (lane < lower + EXT)
    return first, second


def payload_kernel(flags, orbitals, potential, first, second):
    mask1, mask2 = face_masks(flags, ORB)
    row1, row2 = face_masks(flags, 1)
    for high in range(2):
        sums = [jnp.zeros((ORB, LANES), jnp.float32)] * 2 + [jnp.zeros((1, LANES), jnp.float32)] * 2
        for low in range(8):
            cell = 8 * high + low
            value = orbitals[pl.ds(cell, ORB, stride=CELLS), :]
            local = potential[cell : cell + 1, :]
            parts = (
                jnp.where(mask1, value, 0.0),
                jnp.where(mask2, value, 0.0),
                jnp.where(row1, local, 0.0),
                jnp.where(row2, local, 0.0),
            )
            sums = [s + rolled(p, EXT * low) for s, p in zip(sums, parts)]
        for out, value, local in ((first, sums[0], sums[2]), (second, sums[1], sums[3])):
            out[high * ORB : (high + 1) * ORB, :] = value
            out[2 * ORB + high : 2 * ORB + high + 1, :] = local
    for out in (first, second):
        out[2 * ORB + 2 :, :] = jnp.zeros((PAYLOAD - 2 * ORB - 2, LANES), jnp.float32)


def extend_kernel(flags, orbitals, second, first, field, edge_potential):
    mask1, mask2 = face_masks(flags, ORB)
    row1, row2 = face_masks(flags, 1)
    for cell in range(CELLS):
        field[cell * ORB : (cell + 1) * ORB, :] = orbitals[pl.ds(cell, ORB, stride=CELLS), :]
    for x in range(SIDE):
        total, total_potential = 0.0, 0.0
        for y in range(SIDE):
            high, low = divmod(x * SIDE + y, 8)

            def unpack(start, size, keep1, keep2):
                one = rolled(first[start : start + size, :], -EXT * low)
                two = rolled(second[start : start + size, :], -EXT * low)
                return rolled(jnp.where(keep2, one, 0.0) + jnp.where(keep1, two, 0.0), 2 * EXT * y)

            total = total + unpack(high * ORB, ORB, mask1, mask2)
            total_potential = total_potential + unpack(2 * ORB + high, 1, row1, row2)
        field[BLOCK + x * ORB : BLOCK + (x + 1) * ORB, :] = total
        edge_potential[x : x + 1, :] = total_potential


def edge_of(ref, x):
    return ref[x * ORB : (x + 1) * ORB, :]


def sides(is_above, get):
    layers = [get(i) for i in range(SIDE)]
    return [jnp.where(is_above, 0.0, v) for v in layers], [jnp.where(is_above, v, 0.0) for v in layers]


def block_kernel(scale, with_previous, flags, potential, field, *rest):
    previous = rest[0] if with_previous else None
    x1, y2, out = rest[-3:]
    lane = lane_index(ORB)
    weight = [-0.5 * scale * w for w in WEIGHTS]
    shift = MIDDLE + 1.5 * WEIGHTS[0]
    for y in range(SIDE):
        below, above = sides(flags[0] == 0, lambda x: rows_of(x1, x * SIDE + y))
        along = below + [rows_of(field, x * SIDE + y) for x in range(SIDE)] + above
        for x in range(SIDE):
            cell = x * SIDE + y
            here = along[SIDE + x]
            there = rolled(edge_of(field, CELLS + x), -2 * EXT * y)
            total = (potential[cell : cell + 1, :] - shift) * scale * here
            for k in range(1, 5):
                pairs = along[SIDE + x + k] + along[SIDE + x - k]
                pairs = pairs + rolled(jnp.where(lane < k, there, here), -k)
                pairs = pairs + rolled(jnp.where(lane >= LANES - k, there, here), k)
                total = total + weight[k] * pairs
            if with_previous:
                total = total - rows_of(previous, cell)
            out[cell * ORB : (cell + 1) * ORB, :] = total
    for x in range(SIDE):
        below, above = sides(flags[1] != 0, lambda y: rows_of(y2, x * SIDE + y))
        along = below + [rows_of(field, x * SIDE + y) for y in range(SIDE)] + above
        for y in range(SIDE):
            cell = x * SIDE + y
            total = rows_of(out, cell)
            for k in range(1, 5):
                total = total + weight[k] * (along[SIDE + y + k] + along[SIDE + y - k])
            out[cell * ORB : (cell + 1) * ORB, :] = total


def join_kernel(scale, with_previous, split, flags, edge_potential, part, field, y1, x2, x1, y2, *rest):
    previous = rest[0] if with_previous else None
    out = rest[-2] if split else rest[-1]
    lane = lane_index(ORB)
    place = lane % (2 * EXT)
    lane_y = ((lane + EXT) // (2 * EXT)) % SIDE
    inside = ((place < EXT) & (flags[4] != 0)) | ((place >= EXT) & (flags[3] != 0))
    window = (lane < EXT) | (lane >= LANES - EXT)
    even_x, even_y = flags[0] == 0, flags[1] == 0
    weight = [-0.5 * scale * w for w in WEIGHTS]
    shift = MIDDLE + 1.5 * WEIGHTS[0]

    def face_terms(below, above, i):
        terms = [weight[k] * above[i + k - SIDE] for k in range(SIDE - i, 5)]
        return sum(terms + [weight[k] * below[i - k + SIDE] for k in range(i + 1, 5)])

    for y in range(SIDE):
        below, above = sides(flags[0] != 0, lambda x: rows_of(x2, x * SIDE + y))
        for x in range(SIDE):
            cell = x * SIDE + y
            out[cell * ORB : (cell + 1) * ORB, :] = rows_of(part, cell) + face_terms(below, above, x)
    for x in range(SIDE):
        below, above = sides(even_y, lambda y: rows_of(y1, x * SIDE + y))
        for y in range(SIDE):
            cell = x * SIDE + y
            out[cell * ORB : (cell + 1) * ORB, :] = rows_of(out, cell) + face_terms(below, above, y)
    pairs = [(edge_of(x1, CELLS + x), edge_of(x2, CELLS + x)) for x in range(SIDE)]
    along = [jnp.where(even_x, b, a) for a, b in pairs]
    along = along + [edge_of(field, CELLS + x) for x in range(SIDE)] + [jnp.where(even_x, a, b) for a, b in pairs]
    for x in range(SIDE):
        here = along[SIDE + x]
        one, two = edge_of(y1, CELLS + x), edge_of(y2, CELLS + x)
        below, above = jnp.where(even_y, two, one), jnp.where(even_y, one, two)
        there = 0.0
        for y in range(SIDE):
            there = there + rolled(jnp.where(window, rows_of(field, x * SIDE + y), 0.0), 2 * EXT * y)
        total = (edge_potential[x : x + 1, :] - shift) * scale * here
        for k in range(1, 5):
            terms = along[SIDE + x + k] + along[SIDE + x - k]
            terms = terms + rolled(jnp.where(lane_y < k, above, here), -2 * EXT * k)
            terms = terms + rolled(jnp.where(lane_y >= SIDE - k, below, here), 2 * EXT * k)
            terms = terms + rolled(jnp.where(place < k, there, here), -k)
            terms = terms + rolled(jnp.where(place >= 2 * EXT - k, there, here), k)
            total = total + weight[k] * terms
        if with_previous:
            total = total - edge_of(previous, CELLS + x)
        total = jnp.where(inside, total, 0.0)
        if split:
            rest[-1][x * ORB : (x + 1) * ORB, :] = total
        else:
            out[BLOCK + x * ORB : BLOCK + (x + 1) * ORB, :] = total


def dot(a, b, contract):
    return lax.dot_general(
        a, b, ((contract[:1], contract[1:]), ((), ())), precision=lax.Precision.HIGHEST, preferred_element_type=jnp.float32
    )


def image_kernel(flags, potential, field, edge, out):
    lane = lane_index(ORB)
    up = flags[1] == 0
    weight = [-0.5 * w for w in WEIGHTS]
    for x in range(SIDE):
        for y in range(SIDE):
            cell = x * SIDE + y
            here, there = rows_of(field, cell), rolled(edge_of(edge, x), -2 * EXT * y)
            total = (0.5 * potential[cell : cell + 1, :] + 1.5 * weight[0]) * here
            above = sum([weight[k] * rows_of(field, cell + k * SIDE) for k in range(1, SIDE - x)], jnp.zeros_like(here))
            below = sum([weight[k] * rows_of(field, cell - k * SIDE) for k in range(1, x + 1)], jnp.zeros_like(here))
            total = total + jnp.where(up, above, below)
            for k in range(1, 5):
                pair = rolled(jnp.where(lane < k, there, here), -k)
                if y + k < SIDE:
                    pair = pair + rows_of(field, cell + k)
                total = total + weight[k] * pair
            out[cell * ORB : (cell + 1) * ORB, :] = total


def group_of(rows):
    return lax.broadcasted_iota(jnp.int32, (rows, LANES), 0) // 4


def sums_kernel(flags, part, field, after_y, beside_x, sums, wide):
    up = flags[1] == 0
    weight = [-0.5 * w for w in WEIGHTS]
    here_all, image_all = [], []
    for x in range(SIDE):
        for y in range(SIDE):
            cell = x * SIDE + y
            above = sum(weight[k] * rows_of(beside_x, cell + (k - SIDE) * SIDE) for k in range(SIDE - x, 5))
            below = sum(weight[k] * rows_of(beside_x, cell + (SIDE - k) * SIDE) for k in range(x + 1, 5))
            image = rows_of(part, cell) + jnp.where(up, above, below)
            image = image + sum(weight[k] * rows_of(after_y, cell + k - SIDE) for k in range(SIDE - y, 5))
            here_all.append(rows_of(field, cell))
            image_all.append(image)
    here = jnp.concatenate(here_all, axis=1)
    image = jnp.concatenate(image_all, axis=1)
    wide[...] = jnp.zeros_like(wide)
    wide[:, : 2 * ORB] = dot(here, jnp.concatenate([here, image], axis=0), (1, 1))
    value, group = wide[...], group_of(ORB)
    wide[...] = sum(jnp.where(group == g, rolled(value, 2 * ORB * g), 0.0) for g in range(4))
    sums[...] = (wide[0:4, :] + wide[4:8, :]) + (wide[8:12, :] + wide[12:16, :])


def finish_kernel(cell_total, sums, field, q_block, ritz, wide):
    for g in range(4):
        wide[4 * g : 4 * g + 4, :] = sums[...]
    value, group = wide[...], group_of(ORB)
    sums = sum(jnp.where(group == g, rolled(value, -2 * ORB * g), 0.0) for g in range(4)) * (1.0 / cell_total)
    row = lax.broadcasted_iota(jnp.int32, (ORB, LANES), 0)
    lane = lane_index(ORB)
    work = jnp.where(lane < ORB, sums, jnp.where(lane == row + ORB, 1.0, 0.0))
    for k in range(ORB - 1):
        pivot = work[k : k + 1, :]
        factor = work[:, k : k + 1] / pivot[:, k : k + 1]
        work = work - jnp.where(row > k, factor, 0.0) * pivot
    diagonal = jnp.sum(jnp.where(lane == row, work, 0.0), axis=1, keepdims=True)
    inverse = (work * (1.0 / jnp.sqrt(diagonal)))[:, ORB : 2 * ORB]
    half = sums[:, ORB : 2 * ORB]
    part = dot(dot(inverse, half, (1, 0)), inverse, (1, 1))
    ritz[...] = part + part.T
    for cell in range(CELLS):
        q_block[pl.ds(cell, ORB, stride=CELLS), :] = dot(inverse, rows_of(field, cell), (1, 0))


def swap(value, axis, first):
    pairs = []
    for i in range(first, lax.axis_size(axis) - 1, 2):
        pairs += [(i, i + 1), (i + 1, i)]
    return lax.ppermute(value, axis, pairs)


def swap_x(value, turn):
    deep, wide = lax.axis_size("gx"), lax.axis_size("gy")
    pairs = []
    for j in range(wide):
        for i in range((turn + j) % 2, deep - 1, 2):
            pairs += [(i * wide + j, (i + 1) * wide + j), ((i + 1) * wide + j, i * wide + j)]
    return lax.ppermute(value, ("gx", "gy"), pairs)


def one_side_x(value):
    deep, wide = lax.axis_size("gx"), lax.axis_size("gy")
    pairs = []
    for j in range(wide):
        for i in range(deep - 1):
            low, high = i * wide + j, (i + 1) * wide + j
            pairs.append((low, high) if j % 2 else (high, low))
    return lax.ppermute(value, ("gx", "gy"), pairs)


def from_above(value, axis):
    return lax.ppermute(value, axis, [(i + 1, i) for i in range(lax.axis_size(axis) - 1)])


def sum_everywhere(value):
    if all(lax.axis_size(axis) == 8 for axis in ("gx", "gy", "gz")):
        fours = [[0, 1, 2, 3], [4, 5, 6, 7]]
        value = value + lax.ppermute(value, "gy", [(i, i ^ 1) for i in range(8)])
        value = lax.psum(value, "gy", axis_index_groups=[[0, 2, 4, 6], [1, 3, 5, 7]])
        value = lax.psum(value, "gz", axis_index_groups=fours)
        value = lax.psum(value, "gx", axis_index_groups=fours)
        rings = [[8 * gx + gz, 8 * gx + 32 + gz, 8 * gx + gz + 4, 8 * gx + 32 + gz + 4] for gx in range(4) for gz in range(4)]
        return lax.psum(value, ("gx", "gz"), axis_index_groups=rings)
    return lax.psum(value, ("gx", "gy", "gz"))


def call(kernel, outs, smem=True, scratch=()):
    def run(*operands):
        specs = [pl.BlockSpec(memory_space=pltpu.VMEM)] * len(operands)
        if smem:
            specs[0] = pl.BlockSpec(memory_space=pltpu.SMEM)
        return pl.pallas_call(
            kernel,
            out_shape=[jax.ShapeDtypeStruct(shape, jnp.float32) for shape in outs],
            in_specs=specs,
            out_specs=[pl.BlockSpec(memory_space=pltpu.VMEM)] * len(outs),
            scratch_shapes=[pltpu.VMEM(shape, jnp.float32) for shape in scratch],
            compiler_params=pltpu.CompilerParams(vmem_limit_bytes=8 * 1024 * 1024),
        )(*operands)

    return run


def body(orbitals, potential):
    at = [lax.axis_index(axis) for axis in ("gx", "gy", "gz")]
    cell_total = orbitals[0].size * lax.axis_size("gx") * lax.axis_size("gy") * lax.axis_size("gz")
    flags = jnp.stack(
        [(at[0] + at[1]) % 2, at[1] % 2, at[2] % 2, (at[2] > 0).astype(jnp.int32), (at[2] < lax.axis_size("gz") - 1).astype(jnp.int32)]
    ).astype(jnp.int32)
    shape = orbitals.shape
    orbitals = orbitals.reshape(BLOCK, LANES)
    potential = potential.reshape(CELLS, LANES)
    block, edge, sent = (BLOCK, LANES), (EDGE, LANES), (BLOCK + EDGE, LANES)

    first, second = call(payload_kernel, ((PAYLOAD, LANES),) * 2)(flags, orbitals, potential)
    second, first = swap(second, "gz", 1), swap(first, "gz", 0)
    field, edge_potential = call(extend_kernel, (sent, (8, LANES)))(flags, orbitals, second, first)

    def advance(field, scale, previous, split):
        y2, y1, x2, x1 = swap(field, "gy", 1), swap(field, "gy", 0), swap_x(field, 1), swap_x(field, 0)
        kernel = functools.partial(block_kernel, scale, bool(previous))
        (part,) = call(kernel, (block,))(flags, potential, field, *previous, x1, y2)
        kernel = functools.partial(join_kernel, scale, bool(previous), split)
        outs = (block, edge) if split else (sent,)
        return call(kernel, outs)(flags, edge_potential, part, field, y1, x2, x1, y2, *previous)

    (field1,) = advance(field, 1.0 / HALF, (), False)
    (field2,) = advance(field1, 2.0 / HALF, (field,), False)
    field, edge = advance(field2, 2.0 / HALF, (field1,), True)
    after_y, beside_x = from_above(field, "gy"), one_side_x(field)
    (part,) = call(image_kernel, (block,))(flags, potential, field, edge)
    wide = (ORB, LANES)
    (sums,) = call(sums_kernel, ((4, LANES),), scratch=(wide,))(flags, part, field, after_y, beside_x)
    sums = sum_everywhere(sums)
    q_block, ritz = call(functools.partial(finish_kernel, cell_total), (block, (ORB, ORB)), False, (wide,))(sums, field)
    return q_block.reshape(shape), ritz


def solution(mesh):
    placed = (P(None, "gx", "gy", "gz"), P("gx", "gy", "gz"))
    return jax.shard_map(
        body,
        mesh=mesh,
        in_specs=placed,
        out_specs=(P(None, "gx", "gy", "gz"), P()),
        check_vma=False,
    )
```

```python
import functools

import jax
import jax.numpy as jnp
from jax import lax
from jax.experimental import pallas as pl
from jax.experimental.pallas import tpu as pltpu
from jax.sharding import PartitionSpec as P

WEIGHTS = (-205.0 / 72.0, 8.0 / 5.0, -1.0 / 5.0, 8.0 / 315.0, -1.0 / 560.0)
HALF = (12.0 - 1.5) / 2.0
MIDDLE = (12.0 + 1.5) / 2.0
ORB = 16
SIDE = 4
CELLS = SIDE * SIDE
LANES = 128
EXT = 16
BLOCK = CELLS * ORB
EDGE = SIDE * ORB
PAYLOAD = 2 * ORB + 8


def lane_index(rows):
    return lax.broadcasted_iota(jnp.int32, (rows, LANES), 1)


def rolled(value, amount):
    amount %= LANES
    return pltpu.roll(value, amount, 1) if amount else value


def rows_of(ref, cell):
    return ref[cell * ORB : (cell + 1) * ORB, :]


def face_masks(flags, rows):
    lane = lane_index(rows)
    even = flags[2] == 0
    upper = jnp.where(even, LANES - EXT, 0)
    lower = jnp.where(even, 0, LANES - EXT)
    first = (lane >= upper) & (lane < upper + EXT)
    second = (lane >= lower) & (lane < lower + EXT)
    return first, second


def payload_kernel(flags, orbitals, potential, first, second):
    mask1, mask2 = face_masks(flags, ORB)
    row1, row2 = face_masks(flags, 1)
    for high in range(2):
        sums = [jnp.zeros((ORB, LANES), jnp.float32)] * 2 + [jnp.zeros((1, LANES), jnp.float32)] * 2
        for low in range(8):
            cell = 8 * high + low
            value = orbitals[pl.ds(cell, ORB, stride=CELLS), :]
            local = potential[cell : cell + 1, :]
            parts = (
                jnp.where(mask1, value, 0.0),
                jnp.where(mask2, value, 0.0),
                jnp.where(row1, local, 0.0),
                jnp.where(row2, local, 0.0),
            )
            sums = [s + rolled(p, EXT * low) for s, p in zip(sums, parts)]
        for out, value, local in ((first, sums[0], sums[2]), (second, sums[1], sums[3])):
            out[high * ORB : (high + 1) * ORB, :] = value
            out[2 * ORB + high : 2 * ORB + high + 1, :] = local
    for out in (first, second):
        out[2 * ORB + 2 :, :] = jnp.zeros((PAYLOAD - 2 * ORB - 2, LANES), jnp.float32)


def extend_kernel(flags, orbitals, second, first, field, edge_potential):
    mask1, mask2 = face_masks(flags, ORB)
    row1, row2 = face_masks(flags, 1)
    for cell in range(CELLS):
        field[cell * ORB : (cell + 1) * ORB, :] = orbitals[pl.ds(cell, ORB, stride=CELLS), :]
    for x in range(SIDE):
        total, total_potential = 0.0, 0.0
        for y in range(SIDE):
            high, low = divmod(x * SIDE + y, 8)

            def unpack(start, size, keep1, keep2):
                one = rolled(first[start : start + size, :], -EXT * low)
                two = rolled(second[start : start + size, :], -EXT * low)
                return rolled(jnp.where(keep2, one, 0.0) + jnp.where(keep1, two, 0.0), 2 * EXT * y)

            total = total + unpack(high * ORB, ORB, mask1, mask2)
            total_potential = total_potential + unpack(2 * ORB + high, 1, row1, row2)
        field[BLOCK + x * ORB : BLOCK + (x + 1) * ORB, :] = total
        edge_potential[x : x + 1, :] = total_potential


def edge_of(ref, x):
    return ref[x * ORB : (x + 1) * ORB, :]


def sides(is_above, get):
    layers = [get(i) for i in range(SIDE)]
    return [jnp.where(is_above, 0.0, v) for v in layers], [jnp.where(is_above, v, 0.0) for v in layers]


def block_kernel(scale, with_previous, flags, potential, field, *rest):
    previous = rest[0] if with_previous else None
    y2, x1, out = rest[-3:]
    lane = lane_index(ORB)
    weight = [-0.5 * scale * w for w in WEIGHTS]
    shift = MIDDLE + 1.5 * WEIGHTS[0]
    for y in range(SIDE):
        below, above = sides(flags[0] == 0, lambda x: rows_of(x1, x * SIDE + y))
        along = below + [rows_of(field, x * SIDE + y) for x in range(SIDE)] + above
        for x in range(SIDE):
            cell = x * SIDE + y
            here = along[SIDE + x]
            there = rolled(edge_of(field, CELLS + x), -2 * EXT * y)
            total = (potential[cell : cell + 1, :] - shift) * scale * here
            for k in range(1, 5):
                pairs = along[SIDE + x + k] + along[SIDE + x - k]
                pairs = pairs + rolled(jnp.where(lane < k, there, here), -k)
                pairs = pairs + rolled(jnp.where(lane >= LANES - k, there, here), k)
                total = total + weight[k] * pairs
            if with_previous:
                total = total - rows_of(previous, cell)
            out[cell * ORB : (cell + 1) * ORB, :] = total
    for x in range(SIDE):
        below, above = sides(flags[1] != 0, lambda y: rows_of(y2, x * SIDE + y))
        along = below + [rows_of(field, x * SIDE + y) for y in range(SIDE)] + above
        for y in range(SIDE):
            cell = x * SIDE + y
            total = rows_of(out, cell)
            for k in range(1, 5):
                total = total + weight[k] * (along[SIDE + y + k] + along[SIDE + y - k])
            out[cell * ORB : (cell + 1) * ORB, :] = total


def join_kernel(scale, with_previous, split, flags, edge_potential, part, field, y1, x2, y2, x1, *rest):
    previous = rest[0] if with_previous else None
    out = rest[-2] if split else rest[-1]
    lane = lane_index(ORB)
    place = lane % (2 * EXT)
    lane_y = ((lane + EXT) // (2 * EXT)) % SIDE
    inside = ((place < EXT) & (flags[4] != 0)) | ((place >= EXT) & (flags[3] != 0))
    window = (lane < EXT) | (lane >= LANES - EXT)
    even_x, even_y = flags[0] == 0, flags[1] == 0
    weight = [-0.5 * scale * w for w in WEIGHTS]
    shift = MIDDLE + 1.5 * WEIGHTS[0]

    def face_terms(below, above, i):
        terms = [weight[k] * above[i + k - SIDE] for k in range(SIDE - i, 5)]
        return sum(terms + [weight[k] * below[i - k + SIDE] for k in range(i + 1, 5)])

    for y in range(SIDE):
        below, above = sides(flags[0] != 0, lambda x: rows_of(x2, x * SIDE + y))
        for x in range(SIDE):
            cell = x * SIDE + y
            out[cell * ORB : (cell + 1) * ORB, :] = rows_of(part, cell) + face_terms(below, above, x)
    for x in range(SIDE):
        below, above = sides(even_y, lambda y: rows_of(y1, x * SIDE + y))
        for y in range(SIDE):
            cell = x * SIDE + y
            out[cell * ORB : (cell + 1) * ORB, :] = rows_of(out, cell) + face_terms(below, above, y)
    pairs = [(edge_of(x1, CELLS + x), edge_of(x2, CELLS + x)) for x in range(SIDE)]
    along = [jnp.where(even_x, b, a) for a, b in pairs]
    along = along + [edge_of(field, CELLS + x) for x in range(SIDE)] + [jnp.where(even_x, a, b) for a, b in pairs]
    for x in range(SIDE):
        here = along[SIDE + x]
        one, two = edge_of(y1, CELLS + x), edge_of(y2, CELLS + x)
        below, above = jnp.where(even_y, two, one), jnp.where(even_y, one, two)
        there = 0.0
        for y in range(SIDE):
            there = there + rolled(jnp.where(window, rows_of(field, x * SIDE + y), 0.0), 2 * EXT * y)
        total = (edge_potential[x : x + 1, :] - shift) * scale * here
        for k in range(1, 5):
            terms = along[SIDE + x + k] + along[SIDE + x - k]
            terms = terms + rolled(jnp.where(lane_y < k, above, here), -2 * EXT * k)
            terms = terms + rolled(jnp.where(lane_y >= SIDE - k, below, here), 2 * EXT * k)
            terms = terms + rolled(jnp.where(place < k, there, here), -k)
            terms = terms + rolled(jnp.where(place >= 2 * EXT - k, there, here), k)
            total = total + weight[k] * terms
        if with_previous:
            total = total - edge_of(previous, CELLS + x)
        total = jnp.where(inside, total, 0.0)
        if split:
            rest[-1][x * ORB : (x + 1) * ORB, :] = total
        else:
            out[BLOCK + x * ORB : BLOCK + (x + 1) * ORB, :] = total


def dot(a, b, contract):
    return lax.dot_general(
        a, b, ((contract[:1], contract[1:]), ((), ())), precision=lax.Precision.HIGHEST, preferred_element_type=jnp.float32
    )


def image_kernel(flags, potential, field, edge, out):
    lane = lane_index(ORB)
    up = flags[1] == 0
    weight = [-0.5 * w for w in WEIGHTS]
    for x in range(SIDE):
        for y in range(SIDE):
            cell = x * SIDE + y
            here, there = rows_of(field, cell), rolled(edge_of(edge, x), -2 * EXT * y)
            total = (0.5 * potential[cell : cell + 1, :] + 1.5 * weight[0]) * here
            above = sum([weight[k] * rows_of(field, cell + k * SIDE) for k in range(1, SIDE - x)], jnp.zeros_like(here))
            below = sum([weight[k] * rows_of(field, cell - k * SIDE) for k in range(1, x + 1)], jnp.zeros_like(here))
            total = total + jnp.where(up, above, below)
            for k in range(1, 5):
                pair = rolled(jnp.where(lane < k, there, here), -k)
                if y + k < SIDE:
                    pair = pair + rows_of(field, cell + k)
                total = total + weight[k] * pair
            out[cell * ORB : (cell + 1) * ORB, :] = total


def group_of(rows):
    return lax.broadcasted_iota(jnp.int32, (rows, LANES), 0) // 4


def sums_kernel(flags, part, field, after_y, beside_x, sums, wide):
    up = flags[1] == 0
    weight = [-0.5 * w for w in WEIGHTS]
    here_all, image_all = [], []
    for x in range(SIDE):
        for y in range(SIDE):
            cell = x * SIDE + y
            above = sum(weight[k] * rows_of(beside_x, cell + (k - SIDE) * SIDE) for k in range(SIDE - x, 5))
            below = sum(weight[k] * rows_of(beside_x, cell + (SIDE - k) * SIDE) for k in range(x + 1, 5))
            image = rows_of(part, cell) + jnp.where(up, above, below)
            image = image + sum(weight[k] * rows_of(after_y, cell + k - SIDE) for k in range(SIDE - y, 5))
            here_all.append(rows_of(field, cell))
            image_all.append(image)
    here = jnp.concatenate(here_all, axis=1)
    image = jnp.concatenate(image_all, axis=1)
    wide[...] = jnp.zeros_like(wide)
    wide[:, : 2 * ORB] = dot(here, jnp.concatenate([here, image], axis=0), (1, 1))
    value, group = wide[...], group_of(ORB)
    wide[...] = sum(jnp.where(group == g, rolled(value, 2 * ORB * g), 0.0) for g in range(4))
    sums[...] = (wide[0:4, :] + wide[4:8, :]) + (wide[8:12, :] + wide[12:16, :])


def finish_kernel(cell_total, sums, field, q_block, ritz, wide):
    for g in range(4):
        wide[4 * g : 4 * g + 4, :] = sums[...]
    value, group = wide[...], group_of(ORB)
    sums = sum(jnp.where(group == g, rolled(value, -2 * ORB * g), 0.0) for g in range(4)) * (1.0 / cell_total)
    row = lax.broadcasted_iota(jnp.int32, (ORB, LANES), 0)
    lane = lane_index(ORB)
    work = jnp.where(lane < ORB, sums, jnp.where(lane == row + ORB, 1.0, 0.0))
    for k in range(0, ORB, 2):
        top, next_row = work[k : k + 1, :], work[k + 1 : k + 2, :]
        left, right = work[:, k : k + 1], work[:, k + 1 : k + 2]
        corner, beside = top[:, k : k + 1], top[:, k + 1 : k + 2]
        ratio = next_row[:, k : k + 1] / corner
        low = next_row - ratio * top
        pivot = next_row[:, k + 1 : k + 2] - ratio * beside
        first = left / corner
        second = (right - first * beside) / pivot
        changed = work - first * top - second * low
        work = jnp.where(row > k + 1, changed, jnp.where(row == k + 1, low, work))
    diagonal = jnp.sum(jnp.where(lane == row, work, 0.0), axis=1, keepdims=True)
    inverse = (work * (1.0 / jnp.sqrt(diagonal)))[:, ORB : 2 * ORB]
    half = sums[:, ORB : 2 * ORB]
    part = dot(dot(inverse, half, (1, 0)), inverse, (1, 1))
    ritz[...] = part + part.T
    product = dot(inverse, jnp.concatenate([rows_of(field, cell) for cell in range(CELLS)], axis=1), (1, 0))
    for cell in range(CELLS):
        q_block[pl.ds(cell, ORB, stride=CELLS), :] = product[:, cell * LANES : (cell + 1) * LANES]


def swap(value, axis, first):
    pairs = []
    for i in range(first, lax.axis_size(axis) - 1, 2):
        pairs += [(i, i + 1), (i + 1, i)]
    return lax.ppermute(value, axis, pairs)


def swap_x(value, turn):
    deep, wide = lax.axis_size("gx"), lax.axis_size("gy")
    pairs = []
    for j in range(wide):
        for i in range((turn + j) % 2, deep - 1, 2):
            pairs += [(i * wide + j, (i + 1) * wide + j), ((i + 1) * wide + j, i * wide + j)]
    return lax.ppermute(value, ("gx", "gy"), pairs)


def one_side_x(value):
    deep, wide = lax.axis_size("gx"), lax.axis_size("gy")
    pairs = []
    for j in range(wide):
        for i in range(deep - 1):
            low, high = i * wide + j, (i + 1) * wide + j
            pairs.append((low, high) if j % 2 else (high, low))
    return lax.ppermute(value, ("gx", "gy"), pairs)


def from_above(value, axis):
    return lax.ppermute(value, axis, [(i + 1, i) for i in range(lax.axis_size(axis) - 1)])


def sum_everywhere(value):
    if all(lax.axis_size(axis) == 8 for axis in ("gx", "gy", "gz")):
        fours = [[0, 1, 2, 3], [4, 5, 6, 7]]
        value = value + lax.ppermute(value, "gy", [(i, i ^ 1) for i in range(8)])
        value = lax.psum(value, "gy", axis_index_groups=[[0, 2, 4, 6], [1, 3, 5, 7]])
        value = lax.psum(value, "gz", axis_index_groups=fours)
        value = lax.psum(value, "gx", axis_index_groups=fours)
        rings = [[8 * gx + gz, 8 * gx + 32 + gz, 8 * gx + gz + 4, 8 * gx + 32 + gz + 4] for gx in range(4) for gz in range(4)]
        return lax.psum(value, ("gx", "gz"), axis_index_groups=rings)
    return lax.psum(value, ("gx", "gy", "gz"))


def call(kernel, outs, smem=True, scratch=()):
    def run(*operands):
        specs = [pl.BlockSpec(memory_space=pltpu.VMEM)] * len(operands)
        if smem:
            specs[0] = pl.BlockSpec(memory_space=pltpu.SMEM)
        return pl.pallas_call(
            kernel,
            out_shape=[jax.ShapeDtypeStruct(shape, jnp.float32) for shape in outs],
            in_specs=specs,
            out_specs=[pl.BlockSpec(memory_space=pltpu.VMEM)] * len(outs),
            scratch_shapes=[pltpu.VMEM(shape, jnp.float32) for shape in scratch],
            compiler_params=pltpu.CompilerParams(vmem_limit_bytes=8 * 1024 * 1024),
        )(*operands)

    return run


def body(orbitals, potential):
    at = [lax.axis_index(axis) for axis in ("gx", "gy", "gz")]
    cell_total = orbitals[0].size * lax.axis_size("gx") * lax.axis_size("gy") * lax.axis_size("gz")
    flags = jnp.stack(
        [(at[0] + at[1]) % 2, at[1] % 2, at[2] % 2, (at[2] > 0).astype(jnp.int32), (at[2] < lax.axis_size("gz") - 1).astype(jnp.int32)]
    ).astype(jnp.int32)
    shape = orbitals.shape
    orbitals = orbitals.reshape(BLOCK, LANES)
    potential = potential.reshape(CELLS, LANES)
    block, edge, sent = (BLOCK, LANES), (EDGE, LANES), (BLOCK + EDGE, LANES)

    first, second = call(payload_kernel, ((PAYLOAD, LANES),) * 2)(flags, orbitals, potential)
    second, first = swap(second, "gz", 1), swap(first, "gz", 0)
    field, edge_potential = call(extend_kernel, (sent, (8, LANES)))(flags, orbitals, second, first)

    def advance(field, scale, previous, split):
        y2, y1, x2, x1 = swap(field, "gy", 1), swap(field, "gy", 0), swap_x(field, 1), swap_x(field, 0)
        kernel = functools.partial(block_kernel, scale, bool(previous))
        (part,) = call(kernel, (block,))(flags, potential, field, *previous, y2, x1)
        kernel = functools.partial(join_kernel, scale, bool(previous), split)
        outs = (block, edge) if split else (sent,)
        return call(kernel, outs)(flags, edge_potential, part, field, y1, x2, y2, x1, *previous)

    (field1,) = advance(field, 1.0 / HALF, (), False)
    (field2,) = advance(field1, 2.0 / HALF, (field,), False)
    field, edge = advance(field2, 2.0 / HALF, (field1,), True)
    after_y, beside_x = from_above(field, "gy"), one_side_x(field)
    (part,) = call(image_kernel, (block,))(flags, potential, field, edge)
    wide = (ORB, LANES)
    (sums,) = call(sums_kernel, ((4, LANES),), scratch=(wide,))(flags, part, field, after_y, beside_x)
    sums = sum_everywhere(sums)
    q_block, ritz = call(functools.partial(finish_kernel, cell_total), (block, (ORB, ORB)), False, (wide,))(sums, field)
    return q_block.reshape(shape), ritz


def solution(mesh):
    placed = (P(None, "gx", "gy", "gz"), P("gx", "gy", "gz"))
    return jax.shard_map(
        body,
        mesh=mesh,
        in_specs=placed,
        out_specs=(P(None, "gx", "gy", "gz"), P()),
        check_vma=False,
    )
```

```python
import functools

import jax
import jax.numpy as jnp
from jax import lax
from jax.experimental import pallas as pl
from jax.experimental.pallas import tpu as pltpu
from jax.sharding import PartitionSpec as P

WEIGHTS = (-205.0 / 72.0, 8.0 / 5.0, -1.0 / 5.0, 8.0 / 315.0, -1.0 / 560.0)
HALF = (12.0 - 1.5) / 2.0
MIDDLE = (12.0 + 1.5) / 2.0
ORB = 16
SIDE = 4
CELLS = SIDE * SIDE
LANES = 128
EXT = 16
BLOCK = CELLS * ORB
EDGE = SIDE * ORB
PAYLOAD = 2 * ORB + 8


def lane_index(rows):
    return lax.broadcasted_iota(jnp.int32, (rows, LANES), 1)


def rolled(value, amount):
    amount %= LANES
    return pltpu.roll(value, amount, 1) if amount else value


def rows_of(ref, cell):
    return ref[cell * ORB : (cell + 1) * ORB, :]


def face_masks(flags, rows):
    lane = lane_index(rows)
    even = flags[2] == 0
    upper = jnp.where(even, LANES - EXT, 0)
    lower = jnp.where(even, 0, LANES - EXT)
    first = (lane >= upper) & (lane < upper + EXT)
    second = (lane >= lower) & (lane < lower + EXT)
    return first, second


def payload_kernel(flags, orbitals, potential, first, second):
    mask1, mask2 = face_masks(flags, ORB)
    row1, row2 = face_masks(flags, 1)
    for high in range(2):
        sums = [jnp.zeros((ORB, LANES), jnp.float32)] * 2 + [jnp.zeros((1, LANES), jnp.float32)] * 2
        for low in range(8):
            cell = 8 * high + low
            value = orbitals[pl.ds(cell, ORB, stride=CELLS), :]
            local = potential[cell : cell + 1, :]
            parts = (
                jnp.where(mask1, value, 0.0),
                jnp.where(mask2, value, 0.0),
                jnp.where(row1, local, 0.0),
                jnp.where(row2, local, 0.0),
            )
            sums = [s + rolled(p, EXT * low) for s, p in zip(sums, parts)]
        for out, value, local in ((first, sums[0], sums[2]), (second, sums[1], sums[3])):
            out[high * ORB : (high + 1) * ORB, :] = value
            out[2 * ORB + high : 2 * ORB + high + 1, :] = local
    for out in (first, second):
        out[2 * ORB + 2 :, :] = jnp.zeros((PAYLOAD - 2 * ORB - 2, LANES), jnp.float32)


def extend_kernel(flags, orbitals, second, first, field, edge_potential):
    mask1, mask2 = face_masks(flags, ORB)
    row1, row2 = face_masks(flags, 1)
    for cell in range(CELLS):
        field[cell * ORB : (cell + 1) * ORB, :] = orbitals[pl.ds(cell, ORB, stride=CELLS), :]
    for x in range(SIDE):
        total, total_potential = 0.0, 0.0
        for y in range(SIDE):
            high, low = divmod(x * SIDE + y, 8)

            def unpack(start, size, keep1, keep2):
                one = rolled(first[start : start + size, :], -EXT * low)
                two = rolled(second[start : start + size, :], -EXT * low)
                return rolled(jnp.where(keep2, one, 0.0) + jnp.where(keep1, two, 0.0), 2 * EXT * y)

            total = total + unpack(high * ORB, ORB, mask1, mask2)
            total_potential = total_potential + unpack(2 * ORB + high, 1, row1, row2)
        field[BLOCK + x * ORB : BLOCK + (x + 1) * ORB, :] = total
        edge_potential[x : x + 1, :] = total_potential


def edge_of(ref, x):
    return ref[x * ORB : (x + 1) * ORB, :]


def sides(is_above, get):
    layers = [get(i) for i in range(SIDE)]
    return [jnp.where(is_above, 0.0, v) for v in layers], [jnp.where(is_above, v, 0.0) for v in layers]


def block_kernel(scale, with_previous, flags, potential, field, *rest):
    previous = rest[0] if with_previous else None
    y2, x1, out = rest[-3:]
    lane = lane_index(ORB)
    weight = [-0.5 * scale * w for w in WEIGHTS]
    shift = MIDDLE + 1.5 * WEIGHTS[0]
    for y in range(SIDE):
        below, above = sides(flags[0] == 0, lambda x: rows_of(x1, x * SIDE + y))
        along = below + [rows_of(field, x * SIDE + y) for x in range(SIDE)] + above
        for x in range(SIDE):
            cell = x * SIDE + y
            here = along[SIDE + x]
            there = rolled(edge_of(field, CELLS + x), -2 * EXT * y)
            total = (potential[cell : cell + 1, :] - shift) * scale * here
            for k in range(1, 5):
                pairs = along[SIDE + x + k] + along[SIDE + x - k]
                pairs = pairs + rolled(jnp.where(lane < k, there, here), -k)
                pairs = pairs + rolled(jnp.where(lane >= LANES - k, there, here), k)
                total = total + weight[k] * pairs
            if with_previous:
                total = total - rows_of(previous, cell)
            out[cell * ORB : (cell + 1) * ORB, :] = total
    for x in range(SIDE):
        below, above = sides(flags[1] != 0, lambda y: rows_of(y2, x * SIDE + y))
        along = below + [rows_of(field, x * SIDE + y) for y in range(SIDE)] + above
        for y in range(SIDE):
            cell = x * SIDE + y
            total = rows_of(out, cell)
            for k in range(1, 5):
                total = total + weight[k] * (along[SIDE + y + k] + along[SIDE + y - k])
            out[cell * ORB : (cell + 1) * ORB, :] = total


def join_kernel(scale, with_previous, split, flags, edge_potential, part, field, y1, x2, y2, x1, *rest):
    previous = rest[0] if with_previous else None
    out = rest[-2] if split else rest[-1]
    lane = lane_index(ORB)
    place = lane % (2 * EXT)
    lane_y = ((lane + EXT) // (2 * EXT)) % SIDE
    inside = ((place < EXT) & (flags[4] != 0)) | ((place >= EXT) & (flags[3] != 0))
    window = (lane < EXT) | (lane >= LANES - EXT)
    even_x, even_y = flags[0] == 0, flags[1] == 0
    weight = [-0.5 * scale * w for w in WEIGHTS]
    shift = MIDDLE + 1.5 * WEIGHTS[0]

    def face_terms(below, above, i):
        terms = [weight[k] * above[i + k - SIDE] for k in range(SIDE - i, 5)]
        return sum(terms + [weight[k] * below[i - k + SIDE] for k in range(i + 1, 5)])

    for y in range(SIDE):
        below, above = sides(flags[0] != 0, lambda x: rows_of(x2, x * SIDE + y))
        for x in range(SIDE):
            cell = x * SIDE + y
            out[cell * ORB : (cell + 1) * ORB, :] = rows_of(part, cell) + face_terms(below, above, x)
    for x in range(SIDE):
        below, above = sides(even_y, lambda y: rows_of(y1, x * SIDE + y))
        for y in range(SIDE):
            cell = x * SIDE + y
            out[cell * ORB : (cell + 1) * ORB, :] = rows_of(out, cell) + face_terms(below, above, y)
    pairs = [(edge_of(x1, CELLS + x), edge_of(x2, CELLS + x)) for x in range(SIDE)]
    along = [jnp.where(even_x, b, a) for a, b in pairs]
    along = along + [edge_of(field, CELLS + x) for x in range(SIDE)] + [jnp.where(even_x, a, b) for a, b in pairs]
    for x in range(SIDE):
        here = along[SIDE + x]
        one, two = edge_of(y1, CELLS + x), edge_of(y2, CELLS + x)
        below, above = jnp.where(even_y, two, one), jnp.where(even_y, one, two)
        there = 0.0
        for y in range(SIDE):
            there = there + rolled(jnp.where(window, rows_of(field, x * SIDE + y), 0.0), 2 * EXT * y)
        total = (edge_potential[x : x + 1, :] - shift) * scale * here
        for k in range(1, 5):
            terms = along[SIDE + x + k] + along[SIDE + x - k]
            terms = terms + rolled(jnp.where(lane_y < k, above, here), -2 * EXT * k)
            terms = terms + rolled(jnp.where(lane_y >= SIDE - k, below, here), 2 * EXT * k)
            terms = terms + rolled(jnp.where(place < k, there, here), -k)
            terms = terms + rolled(jnp.where(place >= 2 * EXT - k, there, here), k)
            total = total + weight[k] * terms
        if with_previous:
            total = total - edge_of(previous, CELLS + x)
        total = jnp.where(inside, total, 0.0)
        if split:
            rest[-1][x * ORB : (x + 1) * ORB, :] = total
        else:
            out[BLOCK + x * ORB : BLOCK + (x + 1) * ORB, :] = total


def dot(a, b, contract):
    return lax.dot_general(
        a, b, ((contract[:1], contract[1:]), ((), ())), precision=lax.Precision.HIGHEST, preferred_element_type=jnp.float32
    )


def image_kernel(flags, potential, field, edge, out):
    lane = lane_index(ORB)
    up = flags[1] == 0
    weight = [-0.5 * w for w in WEIGHTS]
    for x in range(SIDE):
        for y in range(SIDE):
            cell = x * SIDE + y
            here, there = rows_of(field, cell), rolled(edge_of(edge, x), -2 * EXT * y)
            total = (0.5 * potential[cell : cell + 1, :] + 1.5 * weight[0]) * here
            above = sum([weight[k] * rows_of(field, cell + k * SIDE) for k in range(1, SIDE - x)], jnp.zeros_like(here))
            below = sum([weight[k] * rows_of(field, cell - k * SIDE) for k in range(1, x + 1)], jnp.zeros_like(here))
            total = total + jnp.where(up, above, below)
            for k in range(1, 5):
                pair = rolled(jnp.where(lane < k, there, here), -k)
                if y + k < SIDE:
                    pair = pair + rows_of(field, cell + k)
                total = total + weight[k] * pair
            out[cell * ORB : (cell + 1) * ORB, :] = total


def group_of(rows):
    return lax.broadcasted_iota(jnp.int32, (rows, LANES), 0) // 4


def sums_kernel(flags, part, field, after_y, beside_x, sums, wide):
    up = flags[1] == 0
    weight = [-0.5 * w for w in WEIGHTS]
    here_all, image_all = [], []
    for x in range(SIDE):
        for y in range(SIDE):
            cell = x * SIDE + y
            above = sum(weight[k] * rows_of(beside_x, cell + (k - SIDE) * SIDE) for k in range(SIDE - x, 5))
            below = sum(weight[k] * rows_of(beside_x, cell + (SIDE - k) * SIDE) for k in range(x + 1, 5))
            image = rows_of(part, cell) + jnp.where(up, above, below)
            image = image + sum(weight[k] * rows_of(after_y, cell + k - SIDE) for k in range(SIDE - y, 5))
            here_all.append(rows_of(field, cell))
            image_all.append(image)
    here = jnp.concatenate(here_all, axis=1)
    image = jnp.concatenate(image_all, axis=1)
    wide[...] = jnp.zeros_like(wide)
    wide[:, : 2 * ORB] = dot(here, jnp.concatenate([here, image], axis=0), (1, 1))
    value, group = wide[...], group_of(ORB)
    wide[...] = sum(jnp.where(group == g, rolled(value, 2 * ORB * g), 0.0) for g in range(4))
    sums[...] = (wide[0:4, :] + wide[4:8, :]) + (wide[8:12, :] + wide[12:16, :])


def finish_kernel(cell_total, sums, field, q_block, ritz, wide):
    for g in range(4):
        wide[4 * g : 4 * g + 4, :] = sums[...]
    value, group = wide[...], group_of(ORB)
    sums = sum(jnp.where(group == g, rolled(value, -2 * ORB * g), 0.0) for g in range(4)) * (1.0 / cell_total)
    row = lax.broadcasted_iota(jnp.int32, (ORB, LANES), 0)
    lane = lane_index(ORB)
    work = jnp.where(lane < ORB, sums, jnp.where(lane == row + ORB, 1.0, 0.0))
    for k in range(ORB - 1):
        pivot = work[k : k + 1, :]
        factor = work[:, k : k + 1] / pivot[:, k : k + 1]
        work = work - jnp.where(row > k, factor, 0.0) * pivot
    diagonal = jnp.sum(jnp.where(lane == row, work, 0.0), axis=1, keepdims=True)
    inverse = (work * (1.0 / jnp.sqrt(diagonal)))[:, ORB : 2 * ORB]
    half = sums[:, ORB : 2 * ORB]
    part = dot(dot(inverse, half, (1, 0)), inverse, (1, 1))
    ritz[...] = part + part.T
    for cell in range(CELLS):
        q_block[pl.ds(cell, ORB, stride=CELLS), :] = dot(inverse, rows_of(field, cell), (1, 0))


def swap(value, axis, first):
    pairs = []
    for i in range(first, lax.axis_size(axis) - 1, 2):
        pairs += [(i, i + 1), (i + 1, i)]
    return lax.ppermute(value, axis, pairs)


def swap_x(value, turn):
    deep, wide = lax.axis_size("gx"), lax.axis_size("gy")
    pairs = []
    for j in range(wide):
        for i in range((turn + j) % 2, deep - 1, 2):
            pairs += [(i * wide + j, (i + 1) * wide + j), ((i + 1) * wide + j, i * wide + j)]
    return lax.ppermute(value, ("gx", "gy"), pairs)


def one_side_x(value):
    deep, wide = lax.axis_size("gx"), lax.axis_size("gy")
    pairs = []
    for j in range(wide):
        for i in range(deep - 1):
            low, high = i * wide + j, (i + 1) * wide + j
            pairs.append((low, high) if j % 2 else (high, low))
    return lax.ppermute(value, ("gx", "gy"), pairs)


def from_above(value, axis):
    return lax.ppermute(value, axis, [(i + 1, i) for i in range(lax.axis_size(axis) - 1)])


def sum_everywhere(value):
    if all(lax.axis_size(axis) == 8 for axis in ("gx", "gy", "gz")):
        fours = [[0, 1, 2, 3], [4, 5, 6, 7]]
        value = lax.psum(value, "gy", axis_index_groups=[[0, 2, 4, 6], [1, 3, 5, 7]])
        value = lax.psum(value, "gz", axis_index_groups=fours)
        value = lax.psum(value, "gx", axis_index_groups=fours)
        rings = [[8 * gx + gz, 8 * gx + 32 + gz, 8 * gx + gz + 4, 8 * gx + 32 + gz + 4] for gx in range(4) for gz in range(4)]
        value = lax.psum(value, ("gx", "gz"), axis_index_groups=rings)
        return value + lax.ppermute(value, "gy", [(i, i ^ 1) for i in range(8)])
    return lax.psum(value, ("gx", "gy", "gz"))


def call(kernel, outs, smem=True, scratch=()):
    def run(*operands):
        specs = [pl.BlockSpec(memory_space=pltpu.VMEM)] * len(operands)
        if smem:
            specs[0] = pl.BlockSpec(memory_space=pltpu.SMEM)
        return pl.pallas_call(
            kernel,
            out_shape=[jax.ShapeDtypeStruct(shape, jnp.float32) for shape in outs],
            in_specs=specs,
            out_specs=[pl.BlockSpec(memory_space=pltpu.VMEM)] * len(outs),
            scratch_shapes=[pltpu.VMEM(shape, jnp.float32) for shape in scratch],
            compiler_params=pltpu.CompilerParams(vmem_limit_bytes=8 * 1024 * 1024),
        )(*operands)

    return run


def body(orbitals, potential):
    at = [lax.axis_index(axis) for axis in ("gx", "gy", "gz")]
    cell_total = orbitals[0].size * lax.axis_size("gx") * lax.axis_size("gy") * lax.axis_size("gz")
    flags = jnp.stack(
        [(at[0] + at[1]) % 2, at[1] % 2, at[2] % 2, (at[2] > 0).astype(jnp.int32), (at[2] < lax.axis_size("gz") - 1).astype(jnp.int32)]
    ).astype(jnp.int32)
    shape = orbitals.shape
    orbitals = orbitals.reshape(BLOCK, LANES)
    potential = potential.reshape(CELLS, LANES)
    block, edge, sent = (BLOCK, LANES), (EDGE, LANES), (BLOCK + EDGE, LANES)

    first, second = call(payload_kernel, ((PAYLOAD, LANES),) * 2)(flags, orbitals, potential)
    second, first = swap(second, "gz", 1), swap(first, "gz", 0)
    field, edge_potential = call(extend_kernel, (sent, (8, LANES)))(flags, orbitals, second, first)

    def advance(field, scale, previous, split):
        y2, y1, x2, x1 = swap(field, "gy", 1), swap(field, "gy", 0), swap_x(field, 1), swap_x(field, 0)
        kernel = functools.partial(block_kernel, scale, bool(previous))
        (part,) = call(kernel, (block,))(flags, potential, field, *previous, y2, x1)
        kernel = functools.partial(join_kernel, scale, bool(previous), split)
        outs = (block, edge) if split else (sent,)
        return call(kernel, outs)(flags, edge_potential, part, field, y1, x2, y2, x1, *previous)

    (field1,) = advance(field, 1.0 / HALF, (), False)
    (field2,) = advance(field1, 2.0 / HALF, (field,), False)
    field, edge = advance(field2, 2.0 / HALF, (field1,), True)
    after_y, beside_x = from_above(field, "gy"), one_side_x(field)
    (part,) = call(image_kernel, (block,))(flags, potential, field, edge)
    wide = (ORB, LANES)
    (sums,) = call(sums_kernel, ((4, LANES),), scratch=(wide,))(flags, part, field, after_y, beside_x)
    sums = sum_everywhere(sums)
    q_block, ritz = call(functools.partial(finish_kernel, cell_total), (block, (ORB, ORB)), False, (wide,))(sums, field)
    return q_block.reshape(shape), ritz


def solution(mesh):
    placed = (P(None, "gx", "gy", "gz"), P("gx", "gy", "gz"))
    return jax.shard_map(
        body,
        mesh=mesh,
        in_specs=placed,
        out_specs=(P(None, "gx", "gy", "gz"), P()),
        check_vma=False,
    )
```

```python
import functools

import jax
import jax.numpy as jnp
from jax import lax
from jax.experimental import pallas as pl
from jax.experimental.pallas import tpu as pltpu
from jax.sharding import PartitionSpec as P

WEIGHTS = (-205.0 / 72.0, 8.0 / 5.0, -1.0 / 5.0, 8.0 / 315.0, -1.0 / 560.0)
HALF = (12.0 - 1.5) / 2.0
MIDDLE = (12.0 + 1.5) / 2.0
ORB = 16
SIDE = 4
CELLS = SIDE * SIDE
LANES = 128
EXT = 16
BLOCK = CELLS * ORB
EDGE = SIDE * ORB
PAYLOAD = 2 * ORB + 8


def lane_index(rows):
    return lax.broadcasted_iota(jnp.int32, (rows, LANES), 1)


def rolled(value, amount):
    amount %= LANES
    return pltpu.roll(value, amount, 1) if amount else value


def rows_of(ref, cell):
    return ref[cell * ORB : (cell + 1) * ORB, :]


def face_masks(flags, rows):
    lane = lane_index(rows)
    even = flags[2] == 0
    upper = jnp.where(even, LANES - EXT, 0)
    lower = jnp.where(even, 0, LANES - EXT)
    first = (lane >= upper) & (lane < upper + EXT)
    second = (lane >= lower) & (lane < lower + EXT)
    return first, second


def payload_kernel(flags, orbitals, potential, first, second):
    mask1, mask2 = face_masks(flags, ORB)
    row1, row2 = face_masks(flags, 1)
    for high in range(2):
        sums = [jnp.zeros((ORB, LANES), jnp.float32)] * 2 + [jnp.zeros((1, LANES), jnp.float32)] * 2
        for low in range(8):
            cell = 8 * high + low
            value = orbitals[pl.ds(cell, ORB, stride=CELLS), :]
            local = potential[cell : cell + 1, :]
            parts = (
                jnp.where(mask1, value, 0.0),
                jnp.where(mask2, value, 0.0),
                jnp.where(row1, local, 0.0),
                jnp.where(row2, local, 0.0),
            )
            sums = [s + rolled(p, EXT * low) for s, p in zip(sums, parts)]
        for out, value, local in ((first, sums[0], sums[2]), (second, sums[1], sums[3])):
            out[high * ORB : (high + 1) * ORB, :] = value
            out[2 * ORB + high : 2 * ORB + high + 1, :] = local
    for out in (first, second):
        out[2 * ORB + 2 :, :] = jnp.zeros((PAYLOAD - 2 * ORB - 2, LANES), jnp.float32)


def extend_kernel(flags, orbitals, second, first, field, edge_potential):
    mask1, mask2 = face_masks(flags, ORB)
    row1, row2 = face_masks(flags, 1)
    for cell in range(CELLS):
        field[cell * ORB : (cell + 1) * ORB, :] = orbitals[pl.ds(cell, ORB, stride=CELLS), :]
    for x in range(SIDE):
        total, total_potential = 0.0, 0.0
        for y in range(SIDE):
            high, low = divmod(x * SIDE + y, 8)

            def unpack(start, size, keep1, keep2):
                one = rolled(first[start : start + size, :], -EXT * low)
                two = rolled(second[start : start + size, :], -EXT * low)
                return rolled(jnp.where(keep2, one, 0.0) + jnp.where(keep1, two, 0.0), 2 * EXT * y)

            total = total + unpack(high * ORB, ORB, mask1, mask2)
            total_potential = total_potential + unpack(2 * ORB + high, 1, row1, row2)
        field[BLOCK + x * ORB : BLOCK + (x + 1) * ORB, :] = total
        edge_potential[x : x + 1, :] = total_potential


def edge_of(ref, x):
    return ref[x * ORB : (x + 1) * ORB, :]


def sides(is_above, get):
    layers = [get(i) for i in range(SIDE)]
    return [jnp.where(is_above, 0.0, v) for v in layers], [jnp.where(is_above, v, 0.0) for v in layers]


def block_kernel(scale, with_previous, flags, potential, field, *rest):
    previous = rest[0] if with_previous else None
    y2, x1, out = rest[-3:]
    lane = lane_index(ORB)
    weight = [-0.5 * scale * w for w in WEIGHTS]
    shift = MIDDLE + 1.5 * WEIGHTS[0]
    for y in range(SIDE):
        below, above = sides(flags[0] == 0, lambda x: rows_of(x1, x * SIDE + y))
        along = below + [rows_of(field, x * SIDE + y) for x in range(SIDE)] + above
        for x in range(SIDE):
            cell = x * SIDE + y
            here = along[SIDE + x]
            there = rolled(edge_of(field, CELLS + x), -2 * EXT * y)
            total = (potential[cell : cell + 1, :] - shift) * scale * here
            for k in range(1, 5):
                pairs = along[SIDE + x + k] + along[SIDE + x - k]
                pairs = pairs + rolled(jnp.where(lane < k, there, here), -k)
                pairs = pairs + rolled(jnp.where(lane >= LANES - k, there, here), k)
                total = total + weight[k] * pairs
            if with_previous:
                total = total - rows_of(previous, cell)
            out[cell * ORB : (cell + 1) * ORB, :] = total
    for x in range(SIDE):
        below, above = sides(flags[1] != 0, lambda y: rows_of(y2, x * SIDE + y))
        along = below + [rows_of(field, x * SIDE + y) for y in range(SIDE)] + above
        for y in range(SIDE):
            cell = x * SIDE + y
            total = rows_of(out, cell)
            for k in range(1, 5):
                total = total + weight[k] * (along[SIDE + y + k] + along[SIDE + y - k])
            out[cell * ORB : (cell + 1) * ORB, :] = total


def join_kernel(scale, with_previous, split, flags, edge_potential, part, field, y1, x2, y2, x1, *rest):
    previous = rest[0] if with_previous else None
    out = rest[-2] if split else rest[-1]
    lane = lane_index(ORB)
    place = lane % (2 * EXT)
    lane_y = ((lane + EXT) // (2 * EXT)) % SIDE
    inside = ((place < EXT) & (flags[4] != 0)) | ((place >= EXT) & (flags[3] != 0))
    window = (lane < EXT) | (lane >= LANES - EXT)
    even_x, even_y = flags[0] == 0, flags[1] == 0
    weight = [-0.5 * scale * w for w in WEIGHTS]
    shift = MIDDLE + 1.5 * WEIGHTS[0]

    def face_terms(below, above, i):
        terms = [weight[k] * above[i + k - SIDE] for k in range(SIDE - i, 5)]
        return sum(terms + [weight[k] * below[i - k + SIDE] for k in range(i + 1, 5)])

    for y in range(SIDE):
        below, above = sides(flags[0] != 0, lambda x: rows_of(x2, x * SIDE + y))
        for x in range(SIDE):
            cell = x * SIDE + y
            out[cell * ORB : (cell + 1) * ORB, :] = rows_of(part, cell) + face_terms(below, above, x)
    for x in range(SIDE):
        below, above = sides(even_y, lambda y: rows_of(y1, x * SIDE + y))
        for y in range(SIDE):
            cell = x * SIDE + y
            out[cell * ORB : (cell + 1) * ORB, :] = rows_of(out, cell) + face_terms(below, above, y)
    pairs = [(edge_of(x1, CELLS + x), edge_of(x2, CELLS + x)) for x in range(SIDE)]
    along = [jnp.where(even_x, b, a) for a, b in pairs]
    along = along + [edge_of(field, CELLS + x) for x in range(SIDE)] + [jnp.where(even_x, a, b) for a, b in pairs]
    for x in range(SIDE):
        here = along[SIDE + x]
        one, two = edge_of(y1, CELLS + x), edge_of(y2, CELLS + x)
        below, above = jnp.where(even_y, two, one), jnp.where(even_y, one, two)
        there = 0.0
        for y in range(SIDE):
            there = there + rolled(jnp.where(window, rows_of(field, x * SIDE + y), 0.0), 2 * EXT * y)
        total = (edge_potential[x : x + 1, :] - shift) * scale * here
        for k in range(1, 5):
            terms = along[SIDE + x + k] + along[SIDE + x - k]
            terms = terms + rolled(jnp.where(lane_y < k, above, here), -2 * EXT * k)
            terms = terms + rolled(jnp.where(lane_y >= SIDE - k, below, here), 2 * EXT * k)
            terms = terms + rolled(jnp.where(place < k, there, here), -k)
            terms = terms + rolled(jnp.where(place >= 2 * EXT - k, there, here), k)
            total = total + weight[k] * terms
        if with_previous:
            total = total - edge_of(previous, CELLS + x)
        total = jnp.where(inside, total, 0.0)
        if split:
            rest[-1][x * ORB : (x + 1) * ORB, :] = total
        else:
            out[BLOCK + x * ORB : BLOCK + (x + 1) * ORB, :] = total


def dot(a, b, contract):
    return lax.dot_general(
        a, b, ((contract[:1], contract[1:]), ((), ())), precision=lax.Precision.HIGHEST, preferred_element_type=jnp.float32
    )


def image_kernel(flags, potential, field, edge, out):
    lane = lane_index(ORB)
    up = flags[1] == 0
    weight = [-0.5 * w for w in WEIGHTS]
    for x in range(SIDE):
        for y in range(SIDE):
            cell = x * SIDE + y
            here, there = rows_of(field, cell), rolled(edge_of(edge, x), -2 * EXT * y)
            total = (0.5 * potential[cell : cell + 1, :] + 1.5 * weight[0]) * here
            above = sum([weight[k] * rows_of(field, cell + k * SIDE) for k in range(1, SIDE - x)], jnp.zeros_like(here))
            below = sum([weight[k] * rows_of(field, cell - k * SIDE) for k in range(1, x + 1)], jnp.zeros_like(here))
            total = total + jnp.where(up, above, below)
            for k in range(1, 5):
                pair = rolled(jnp.where(lane < k, there, here), -k)
                if y + k < SIDE:
                    pair = pair + rows_of(field, cell + k)
                total = total + weight[k] * pair
            out[cell * ORB : (cell + 1) * ORB, :] = total


def group_of(rows):
    return lax.broadcasted_iota(jnp.int32, (rows, LANES), 0) // 4


def sums_kernel(flags, part, field, after_y, beside_x, sums, wide):
    up = flags[1] == 0
    weight = [-0.5 * w for w in WEIGHTS]
    here_all, image_all = [], []
    for x in range(SIDE):
        for y in range(SIDE):
            cell = x * SIDE + y
            above = sum(weight[k] * rows_of(beside_x, cell + (k - SIDE) * SIDE) for k in range(SIDE - x, 5))
            below = sum(weight[k] * rows_of(beside_x, cell + (SIDE - k) * SIDE) for k in range(x + 1, 5))
            image = rows_of(part, cell) + jnp.where(up, above, below)
            image = image + sum(weight[k] * rows_of(after_y, cell + k - SIDE) for k in range(SIDE - y, 5))
            here_all.append(rows_of(field, cell))
            image_all.append(image)
    here = jnp.concatenate(here_all, axis=1)
    image = jnp.concatenate(image_all, axis=1)
    wide[...] = jnp.zeros_like(wide)
    wide[:, : 2 * ORB] = dot(here, jnp.concatenate([here, image], axis=0), (1, 1))
    value, group = wide[...], group_of(ORB)
    wide[...] = sum(jnp.where(group == g, rolled(value, 2 * ORB * g), 0.0) for g in range(4))
    sums[...] = (wide[0:4, :] + wide[4:8, :]) + (wide[8:12, :] + wide[12:16, :])


def finish_kernel(cell_total, sums, field, q_block, ritz, wide):
    for g in range(4):
        wide[4 * g : 4 * g + 4, :] = sums[...]
    value, group = wide[...], group_of(ORB)
    sums = sum(jnp.where(group == g, rolled(value, -2 * ORB * g), 0.0) for g in range(4)) * (1.0 / cell_total)
    row = lax.broadcasted_iota(jnp.int32, (ORB, LANES), 0)
    lane = lane_index(ORB)
    work = jnp.where(lane < ORB, sums, jnp.where(lane == row + ORB, 1.0, 0.0))
    for k in range(ORB - 1):
        pivot = work[k : k + 1, :]
        factor = work[:, k : k + 1] / pivot[:, k : k + 1]
        work = work - jnp.where(row > k, factor, 0.0) * pivot
    diagonal = jnp.sum(jnp.where(lane == row, work, 0.0), axis=1, keepdims=True)
    inverse = (work * (1.0 / jnp.sqrt(diagonal)))[:, ORB : 2 * ORB]
    half = sums[:, ORB : 2 * ORB]
    part = dot(dot(inverse, half, (1, 0)), inverse, (1, 1))
    ritz[...] = part + part.T
    for cell in range(CELLS):
        q_block[pl.ds(cell, ORB, stride=CELLS), :] = dot(inverse, rows_of(field, cell), (1, 0))


def swap(value, axis, first):
    pairs = []
    for i in range(first, lax.axis_size(axis) - 1, 2):
        pairs += [(i, i + 1), (i + 1, i)]
    return lax.ppermute(value, axis, pairs)


def swap_x(value, turn):
    deep, wide = lax.axis_size("gx"), lax.axis_size("gy")
    pairs = []
    for j in range(wide):
        for i in range((turn + j) % 2, deep - 1, 2):
            pairs += [(i * wide + j, (i + 1) * wide + j), ((i + 1) * wide + j, i * wide + j)]
    return lax.ppermute(value, ("gx", "gy"), pairs)


def one_side_x(value):
    deep, wide = lax.axis_size("gx"), lax.axis_size("gy")
    pairs = []
    for j in range(wide):
        for i in range(deep - 1):
            low, high = i * wide + j, (i + 1) * wide + j
            pairs.append((low, high) if j % 2 else (high, low))
    return lax.ppermute(value, ("gx", "gy"), pairs)


def from_above(value, axis):
    return lax.ppermute(value, axis, [(i + 1, i) for i in range(lax.axis_size(axis) - 1)])


def sum_everywhere(value):
    if all(lax.axis_size(axis) == 8 for axis in ("gx", "gy", "gz")):
        fours = [[0, 1, 2, 3], [4, 5, 6, 7]]
        value = value + lax.ppermute(value, "gy", [(i, i ^ 1) for i in range(8)])
        rings = [[8 * gx + gz, 8 * gx + 32 + gz, 8 * gx + gz + 4, 8 * gx + 32 + gz + 4] for gx in range(4) for gz in range(4)]
        value = lax.psum(value, ("gx", "gz"), axis_index_groups=rings)
        value = lax.psum(value, "gz", axis_index_groups=fours)
        value = lax.psum(value, "gx", axis_index_groups=fours)
        return lax.psum(value, "gy", axis_index_groups=[[0, 2, 4, 6], [1, 3, 5, 7]])
    return lax.psum(value, ("gx", "gy", "gz"))


def call(kernel, outs, smem=True, scratch=()):
    def run(*operands):
        specs = [pl.BlockSpec(memory_space=pltpu.VMEM)] * len(operands)
        if smem:
            specs[0] = pl.BlockSpec(memory_space=pltpu.SMEM)
        return pl.pallas_call(
            kernel,
            out_shape=[jax.ShapeDtypeStruct(shape, jnp.float32) for shape in outs],
            in_specs=specs,
            out_specs=[pl.BlockSpec(memory_space=pltpu.VMEM)] * len(outs),
            scratch_shapes=[pltpu.VMEM(shape, jnp.float32) for shape in scratch],
            compiler_params=pltpu.CompilerParams(vmem_limit_bytes=8 * 1024 * 1024),
        )(*operands)

    return run


def body(orbitals, potential):
    at = [lax.axis_index(axis) for axis in ("gx", "gy", "gz")]
    cell_total = orbitals[0].size * lax.axis_size("gx") * lax.axis_size("gy") * lax.axis_size("gz")
    flags = jnp.stack(
        [(at[0] + at[1]) % 2, at[1] % 2, at[2] % 2, (at[2] > 0).astype(jnp.int32), (at[2] < lax.axis_size("gz") - 1).astype(jnp.int32)]
    ).astype(jnp.int32)
    shape = orbitals.shape
    orbitals = orbitals.reshape(BLOCK, LANES)
    potential = potential.reshape(CELLS, LANES)
    block, edge, sent = (BLOCK, LANES), (EDGE, LANES), (BLOCK + EDGE, LANES)

    first, second = call(payload_kernel, ((PAYLOAD, LANES),) * 2)(flags, orbitals, potential)
    second, first = swap(second, "gz", 1), swap(first, "gz", 0)
    field, edge_potential = call(extend_kernel, (sent, (8, LANES)))(flags, orbitals, second, first)

    def advance(field, scale, previous, split):
        y2, y1, x2, x1 = swap(field, "gy", 1), swap(field, "gy", 0), swap_x(field, 1), swap_x(field, 0)
        kernel = functools.partial(block_kernel, scale, bool(previous))
        (part,) = call(kernel, (block,))(flags, potential, field, *previous, y2, x1)
        kernel = functools.partial(join_kernel, scale, bool(previous), split)
        outs = (block, edge) if split else (sent,)
        return call(kernel, outs)(flags, edge_potential, part, field, y1, x2, y2, x1, *previous)

    (field1,) = advance(field, 1.0 / HALF, (), False)
    (field2,) = advance(field1, 2.0 / HALF, (field,), False)
    field, edge = advance(field2, 2.0 / HALF, (field1,), True)
    after_y, beside_x = from_above(field, "gy"), one_side_x(field)
    (part,) = call(image_kernel, (block,))(flags, potential, field, edge)
    wide = (ORB, LANES)
    (sums,) = call(sums_kernel, ((4, LANES),), scratch=(wide,))(flags, part, field, after_y, beside_x)
    sums = sum_everywhere(sums)
    q_block, ritz = call(functools.partial(finish_kernel, cell_total), (block, (ORB, ORB)), False, (wide,))(sums, field)
    return q_block.reshape(shape), ritz


def solution(mesh):
    placed = (P(None, "gx", "gy", "gz"), P("gx", "gy", "gz"))
    return jax.shard_map(
        body,
        mesh=mesh,
        in_specs=placed,
        out_specs=(P(None, "gx", "gy", "gz"), P()),
        check_vma=False,
    )
```
